32 devices in a mesh: visit: 2 (over x), py: 4 (over y, core), px: 4 (over z).
Axes of the slice: x: 2, y: 2, z: 4, core: 2. Of those that a mesh axis runs over, the one named last changes fastest.
Arguments:
- images: bfloat16 [768, 256, 256], P(('visit', 'py', 'px')), may hold values from -6 to 6
- inv_var: bfloat16 [768, 256, 256], P(('visit', 'py', 'px')), may hold values from 0.25 to 4
- good_columns: int32 [16, 256], P('visit'), may hold values 0 or 1
- warp_rows: bfloat16 [16, 256, 256], P('visit'), may hold values from -0.4 to 1.4, as said below
- warp_cols: bfloat16 [16, 256, 256], P('visit'), may hold values from -0.4 to 1.4, as said below
- block_visit: int32 [768], P(('visit', 'py', 'px')), may hold values from 0 to 7
- dest_tile: int32 [768, 1], P(('visit', 'py', 'px')), may hold values from 0 to 15; in each aligned block of 24 rows (0 to 23, 24 to 47, ...) at most 2 rows name the same one
- offsets: int32 [768, 2], P(('visit', 'py', 'px')), may hold values from 0 to 6
- psf_taps: float32 [7], replicated, may hold values from 0.1 to 1
Outputs:
- detection: float32 [4096, 4096], P('py', 'px')
- local_variance: float32 [4096, 4096], P('py', 'px')
The draws below stay inside these ranges and needn't reach their ends.
Inputs may be any that keep to these rules, and one draw needn't show every extreme that they name: `dest_tile`: among the rows of one device no tile is named more than 2 times, a bound that some block reaches. `warp_rows`: lanczos interpolation weights of each visit. `warp_cols`: lanczos interpolation weights of each visit.
All inputs are finite; a program needn't handle non-finite values. No bound on the sum of `good_columns` on one device may be relied on, other than what follows from the above.
Results may differ from the reference program's by a relative error of at most 0.0057.
Values may be sent and summed in bfloat16 or wider, within the bound.
No kernel may reach another device: no remote copies, remote signals or barrier semaphores. Data moves between devices by JAX's collectives and lax.ppermute only.
A program may use at most 128 MiB of HBM per device.

```python
import math
import jax
import jax.numpy as jnp
import numpy as np
from jax import lax

BS = 256
TY = 1024
TX = 1024
STEP = 128
NB = 24
VD = 8
CAP = 2
PSF = 7
PER_GROUP = 384
NBLOCKS = 768
VISITS = 16
PATCH_COLS = 4
TILES = 16
NY = 4096
NX = 4096


def lanczos_matrix(key):
    shift_key, gain_key = jax.random.split(key)
    shift = jax.random.uniform(shift_key, (VISITS, 1, 1), jnp.float32, -0.5, 0.5)
    row_pos = jnp.arange(BS, dtype=jnp.float32)[None, :, None]
    col_pos = jnp.arange(BS, dtype=jnp.float32)[None, None, :]
    distance = row_pos - col_pos - shift
    kernel = jnp.where(jnp.abs(distance) < 3.0, jnp.sinc(distance) * jnp.sinc(distance / 3.0), 0.0)
    gains = jax.random.uniform(gain_key, (VISITS, BS, BS), jnp.float32, 0.8, 1.2)
    return (kernel * gains).astype(jnp.bfloat16)


def draw_warp_rows(key, part):
    return lanczos_matrix(jax.random.fold_in(key, 101))


def draw_warp_cols(key, part):
    return lanczos_matrix(jax.random.fold_in(key, 202))


def plant(result, stream_key, smallest, top_value):
    shape = result.shape
    index_at = [jax.random.randint(jax.random.fold_in(stream_key, axis), (), 0, shape[axis]) for axis in range(len(shape))]
    result = result.at[tuple(index_at)].set(smallest)
    longest = shape.index(max(shape))
    index_at[longest] = (index_at[longest] + 1) % shape[longest]
    return result.at[tuple(index_at)].set(top_value)


def block_levels(stream_key, dims, cuts, smallest, high):
    def one(axis_at, shards_of):
        draws = jax.random.uniform(jax.random.fold_in(jax.random.fold_in(stream_key, 6), axis_at), (shards_of,), jnp.float32, smallest / len(cuts), high / len(cuts))
        return jnp.repeat(jnp.exp(draws), dims[axis_at] // shards_of).reshape((-1,) + (1,) * (len(dims) - axis_at - 1))

    gain = one(*cuts[0])
    for cut in cuts[1:]:
        gain = gain * one(*cut)
    return gain


def shared_out(key, own, number, rows, count, top, bound, skew):
    order = jax.random.permutation(key, count)
    crowded, common = portions_of(count, rows * top, bound, skew, True), portions_of(count, rows * top, bound, skew, False)
    places = jnp.arange(count)

    def named(sizes, turn):
        used = int((sizes > 0).sum())
        fixed = max(1, used // 4)
        shifted = fixed + (places - fixed + turn * (used - fixed)) % max(1, count - fixed)
        return jnp.zeros((count,), jnp.int32).at[order[jnp.where(places < fixed, places, shifted)]].set(jnp.asarray(sizes, jnp.int32))

    sizes = jnp.where(number % 4 == 0, named(crowded, number // 4), named(common, number - number // 4 - 1))
    mixed = jax.random.permutation(jax.random.fold_in(own, 3), count)
    source_of, sink = mixed[0:count // 2 * 2:2], mixed[1:count // 2 * 2:2]
    margin = jnp.minimum(sizes[source_of] - 1, bound - sizes[sink]) // 2
    margin = jnp.where((source_of == order[0]) | (sink == order[0]) | (sizes[sink] == 0), 0, jnp.maximum(margin, 0))
    shifted = jax.random.randint(jax.random.fold_in(own, 4), (count // 2,), 0, 1 << 20) % (margin + 1)
    sizes = sizes.at[source_of].add(-shifted).at[sink].add(shifted)
    items = jnp.searchsorted(jnp.cumsum(sizes), jnp.arange(rows * top), side="right").astype(jnp.int32)
    table = items.reshape(top, rows).T
    table = table[jax.random.permutation(jax.random.fold_in(own, 1), rows)]
    turn = jax.random.randint(jax.random.fold_in(own, 2), (rows, 1), 0, top)
    return jnp.take_along_axis(table, (jnp.arange(top)[None, :] + turn) % top, axis=1)


def portions_of(amount, total, limit, slope, full):
    weights = [(1 << 20) // math.isqrt(standing ** slope) + 1 for standing in range(1, amount + 1)]
    largest = limit if full else min(limit, max(-(-total // amount), total * weights[0] // sum(weights)))
    least = 1 if total - largest >= amount - 1 else 0
    given, spare = [largest] + [least] * (amount - 1), total - largest - least * (amount - 1)
    while spare > 0:
        free = [i for i in range(1, amount) if given[i] < largest] or [i for i in range(1, amount) if given[i] < limit]
        whole, left = sum([weights[i] for i in free]), spare
        for i in free:
            extra = min(limit - given[i], max(1, left * weights[i] // whole), spare)
            given[i] = given[i] + extra
            spare = spare - extra
    return np.array(given)


def noise(rng, extent, scale, limit, cuts=(), kind=jnp.bfloat16):
    array = scale * jax.random.normal(rng, extent, jnp.float32)
    if cuts:
        array = array * block_levels(rng, extent, cuts, -0.22, 0.18)
    return jnp.clip(array, -limit, limit).astype(kind)


def setup_inputs(seed: int = 0) -> dict:
    streams_of = jax.random.split(jax.random.key(seed), 10)
    images = noise(streams_of[0], (NBLOCKS, BS, BS), 1.0, 6.0, ((0, 32),))
    inv_var = jnp.clip(jnp.exp(math.log(4.0) - 2.7725887 * jax.random.uniform(streams_of[1], (NBLOCKS, BS, BS), jnp.float32) ** block_levels(streams_of[1], (NBLOCKS, BS, BS), ((0, 32),), -0.2, 0.2)), 0.25, 4.0).astype(jnp.bfloat16)
    good_columns = plant((jax.random.randint(streams_of[2], (VISITS, BS), 0, 8) < 7).astype(jnp.int32), jax.random.fold_in(streams_of[2], 1), 0, 1)
    warp_rows = draw_warp_rows(jax.random.fold_in(streams_of[9], 71), 0)
    warp_cols = draw_warp_cols(jax.random.fold_in(streams_of[9], 71), 0)
    block_visit = plant(jax.random.randint(streams_of[5], (NBLOCKS,), 0, VD), jax.random.fold_in(streams_of[5], 1), 0, VD - 1).astype(jnp.int32)
    dest_tile_keys = jax.random.split(jax.random.fold_in(streams_of[6], 1), NBLOCKS // NB)
    dest_tile_turns = jax.random.permutation(jax.random.fold_in(streams_of[6], 3), NBLOCKS // NB)
    dest_tile = jax.vmap(lambda own, number: shared_out(jax.random.fold_in(streams_of[6], 2), own, number, NB, TILES, 1, CAP, 2))(dest_tile_keys, dest_tile_turns).reshape((NBLOCKS, 1))
    offsets = plant(jax.random.randint(streams_of[7], (NBLOCKS, 2), 0, (TY - BS) // STEP + 1), jax.random.fold_in(streams_of[7], 1), 0, ((TY - BS) // STEP + 1) - 1).astype(jnp.int32)
    psf_taps = jnp.clip(jax.random.uniform(streams_of[8], (PSF,), jnp.float32, 0.1, 1.0), 0.1, 1.0)
    return dict(images=images, inv_var=inv_var, good_columns=good_columns, warp_rows=warp_rows, warp_cols=warp_cols, block_visit=block_visit, dest_tile=dest_tile, offsets=offsets, psf_taps=psf_taps)


def box_sum(field, span, height, breadth):
    vertical = sum((field[offset:offset + height, :] for offset in range(span)))
    return sum((vertical[:, offset:offset + breadth] for offset in range(span)))

def filters(padded, taps, height, breadth):
    smooth = box_sum(padded, 3, height + 8, breadth + 8) / 9.0
    resid = padded[1:-1, 1:-1] - smooth
    local_var = box_sum(resid * resid, 9, height, breadth) / 81.0 + 1e-05
    rowwise = sum((taps[offset] * padded[2 + offset:2 + offset + height, :] for offset in range(taps.shape[0])))
    blurred = sum((taps[offset] * rowwise[:, 2 + offset:2 + offset + breadth] for offset in range(taps.shape[0])))
    return (blurred / jnp.sqrt(local_var), local_var)

def reference(images, inv_var, good_columns, warp_rows, warp_cols, block_visit, dest_tile, offsets, psf_taps):

    def place(canvas, number):
        group = number // PER_GROUP
        visit_id = (group * VD + block_visit[number]).astype(jnp.int32)
        good = good_columns[visit_id].astype(jnp.float32)
        weight = inv_var[number].astype(jnp.float32) * good[None, :]
        weighted = (weight * images[number].astype(jnp.float32)).astype(jnp.bfloat16)
        weight_plane = weight.astype(jnp.bfloat16)
        row_mat = warp_rows[visit_id]
        col_mat = warp_cols[visit_id]
        outputs = []
        for plane in (weighted, weight_plane):
            half = jnp.dot(row_mat, plane, preferred_element_type=jnp.float32).astype(jnp.bfloat16)
            outputs.append(jnp.dot(half, col_mat.T, preferred_element_type=jnp.float32).astype(jnp.bfloat16))
        stacked = jnp.stack(outputs).astype(jnp.float32)
        target = dest_tile[number, 0]
        row_start = (target // PATCH_COLS * TY + STEP * offsets[number, 0]).astype(jnp.int32)
        col_start = (target % PATCH_COLS * TX + STEP * offsets[number, 1]).astype(jnp.int32)
        anchor = jnp.zeros((), jnp.int32)
        current = lax.dynamic_slice(canvas, (anchor, row_start, col_start), (2, BS, BS))
        canvas = lax.dynamic_update_slice(canvas, current + stacked, (anchor, row_start, col_start))
        return (canvas, None)
    canvas = jnp.zeros((2, NY, NX), jnp.float32)
    canvas, _ = lax.scan(place, canvas, jnp.arange(NBLOCKS, dtype=jnp.int32))
    coadd = canvas[0] / jnp.maximum(canvas[1], 1.0)
    padded = jnp.pad(coadd, 5)
    detection, local_variance = filters(padded, psf_taps, NY, NX)
    return (detection, local_variance)
```

```python
import functools

import jax
import jax.numpy as jnp
from jax import lax
from jax.experimental import pallas as pl
from jax.experimental.pallas import tpu as pltpu
from jax.sharding import PartitionSpec as P

TY = 1024
TX = 1024
STEP = 128
CAP = 2
EDGE = 16
HALO = 8
SIDE = 128
ROWS = 64
MIB = 1 << 20


def warp_kernel(
    tiles,
    visit_ref,
    tile_ref,
    offset_ref,
    good_ref,
    rows_hbm,
    cols_hbm,
    var_hbm,
    *refs,
):
    more = (len(refs) - 9) // 2
    image_hbm, refs = refs[:more], refs[more:]
    out_hbm, code_ref, rows, cols, var = refs[:5]
    image = refs[5 : 5 + more]
    done, count, sems, out_sems = refs[5 + more :]
    blocks = var.shape[0]
    loads = [
        pltpu.make_async_copy(rows_hbm, rows, sems.at[0]),
        pltpu.make_async_copy(cols_hbm, cols, sems.at[1]),
    ]
    half = blocks // 2
    for part in range(2):
        span = pl.ds(part * half, half)
        loads.append(
            pltpu.make_async_copy(var_hbm.at[span], var.at[span], sems.at[2 + 2 * part])
        )
        if image:
            loads.append(
                pltpu.make_async_copy(
                    image_hbm[0].at[span], image[0].at[span], sems.at[3 + 2 * part]
                )
            )
    for load in loads:
        load.start()

    @pl.loop(0, tiles)
    def _(tile):
        count[tile] = 0
        for slot in range(CAP):
            code_ref[tile * CAP + slot] = -1

    per_part = 1 + len(image)
    for load in loads[: 2 + per_part]:
        load.wait()

    def one(block):
        visit = visit_ref[block]
        tile = tile_ref[block]
        rank = count[tile]
        count[tile] = rank + 1
        slot = tile * CAP + rank
        code_ref[slot] = offset_ref[2 * block] * 8 + offset_ref[2 * block + 1]
        good = good_ref[pl.ds(visit, 1), :].astype(jnp.float32)
        plane = var[block].astype(jnp.float32) * good
        if image:
            plane = plane * image[0][block].astype(jnp.float32)
        plane = plane.astype(jnp.bfloat16)
        turned = jnp.dot(rows[visit], plane, preferred_element_type=jnp.float32)
        warped = lax.dot_general(
            turned.astype(jnp.bfloat16),
            cols[visit],
            (((1,), (1,)), ((), ())),
            preferred_element_type=jnp.float32,
        )
        done[block] = warped.astype(jnp.bfloat16)
        pltpu.make_async_copy(done.at[block], out_hbm.at[slot], out_sems.at[block]).start()

    unroll = 4 if half % 4 == 0 else 1
    for part in range(2):
        if part:
            for load in loads[2 + per_part :]:
                load.wait()

        @pl.loop(part * half, (part + 1) * half, step=unroll)
        def _(block):
            for ahead in range(unroll):
                one(block + ahead)

    @pl.loop(0, blocks)
    def _(block):
        pltpu.make_async_copy(done.at[block], out_hbm.at[0], out_sems.at[block]).wait()


def warp(tiles, visit, tile, offset, good, rows, cols, var, *image):
    blocks, side, _ = var.shape
    smem = pl.BlockSpec(memory_space=pltpu.SMEM)
    anywhere = pl.BlockSpec(memory_space=pl.ANY)
    plane = pltpu.VMEM(var.shape, jnp.bfloat16)
    return pl.pallas_call(
        functools.partial(warp_kernel, tiles),
        out_shape=(
            jax.ShapeDtypeStruct((tiles * CAP, side, side), jnp.bfloat16),
            jax.ShapeDtypeStruct((tiles * CAP,), jnp.int32),
        ),
        in_specs=[smem, smem, smem, pl.BlockSpec(memory_space=pltpu.VMEM)]
        + [anywhere] * (3 + len(image)),
        out_specs=(anywhere, smem),
        scratch_shapes=[
            pltpu.VMEM(rows.shape, jnp.bfloat16),
            pltpu.VMEM(cols.shape, jnp.bfloat16),
            *[plane] * (1 + len(image)),
            plane,
            pltpu.SMEM((tiles,), jnp.int32),
            pltpu.SemaphoreType.DMA((6,)),
            pltpu.SemaphoreType.DMA((blocks,)),
        ],
        compiler_params=pltpu.CompilerParams(vmem_limit_bytes=32 * MIB),
        cost_estimate=pl.CostEstimate(
            flops=4 * blocks * side**3, bytes_accessed=4 * blocks * side**2 * 2, transcendentals=0
        ),
        name="warp_data" if image else "warp_weight",
    )(visit, tile, offset, good, rows, cols, var, *image)


def place_kernel(code_ref, blocks_ref, out_ref, edge_ref, total):
    step = pl.program_id(0)
    some, side, _ = blocks_ref.shape
    height, breadth = total.shape

    @pl.when(step == 0)
    def _():
        total[...] = jnp.zeros_like(total)

    for block in range(some):
        code = code_ref[step * some + block]

        @pl.when(code >= 0)
        def _():
            row = pl.multiple_of((code // 8) * STEP, STEP)
            col = pl.multiple_of((code % 8) * STEP, STEP)
            total[pl.ds(row, side), pl.ds(col, side)] += blocks_ref[block].astype(jnp.float32)

    @pl.when(step == pl.num_programs(0) - 1)
    def _():
        out_ref[...] = total[...].astype(jnp.bfloat16)
        edge_ref[:EDGE] = total[:EDGE].astype(jnp.bfloat16)
        edge_ref[EDGE : 2 * EDGE] = total[height - EDGE :].astype(jnp.bfloat16)
        edge_ref[2 * EDGE : 3 * EDGE] = total[:, :SIDE].T[:EDGE].astype(jnp.bfloat16)
        edge_ref[3 * EDGE :] = total[:, breadth - SIDE :].T[SIDE - EDGE :].astype(jnp.bfloat16)


def place(code, blocks):
    count, side, _ = blocks.shape
    some = 4
    return pl.pallas_call(
        place_kernel,
        grid_spec=pltpu.PrefetchScalarGridSpec(
            num_scalar_prefetch=1,
            grid=(count // some,),
            in_specs=[pl.BlockSpec((some, side, side), lambda step, code: (step, 0, 0))],
            out_specs=(
                pl.BlockSpec((TY, TX), lambda step, code: (0, 0)),
                pl.BlockSpec((4 * EDGE, TX), lambda step, code: (0, 0)),
            ),
            scratch_shapes=[pltpu.VMEM((TY, TX), jnp.float32)],
        ),
        out_shape=(
            jax.ShapeDtypeStruct((TY, TX), jnp.bfloat16),
            jax.ShapeDtypeStruct((4 * EDGE, TX), jnp.bfloat16),
        ),
        compiler_params=pltpu.CompilerParams(vmem_limit_bytes=32 * MIB),
        cost_estimate=pl.CostEstimate(
            flops=count * side**2, bytes_accessed=count * side**2 * 2 + TY * TX * 2, transcendentals=0
        ),
        name="place",
    )(code, blocks)


def visit_parts(shard):
    count = lax.axis_size("visit")
    if count == 1:
        return (shard,)
    if count == 2:
        return (shard, lax.ppermute(shard, "visit", [(0, 1), (1, 0)]))
    return (lax.psum(shard.astype(jnp.float32), "visit"),)


def ratio(data, weight):
    top = sum(part.astype(jnp.float32) for part in data)
    below = sum(part.astype(jnp.float32) for part in weight)
    return top / jnp.maximum(below, 1.0)


def neighbours(first, last, axis):
    count = lax.axis_size(axis)
    up = [(i, i + 1) for i in range(count - 1)]
    down = [(j, i) for i, j in up]
    return lax.ppermute(last, axis, up), lax.ppermute(first, axis, down)


def filter_kernel(parts, taps_ref, *refs):
    data, weight = refs[:parts], refs[parts : 2 * parts]
    above, below, left, right, detection_ref, variance_ref, coadd = refs[2 * parts :]
    height, breadth = detection_ref.shape
    wide = breadth + SIDE

    coadd[:HALO, :] = above[...]
    coadd[HALO + height :, :] = below[...]
    lanes = jnp.concatenate(
        [right[...], jnp.zeros((SIDE - 2 * HALO, height), jnp.float32), left[...]], axis=0
    )
    coadd[HALO : HALO + height, breadth:] = lanes.T

    @pl.loop(0, height, step=ROWS)
    def _(start):
        start = pl.multiple_of(start, ROWS)
        rows = pl.ds(start, ROWS)
        coadd[pl.ds(pl.multiple_of(start + HALO, HALO), ROWS), :breadth] = ratio(
            [ref[rows, :] for ref in data], [ref[rows, :] for ref in weight]
        )

    taps = [taps_ref[tap] for tap in range(7)]
    tall = ROWS + 2 * HALO

    def down(field, by):
        return field if by == 0 else pltpu.roll(field, by % tall, 0)

    def across(field, by):
        return field if by == 0 else pltpu.roll(field, by % wide, 1)

    def three(field, shift, by):
        return field + shift(field, by) + shift(field, -by)

    @pl.loop(0, height, step=ROWS)
    def _(start):
        start = pl.multiple_of(start, ROWS)
        field = coadd[pl.ds(start, tall), :]
        resid = field - three(three(field, down, 1), across, 1) * (1.0 / 9.0)
        square = resid * resid
        tower = three(three(square, down, 1), down, 3)[HALO : HALO + ROWS]
        box = three(three(tower, across, 1), across, 3)
        variance = box[:, :breadth] * (1.0 / 81.0) + 1e-05
        rowwise = sum(taps[tap] * down(field, 3 - tap) for tap in range(7))[HALO : HALO + ROWS]
        blurred = sum(taps[tap] * across(rowwise, 3 - tap) for tap in range(7))
        rows = pl.ds(start, ROWS)
        variance_ref[rows, :] = variance
        detection_ref[rows, :] = blurred[:, :breadth] * lax.rsqrt(variance)


def filters(taps, data, weight, halos):
    shape = jax.ShapeDtypeStruct((TY, TX), jnp.float32)
    vmem = pl.BlockSpec(memory_space=pltpu.VMEM)
    return pl.pallas_call(
        functools.partial(filter_kernel, len(data)),
        out_shape=(shape, shape),
        in_specs=[pl.BlockSpec(memory_space=pltpu.SMEM)]
        + [vmem] * (2 * len(data) + len(halos)),
        out_specs=(vmem, vmem),
        scratch_shapes=[pltpu.VMEM((TY + 2 * HALO, TX + SIDE), jnp.float32)],
        compiler_params=pltpu.CompilerParams(vmem_limit_bytes=48 * MIB),
        name="filters",
    )(taps, *data, *weight, *halos)


def per_device(
    images, inv_var, good_columns, warp_rows, warp_cols, block_visit, dest_tile, offsets, psf_taps
):
    tiles = lax.axis_size("py") * lax.axis_size("px")
    sky = ("py", "px")
    tile, offset = dest_tile[:, 0], offsets.reshape(-1)
    common = (tiles, block_visit, tile, offset, good_columns, warp_rows, warp_cols)

    def send(blocks):
        return lax.all_to_all(blocks, sky, split_axis=0, concat_axis=0, tiled=True)

    weight_out, code_out = warp(*common, inv_var)
    weight_in = send(weight_out)
    code = send(code_out)
    data_out, _ = warp(*common, inv_var, images)
    weight_in, data_out = lax.optimization_barrier((weight_in, data_out))
    data_in = send(data_out)

    weight_own, weight_edge_own = place(code, weight_in)
    weight_edge = visit_parts(weight_edge_own)
    weight = visit_parts(weight_own)
    data_own, data_edge_own = place(code, data_in)
    data_edge = visit_parts(data_edge_own)
    data = visit_parts(data_own)

    edge = ratio(data_edge, weight_edge)
    first_row, last_row, first_col, last_col = (
        edge[:HALO],
        edge[2 * EDGE - HALO : 2 * EDGE],
        edge[2 * EDGE : 2 * EDGE + HALO],
        edge[4 * EDGE - HALO :],
    )
    above, below = neighbours(first_row, last_row, "py")
    left, right = neighbours(
        jnp.concatenate([first_col, above[:, :SIDE], below[:, :SIDE]], axis=1),
        jnp.concatenate([last_col, above[:, TX - SIDE :], below[:, TX - SIDE :]], axis=1),
        "px",
    )
    from_left = jnp.arange(SIDE, dtype=jnp.int32)[None, :] >= SIDE // 2

    def corners(at):
        span = slice(TY + at * SIDE, TY + (at + 1) * SIDE)
        return jnp.where(from_left, left[:, span], right[:, span])

    above = jnp.concatenate([above, corners(0)], axis=1)
    below = jnp.concatenate([below, corners(1)], axis=1)
    return filters(psf_taps, data, weight, (above, below, left[:, :TY], right[:, :TY]))


def solution(mesh):
    in_specs = (
        P(("visit", "py", "px"), None, None),
        P(("visit", "py", "px"), None, None),
        P("visit", None),
        P("visit", None, None),
        P("visit", None, None),
        P(("visit", "py", "px")),
        P(("visit", "py", "px"), None),
        P(("visit", "py", "px"), None),
        P(),
    )
    out_specs = (P("py", "px"), P("py", "px"))
    return jax.shard_map(
        per_device, mesh=mesh, in_specs=in_specs, out_specs=out_specs, check_vma=False
    )
```

```python
import functools

import jax
import jax.numpy as jnp
from jax import lax
from jax.experimental import pallas as pl
from jax.experimental.pallas import tpu as pltpu
from jax.sharding import PartitionSpec as P

TY = 1024
TX = 1024
STEP = 128
CAP = 2
UNITS = TY // STEP
HALO = 8
SIDE = 128
WIDE = TX + SIDE
GROUP = 4
MIB = 1 << 20
EVERY = ("visit", "py", "px")
HBM = pl.BlockSpec(memory_space=pltpu.HBM)
SMEM = pl.BlockSpec(memory_space=pltpu.SMEM)
VMEM = pl.BlockSpec(memory_space=pltpu.VMEM)


def shares(visits):
    if visits == 2:
        edge, inner = 48, 16
        return [(edge, (0, STEP - edge)), (inner, (edge, edge + inner))]
    rows = STEP // visits
    return [(rows, tuple(visit * rows for visit in range(visits)))]


def warp_kernel(
    tiles, share, visit_ref, tile_ref, good_ref, rows_hbm, cols_hbm, var_hbm, image_hbm, out_hbm,
    rows, cols, var, image, done, count, table_sems, sems, out_sems,
):
    blocks, side, _ = var.shape
    some, firsts = share
    groups = blocks // GROUP
    tables = [
        pltpu.make_async_copy(rows_hbm, rows, table_sems.at[0]),
        pltpu.make_async_copy(cols_hbm, cols, table_sems.at[1]),
    ]

    def loads(group):
        span = pl.ds(group * GROUP, GROUP)
        return (
            pltpu.make_async_copy(var_hbm.at[span], var.at[span], sems.at[group, 0]),
            pltpu.make_async_copy(image_hbm.at[span], image.at[span], sems.at[group, 1]),
        )

    for load in tables:
        load.start()
    for group in range(groups):
        for load in loads(group):
            load.start()

    @pl.loop(0, tiles)
    def _(tile):
        count[tile] = 0

    for load in tables:
        load.wait()

    strips = [first + strip * STEP for first in firsts for strip in range(side // STEP)]
    tall = some * len(strips)
    part = tall // len(firsts)

    @pl.loop(0, groups)
    def _(group):
        for load in loads(group):
            load.wait()
        visits = [visit_ref[group * GROUP + ahead] for ahead in range(GROUP)]
        planes, turned, warped = [], [], []
        for ahead in range(GROUP):
            block = group * GROUP + ahead
            good = good_ref[pl.ds(visits[ahead], 1), :].astype(jnp.float32)
            weight = var[block].astype(jnp.float32) * good
            data = weight * image[block].astype(jnp.float32)
            planes.append(
                jnp.concatenate([data.astype(jnp.bfloat16), weight.astype(jnp.bfloat16)], axis=1)
            )
        for ahead in range(GROUP):
            matrix = jnp.concatenate(
                [rows[visits[ahead], first : first + some, :] for first in strips], axis=0
            )
            turned.append(
                jnp.dot(matrix, planes[ahead], preferred_element_type=jnp.float32).astype(jnp.bfloat16)
            )
        for ahead in range(GROUP):
            both = jnp.concatenate([turned[ahead][:, :side], turned[ahead][:, side:]], axis=0)
            warped.append(
                lax.dot_general(
                    both,
                    cols[visits[ahead]],
                    (((1,), (1,)), ((), ())),
                    preferred_element_type=jnp.float32,
                ).astype(jnp.bfloat16)
            )
        for ahead in range(GROUP):
            block = group * GROUP + ahead
            for visit in range(len(firsts)):
                for plane in range(2):
                    start = plane * tall + visit * part
                    done[block, visit, plane * part : (plane + 1) * part, :] = warped[ahead][
                        start : start + part
                    ]
        for ahead in range(GROUP):
            block = group * GROUP + ahead
            tile = tile_ref[block]
            rank = count[tile]
            count[tile] = rank + 1
            for visit in range(len(firsts)):
                pltpu.make_async_copy(
                    done.at[block, visit],
                    out_hbm.at[(visit * tiles + tile) * CAP + rank],
                    out_sems.at[block, visit],
                ).start()

    @pl.loop(0, blocks)
    def _(block):
        for visit in range(len(firsts)):
            pltpu.make_async_copy(
                done.at[block, visit], out_hbm.at[0], out_sems.at[block, visit]
            ).wait()


def warp(tiles, share, visit, tile, good, rows, cols, var, image):
    blocks, side, _ = var.shape
    some, firsts = share
    tall = 2 * (side // STEP) * some
    visits = len(firsts)
    return pl.pallas_call(
        functools.partial(warp_kernel, tiles, share),
        out_shape=jax.ShapeDtypeStruct((visits * tiles * CAP, tall, side), jnp.bfloat16),
        in_specs=[SMEM, SMEM, VMEM, HBM, HBM, HBM, HBM],
        out_specs=HBM,
        scratch_shapes=[
            pltpu.VMEM(rows.shape, jnp.bfloat16),
            pltpu.VMEM(cols.shape, jnp.bfloat16),
            pltpu.VMEM(var.shape, jnp.bfloat16),
            pltpu.VMEM(var.shape, jnp.bfloat16),
            pltpu.VMEM((blocks, visits, tall, side), jnp.bfloat16),
            pltpu.SMEM((tiles,), jnp.int32),
            pltpu.SemaphoreType.DMA((2,)),
            pltpu.SemaphoreType.DMA((blocks // GROUP, 2)),
            pltpu.SemaphoreType.DMA((blocks, visits)),
        ],
        compiler_params=pltpu.CompilerParams(vmem_limit_bytes=40 * MIB),
        cost_estimate=pl.CostEstimate(
            flops=8 * blocks * side**3, bytes_accessed=8 * blocks * side**2, transcendentals=0
        ),
        name="warp",
    )(visit, tile, good, rows, cols, var, image)


def place_kernel(code_ref, blocks_ref, coadd_ref, strip_ref, data, weight):
    step = pl.program_id(0)
    some, tall, side = blocks_ref.shape
    part = tall // 2
    lot = data.shape[0] // UNITS

    @pl.when(step == 0)
    def _():
        data[...] = jnp.zeros_like(data)
        weight[...] = jnp.zeros_like(weight)

    for block in range(some):
        code = code_ref[step * some + block]

        @pl.when(code >= 0)
        def _():
            row = pl.multiple_of((code // 8) * lot, lot)
            col = pl.multiple_of((code % 8) * STEP, STEP)
            cells = (pl.ds(row, part), pl.ds(col, side))
            data[cells] += blocks_ref[block, :part].astype(jnp.float32)
            weight[cells] += blocks_ref[block, part:].astype(jnp.float32)

    @pl.when(step == pl.num_programs(0) - 1)
    def _():
        coadd = data[...] / jnp.maximum(weight[...], 1.0)
        coadd_ref[...] = coadd
        strip_ref[:HALO] = coadd[:, :SIDE].T[:HALO]
        strip_ref[HALO:] = coadd[:, TX - SIDE :].T[SIDE - HALO :]


def place(code, blocks):
    count, tall, side = blocks.shape
    some = 8
    height = tall // 4 * UNITS
    return pl.pallas_call(
        place_kernel,
        grid_spec=pltpu.PrefetchScalarGridSpec(
            num_scalar_prefetch=1,
            grid=(count // some,),
            in_specs=[pl.BlockSpec((some, tall, side), lambda step, code: (step, 0, 0))],
            out_specs=(
                pl.BlockSpec((height, TX), lambda step, code: (0, 0)),
                pl.BlockSpec((2 * HALO, height), lambda step, code: (0, 0)),
            ),
            scratch_shapes=[pltpu.VMEM((height, TX), jnp.float32)] * 2,
        ),
        out_shape=(
            jax.ShapeDtypeStruct((height, TX), jnp.float32),
            jax.ShapeDtypeStruct((2 * HALO, height), jnp.float32),
        ),
        compiler_params=pltpu.CompilerParams(vmem_limit_bytes=32 * MIB),
        cost_estimate=pl.CostEstimate(
            flops=count * tall * side, bytes_accessed=count * tall * side * 2, transcendentals=0
        ),
        name="place",
    )(code, blocks)


def beside(axis):
    count = lax.axis_size(axis)
    up = [(i, i + 1) for i in range(count - 1)]
    return up, [(j, i) for i, j in up]


def neighbours(first, last, axis):
    up, down = beside(axis)
    return lax.ppermute(last, axis, up), lax.ppermute(first, axis, down)


def spread(coadd, strip):
    visits = lax.axis_size("visit")
    left, right = neighbours(strip[:HALO], strip[HALO:], "px")
    if visits == 2:
        swap = [(0, 1), (1, 0)]
        count = lax.axis_size("px")
        up, down = beside("px")

        def crossed(pairs):
            return [(v * count + i, (1 - v) * count + j) for v in range(2) for i, j in pairs]

        other_left = lax.ppermute(strip[HALO:], ("visit", "px"), crossed(up))
        other_right = lax.ppermute(strip[:HALO], ("visit", "px"), crossed(down))
        other = lax.ppermute(coadd, "visit", swap)
        return [(coadd, left, right), (other, other_left, other_right)]
    if visits == 1:
        return [(coadd, left, right)]
    every = [lax.all_gather(part, "visit") for part in (coadd, left, right)]
    return [tuple(part[visit] for part in every) for visit in range(visits)]


def rows_between(parts, lot):
    mine = lax.axis_index("visit")
    pair = len(parts) == 2
    top = parts[0][0][:HALO]
    bottom = parts[-1][0][UNITS * lot - HALO :]
    if pair:
        top = jnp.where(mine == 0, top, parts[1][0][:HALO])
        bottom = jnp.where(mine == 1, parts[0][0][UNITS * lot - HALO :], bottom)
    above, below = neighbours(top, bottom, "py")
    both = jnp.concatenate([above, below], axis=0)
    left, right = neighbours(both[:, :SIDE], both[:, TX - SIDE :], "px")
    from_left = jnp.arange(SIDE, dtype=jnp.int32)[None, :] >= SIDE // 2
    return jnp.concatenate([both, jnp.where(from_left, left, right)], axis=1)


def stage_kernel(plan, lots, *refs):
    mine_ref, taps_ref, between_ref = refs[:3]
    fields, copies, outs = plan
    visits = fields["visits"]
    at = 3
    chunks = []
    for lot in lots:
        parts = []
        for _ in range(visits):
            parts.append(refs[at : at + 3])
            at += 3
        chunks.append(parts)
    at += fields["aliased"]
    detection_hbm, variance_hbm = refs[at : at + 2]
    field, detection, variance, sems = refs[at + 2 : at + 6]
    sides = refs[at + 6 :]
    spans, tall, _ = field.shape

    which = 0
    held = []
    for parts in chunks:
        group = []
        for cells, left, right in parts:
            side = sides[which]
            which += 1
            height = cells.shape[0]
            side[...] = jnp.concatenate(
                [right[...], jnp.zeros((SIDE - 2 * HALO, height), jnp.float32), left[...]], axis=0
            ).T
            group.append((cells, side))
        held.append(group)

    def assemble(order):
        for chunk, visit, first, rows, at_row, begin, end, shift in copies:
            cells, side = held[chunk][order[visit]]
            lot = lots[chunk]

            @pl.loop(begin, end)
            def _(unit):
                start = pl.multiple_of(unit * lot + first, HALO)
                into = pl.ds(at_row, rows)
                field[unit + shift, into, :TX] = cells[pl.ds(start, rows), :]
                field[unit + shift, into, TX:] = side[pl.ds(start, rows), :]

    if visits == 2:
        for flip in range(2):

            @pl.when(mine_ref[0] == flip)
            def _():
                assemble((0, 1) if flip == 0 else (1, 0))

    else:
        assemble(tuple(range(visits)))
    if fields["between"]:
        above_at, below_at = fields["between"]
        field[0, above_at : above_at + HALO, :] = between_ref[:HALO, :]
        field[spans - 1, below_at : below_at + HALO, :] = between_ref[HALO:, :]

    taps = [taps_ref[tap] for tap in range(7)]

    def down(value, by):
        return value if by == 0 else pltpu.roll(value, by % tall, 0)

    def across(value, by):
        return value if by == 0 else pltpu.roll(value, by % WIDE, 1)

    def three(value, shift, by):
        return value + shift(value, by) + shift(value, -by)

    def stores(unit, source, rows, target):
        return [
            pltpu.make_async_copy(
                scratch.at[unit, pl.ds(source, rows)], hbm.at[pl.ds(target, rows)], sems.at[unit, at]
            )
            for at, (scratch, hbm) in enumerate(
                ((detection, detection_hbm), (variance, variance_hbm))
            )
        ]

    @pl.loop(0, spans)
    def _(unit):
        value = field[unit]
        resid = value - three(three(value, down, 1), across, 1) * (1.0 / 9.0)
        square = resid * resid
        tower = three(three(square, down, 1), down, 3)[HALO : tall - HALO]
        box = three(three(tower, across, 1), across, 3)
        local = box[:, :TX] * (1.0 / 81.0) + 1e-05
        rowwise = sum(taps[tap] * down(value, 3 - tap) for tap in range(7))[HALO : tall - HALO]
        blurred = sum(taps[tap] * across(rowwise, 3 - tap) for tap in range(7))
        variance[unit] = local
        detection[unit] = blurred[:, :TX] * lax.rsqrt(local)
        for begin, end, source, rows, shift in outs:

            @pl.when((unit >= begin) & (unit < end))
            def _():
                target = pl.multiple_of(unit * STEP + shift, HALO)
                for store in stores(unit, source, rows, target):
                    store.start()

    @pl.loop(0, spans)
    def _(unit):
        for begin, end, source, rows, shift in outs:

            @pl.when((unit >= begin) & (unit < end))
            def _():
                for store in stores(unit, source, rows, 0):
                    store.wait()


def stage(plan, mine, taps, between, chunks, lots, held=()):
    fields, _, _ = plan
    spans, tall = fields["spans"], fields["tall"]
    shape = jax.ShapeDtypeStruct((TY, TX), jnp.float32)
    flat = [array for parts in chunks for part in parts for array in part]
    first = 3 + len(flat)
    return pl.pallas_call(
        functools.partial(stage_kernel, plan, lots),
        out_shape=(shape, shape),
        in_specs=[SMEM, SMEM, VMEM] + [VMEM] * len(flat) + [HBM] * len(held),
        out_specs=(HBM, HBM),
        input_output_aliases={first + at: at for at in range(len(held))},
        scratch_shapes=[
            pltpu.VMEM((spans, tall, WIDE), jnp.float32),
            pltpu.VMEM((spans, tall - 2 * HALO, TX), jnp.float32),
            pltpu.VMEM((spans, tall - 2 * HALO, TX), jnp.float32),
            pltpu.SemaphoreType.DMA((spans, 2)),
        ]
        + [pltpu.VMEM((part[0].shape[0], SIDE), jnp.float32) for parts in chunks for part in parts],
        compiler_params=pltpu.CompilerParams(vmem_limit_bytes=56 * MIB),
        cost_estimate=pl.CostEstimate(
            flops=80 * spans * tall * WIDE, bytes_accessed=12 * spans * tall * WIDE, transcendentals=0
        ),
        name="stage",
    )(mine, taps, between, *flat, *held)


def outer_plan(lot):
    fields = dict(visits=2, aliased=0, spans=UNITS + 1, tall=2 * lot, between=(lot - HALO, lot))
    copies = [(0, 1, 0, lot, 0, 0, UNITS, 1), (0, 0, 0, lot, lot, 0, UNITS, 0)]
    rows = lot - HALO
    outs = [
        (0, 1, rows, rows, 0),
        (1, UNITS, 0, 2 * rows, -rows),
        (UNITS, UNITS + 1, 0, rows, -rows),
    ]
    return fields, copies, outs


def inner_plan(lot, inner):
    edge = 2 * HALO
    tall = 2 * inner + 2 * edge
    fields = dict(visits=2, aliased=2, spans=UNITS, tall=tall, between=None)
    copies = [
        (0, 0, lot - edge, edge, 0, 0, UNITS, 0),
        (1, 0, 0, inner, edge, 0, UNITS, 0),
        (1, 1, 0, inner, edge + inner, 0, UNITS, 0),
        (0, 1, 0, edge, edge + 2 * inner, 0, UNITS, 0),
    ]
    return fields, copies, [(0, UNITS, 0, tall - edge, lot - HALO)]


def whole_plan(lot, visits):
    fields = dict(
        visits=visits, aliased=0, spans=UNITS, tall=STEP + 2 * HALO, between=(0, HALO + STEP)
    )
    copies = [(0, visit, 0, lot, HALO + visit * lot, 0, UNITS, 0) for visit in range(visits)]
    copies.append((0, visits - 1, lot - HALO, HALO, 0, 0, UNITS - 1, 1))
    copies.append((0, 0, 0, HALO, HALO + STEP, 1, UNITS, -1))
    return fields, copies, [(0, UNITS, 0, STEP, 0)]


def slot_codes(tile, offsets):
    note = tile * 64 + offsets[:, 0] * 8 + offsets[:, 1]
    notes = lax.all_gather(note, EVERY)
    mine = (notes // 64) == lax.axis_index("py") * lax.axis_size("px") + lax.axis_index("px")
    blocks = notes.shape[1]
    at = jnp.arange(blocks, dtype=jnp.int32)
    before = mine[:, None, :] & (at[None, None, :] < at[None, :, None])
    rank = jnp.sum(before.astype(jnp.int32), axis=2)
    slot = jnp.arange(CAP, dtype=jnp.int32)[None, :, None]
    chosen = mine[:, None, :] & (rank[:, None, :] == slot)
    return jnp.max(jnp.where(chosen, (notes % 64)[:, None, :], -1), axis=2).reshape(-1)


def per_device(
    images, inv_var, good_columns, warp_rows, warp_cols, block_visit, dest_tile, offsets, psf_taps
):
    tiles = lax.axis_size("py") * lax.axis_size("px")
    visits = lax.axis_size("visit")
    tile = dest_tile[:, 0]
    plan = shares(visits)
    lots = [rows for rows, _ in plan]
    mine = lax.axis_index("visit").astype(jnp.int32).reshape(1)

    def make(share):
        return warp(
            tiles, share, block_visit, tile, good_columns, warp_rows, warp_cols, inv_var, images
        )

    def send(blocks):
        return lax.all_to_all(blocks, EVERY, split_axis=0, concat_axis=0, tiled=True)

    arrived = send(make(plan[0]))
    code = slot_codes(tile, offsets)
    if len(plan) == 1:
        parts = spread(*place(code, arrived))
        between = rows_between(parts, lots[0])
        return stage(whole_plan(lots[0], visits), mine, psf_taps, between, [parts], lots)

    later = make(plan[1])
    arrived, later = lax.optimization_barrier((arrived, later))
    second = send(later)
    parts = spread(*place(code, arrived))
    between = rows_between(parts, lots[0])
    held = stage(outer_plan(lots[0]), mine, psf_taps, between, [parts], lots[:1])
    second, held = lax.optimization_barrier((second, held))
    more = spread(*place(code, second))
    return stage(inner_plan(*lots), mine, psf_taps, between, [parts, more], lots, held)


def solution(mesh):
    in_specs = (
        P(EVERY, None, None),
        P(EVERY, None, None),
        P("visit", None),
        P("visit", None, None),
        P("visit", None, None),
        P(EVERY),
        P(EVERY, None),
        P(EVERY, None),
        P(),
    )
    out_specs = (P("py", "px"), P("py", "px"))
    return jax.shard_map(
        per_device, mesh=mesh, in_specs=in_specs, out_specs=out_specs, check_vma=False
    )
```

```python
import functools

import jax
import jax.numpy as jnp
from jax import lax
from jax.experimental import pallas as pl
from jax.experimental.pallas import tpu as pltpu
from jax.sharding import PartitionSpec as P

TY = 1024
TX = 1024
STEP = 128
CAP = 2
UNITS = TY // STEP
HALO = 8
SIDE = 128
WIDE = TX + SIDE
GROUP = 4
NOTE = 16
MIB = 1 << 20
EVERY = ("visit", "py", "px")
HBM = pl.BlockSpec(memory_space=pltpu.HBM)
SMEM = pl.BlockSpec(memory_space=pltpu.SMEM)
VMEM = pl.BlockSpec(memory_space=pltpu.VMEM)


def shares(visits):
    if visits == 2:
        edge, inner = 48, 16
        return [(edge, (0, STEP - edge)), (inner, (edge, edge + inner))]
    rows = STEP // visits
    return [(rows, tuple(visit * rows for visit in range(visits)))]


def warp_kernel(
    tiles, share, noted, visit_ref, tile_ref, offset_ref, good_ref, rows_hbm, cols_hbm, var_hbm,
    image_hbm, out_hbm, rows, cols, var, image, done, note, count, table_sems, sems, out_sems,
):
    blocks, side, _ = var.shape
    some, firsts = share
    groups = blocks // GROUP
    slot_rows = done.shape[2]
    tables = [
        pltpu.make_async_copy(rows_hbm, rows, table_sems.at[0]),
        pltpu.make_async_copy(cols_hbm, cols, table_sems.at[1]),
    ]

    def loads(group):
        span = pl.ds(group * GROUP, GROUP)
        return (
            pltpu.make_async_copy(var_hbm.at[span], var.at[span], sems.at[group, 0]),
            pltpu.make_async_copy(image_hbm.at[span], image.at[span], sems.at[group, 1]),
        )

    for load in tables:
        load.start()
    for group in range(groups):
        for load in loads(group):
            load.start()

    @pl.loop(0, tiles)
    def _(tile):
        count[tile] = 0

    if noted:
        note[...] = jnp.full(note.shape, -1, jnp.bfloat16)
        slot_of_lane = lax.broadcasted_iota(jnp.int32, (NOTE, SIDE), 1) // (SIDE // CAP)

    for load in tables:
        load.wait()

    strips = [first + strip * STEP for first in firsts for strip in range(side // STEP)]
    tall = some * len(strips)
    part = tall // len(firsts)

    @pl.loop(0, groups)
    def _(group):
        for load in loads(group):
            load.wait()
        visits = [visit_ref[group * GROUP + ahead] for ahead in range(GROUP)]
        planes, turned, warped = [], [], []
        for ahead in range(GROUP):
            block = group * GROUP + ahead
            good = good_ref[pl.ds(visits[ahead], 1), :].astype(jnp.float32)
            weight = var[block].astype(jnp.float32) * good
            data = weight * image[block].astype(jnp.float32)
            planes.append(
                jnp.concatenate([data.astype(jnp.bfloat16), weight.astype(jnp.bfloat16)], axis=1)
            )
        for ahead in range(GROUP):
            matrix = jnp.concatenate(
                [rows[visits[ahead], first : first + some, :] for first in strips], axis=0
            )
            turned.append(
                jnp.dot(matrix, planes[ahead], preferred_element_type=jnp.float32).astype(jnp.bfloat16)
            )
        for ahead in range(GROUP):
            both = jnp.concatenate([turned[ahead][:, :side], turned[ahead][:, side:]], axis=0)
            warped.append(
                lax.dot_general(
                    both,
                    cols[visits[ahead]],
                    (((1,), (1,)), ((), ())),
                    preferred_element_type=jnp.float32,
                ).astype(jnp.bfloat16)
            )
        for ahead in range(GROUP):
            block = group * GROUP + ahead
            for visit in range(len(firsts)):
                for half in range(side // SIDE):
                    for plane in range(2):
                        start = plane * tall + visit * part
                        into = (2 * half + plane) * part
                        done[block, visit, into : into + part, :] = warped[ahead][
                            start : start + part, half * SIDE : (half + 1) * SIDE
                        ]
        for ahead in range(GROUP):
            block = group * GROUP + ahead
            tile = tile_ref[block]
            rank = count[tile]
            count[tile] = rank + 1
            for visit in range(len(firsts)):
                target = visit * tiles + tile
                pltpu.make_async_copy(
                    done.at[block, visit],
                    out_hbm.at[target, pl.ds(pl.multiple_of(rank * slot_rows, NOTE), slot_rows)],
                    out_sems.at[block, visit],
                ).start()
                if noted:
                    code = offset_ref[2 * block] * 8 + offset_ref[2 * block + 1]
                    note[target] = jnp.where(
                        slot_of_lane == rank, code.astype(jnp.float32), note[target].astype(jnp.float32)
                    ).astype(jnp.bfloat16)

    if noted:
        notes = pltpu.make_async_copy(
            note, out_hbm.at[:, pl.ds(CAP * slot_rows, NOTE)], table_sems.at[0]
        )
        notes.start()

    @pl.loop(0, blocks)
    def _(block):
        for visit in range(len(firsts)):
            pltpu.make_async_copy(
                done.at[block, visit], out_hbm.at[0, pl.ds(0, slot_rows)], out_sems.at[block, visit]
            ).wait()

    if noted:
        notes.wait()


def warp(tiles, share, noted, visit, tile, offset, good, rows, cols, var, image):
    blocks, side, _ = var.shape
    some, firsts = share
    slot_rows = 2 * (side // STEP) * some * (side // SIDE)
    visits = len(firsts)
    return pl.pallas_call(
        functools.partial(warp_kernel, tiles, share, noted),
        out_shape=jax.ShapeDtypeStruct(
            (visits * tiles, CAP * slot_rows + noted * NOTE, SIDE), jnp.bfloat16
        ),
        in_specs=[SMEM, SMEM, SMEM, VMEM, HBM, HBM, HBM, HBM],
        out_specs=HBM,
        scratch_shapes=[
            pltpu.VMEM(rows.shape, jnp.bfloat16),
            pltpu.VMEM(cols.shape, jnp.bfloat16),
            pltpu.VMEM(var.shape, jnp.bfloat16),
            pltpu.VMEM(var.shape, jnp.bfloat16),
            pltpu.VMEM((blocks, visits, slot_rows, SIDE), jnp.bfloat16),
            pltpu.VMEM((visits * tiles, NOTE, SIDE), jnp.bfloat16),
            pltpu.SMEM((tiles,), jnp.int32),
            pltpu.SemaphoreType.DMA((2,)),
            pltpu.SemaphoreType.DMA((blocks // GROUP, 2)),
            pltpu.SemaphoreType.DMA((blocks, visits)),
        ],
        compiler_params=pltpu.CompilerParams(vmem_limit_bytes=60 * MIB),
        cost_estimate=pl.CostEstimate(
            flops=8 * blocks * side**3, bytes_accessed=8 * blocks * side**2, transcendentals=0
        ),
        name="warp",
    )(visit, tile, offset, good, rows, cols, var, image)


def place_kernel(part, code_ref, blocks_ref, coadd_ref, strip_ref, edge_ref, data, weight):
    step = pl.program_id(0)
    some = blocks_ref.shape[0]
    height = data.shape[0]
    lot = height // UNITS

    @pl.when(step == 0)
    def _():
        data[...] = jnp.zeros_like(data)
        weight[...] = jnp.zeros_like(weight)

    for block in range(some):
        for slot in range(CAP):
            code = code_ref[(step * some + block) * CAP + slot]

            @pl.when(code >= 0)
            def _():
                row = pl.multiple_of((code // 8) * lot, lot)
                for half in range(2):
                    col = pl.multiple_of((code % 8 + half) * STEP, STEP)
                    cells = (pl.ds(row, part), pl.ds(col, STEP))
                    first = (slot * 2 + half) * 2 * part
                    data[cells] += blocks_ref[block, first : first + part].astype(jnp.float32)
                    weight[cells] += blocks_ref[block, first + part : first + 2 * part].astype(
                        jnp.float32
                    )

    @pl.when(step == pl.num_programs(0) - 1)
    def _():
        coadd = data[...] / jnp.maximum(weight[...], 1.0)
        coadd_ref[...] = coadd.astype(coadd_ref.dtype)
        strip_ref[:HALO] = coadd[:, :SIDE].T[:HALO]
        strip_ref[HALO:] = coadd[:, TX - SIDE :].T[SIDE - HALO :]
        edge_ref[:HALO] = coadd[:HALO]
        edge_ref[HALO:] = coadd[height - HALO :]


def place(code, blocks, lot, dtype):
    count, tall, side = blocks.shape
    some = 4
    height = lot * UNITS
    shapes = [((height, TX), dtype), ((2 * HALO, height), jnp.float32), ((2 * HALO, TX), jnp.float32)]
    return pl.pallas_call(
        functools.partial(place_kernel, 2 * lot),
        grid_spec=pltpu.PrefetchScalarGridSpec(
            num_scalar_prefetch=1,
            grid=(count // some,),
            in_specs=[pl.BlockSpec((some, tall, side), lambda step, code: (step, 0, 0))],
            out_specs=[pl.BlockSpec(shape, lambda step, code: (0, 0)) for shape, _ in shapes],
            scratch_shapes=[pltpu.VMEM((height, TX), jnp.float32)] * 2,
        ),
        out_shape=[jax.ShapeDtypeStruct(*shape) for shape in shapes],
        compiler_params=pltpu.CompilerParams(vmem_limit_bytes=32 * MIB),
        cost_estimate=pl.CostEstimate(
            flops=count * tall * side, bytes_accessed=count * tall * side * 2, transcendentals=0
        ),
        name="place",
    )(code, blocks)


def beside(axis):
    count = lax.axis_size(axis)
    up = [(i, i + 1) for i in range(count - 1)]
    return up, [(j, i) for i, j in up]


def neighbours(first, last, axis):
    up, down = beside(axis)
    return lax.ppermute(last, axis, up), lax.ppermute(first, axis, down)


def spread(coadd, strip):
    visits = lax.axis_size("visit")
    if visits == 2:
        swap = [(0, 1), (1, 0)]
        other = lax.ppermute(coadd, "visit", swap)
        beyond = jnp.concatenate(neighbours(strip[:HALO], strip[HALO:], "px"), axis=0)
        return [(coadd, beyond), (other, lax.ppermute(beyond, "visit", swap))]
    beyond = jnp.concatenate(neighbours(strip[:HALO], strip[HALO:], "px"), axis=0)
    if visits == 1:
        return [(coadd, beyond)]
    every = [lax.all_gather(part, "visit") for part in (coadd, beyond)]
    return [tuple(part[visit] for part in every) for visit in range(visits)]


def widened(rows, beyond):
    corner = beyond.T
    gap = jnp.zeros((HALO, SIDE - 2 * HALO), jnp.float32)
    return jnp.concatenate([rows, corner[:, HALO:], gap, corner[:, :HALO]], axis=1)


def rows_between(edge, parts):
    visits = len(parts)
    height = parts[0][1].shape[1]
    if visits != 2:
        last = widened(edge[0][HALO:], parts[-1][1][:, height - HALO :])
        first = widened(edge[1][:HALO], parts[0][1][:, :HALO])
        above, below = neighbours(first, last, "py")
        return jnp.concatenate([above, below], axis=0)
    lower = lax.axis_index("visit") == 0
    beyond = parts[0][1]
    mine = widened(
        jnp.where(lower, edge[:HALO], edge[HALO:]),
        jnp.where(lower, beyond[:, :HALO], beyond[:, height - HALO :]),
    )
    count = lax.axis_size("py")
    up, down = beside("py")

    def pairs(cross):
        return [(i, j + cross * count) for i, j in down] + [
            (count + i, j + (1 - cross) * count) for i, j in up
        ]

    straight = lax.ppermute(mine, ("visit", "py"), pairs(0))
    crossed = lax.ppermute(mine, ("visit", "py"), pairs(1))
    return jnp.concatenate(
        [jnp.where(lower, crossed, straight), jnp.where(lower, straight, crossed)], axis=0
    )


def stage_kernel(plan, lots, *refs):
    mine_ref, taps_ref, between_ref = refs[:3]
    fields, copies, outs = plan
    visits = fields["visits"]
    at = 3
    chunks = []
    for lot in lots:
        parts = []
        for _ in range(visits):
            parts.append(refs[at : at + 2])
            at += 2
        chunks.append(parts)
    at += fields["aliased"]
    detection_hbm, variance_hbm = refs[at : at + 2]
    field, detection, variance, sems = refs[at + 2 : at + 6]
    sides = refs[at + 6 :]
    spans, tall, _ = field.shape

    which = 0
    held = []
    for parts in chunks:
        group = []
        for cells, beyond in parts:
            side = sides[which]
            which += 1
            height = cells.shape[0]
            side[...] = jnp.concatenate(
                [
                    beyond[HALO:, :],
                    jnp.zeros((SIDE - 2 * HALO, height), jnp.float32),
                    beyond[:HALO, :],
                ],
                axis=0,
            ).T
            group.append((cells, side))
        held.append(group)

    def assemble(order):
        for chunk, visit, first, rows, at_row, begin, end, shift in copies:
            cells, side = held[chunk][order[visit]]
            lot = lots[chunk]

            @pl.loop(begin, end)
            def _(unit):
                start = pl.multiple_of(unit * lot + first, HALO)
                into = pl.ds(at_row, rows)
                field[unit + shift, into, :TX] = cells[pl.ds(start, rows), :].astype(jnp.float32)
                field[unit + shift, into, TX:] = side[pl.ds(start, rows), :]

    if visits == 2:
        for flip in range(2):

            @pl.when(mine_ref[0] == flip)
            def _():
                assemble((0, 1) if flip == 0 else (1, 0))

    else:
        assemble(tuple(range(visits)))
    if fields["between"]:
        above_at, below_at = fields["between"]
        field[0, above_at : above_at + HALO, :] = between_ref[:HALO, :]
        field[spans - 1, below_at : below_at + HALO, :] = between_ref[HALO:, :]

    taps = [taps_ref[tap] for tap in range(7)]

    def down(value, by):
        return value if by == 0 else pltpu.roll(value, by % tall, 0)

    def across(value, by):
        return value if by == 0 else pltpu.roll(value, by % WIDE, 1)

    def three(value, shift, by):
        return value + shift(value, by) + shift(value, -by)

    def stores(unit, source, rows, target):
        return [
            pltpu.make_async_copy(
                scratch.at[unit, pl.ds(source, rows)], hbm.at[pl.ds(target, rows)], sems.at[unit, at]
            )
            for at, (scratch, hbm) in enumerate(
                ((detection, detection_hbm), (variance, variance_hbm))
            )
        ]

    @pl.loop(0, spans)
    def _(unit):
        value = field[unit]
        resid = value - three(three(value, down, 1), across, 1) * (1.0 / 9.0)
        square = resid * resid
        tower = three(three(square, down, 1), down, 3)[HALO : tall - HALO]
        box = three(three(tower, across, 1), across, 3)
        local = box[:, :TX] * (1.0 / 81.0) + 1e-05
        rowwise = sum(taps[tap] * down(value, 3 - tap) for tap in range(7))[HALO : tall - HALO]
        blurred = sum(taps[tap] * across(rowwise, 3 - tap) for tap in range(7))
        variance[unit] = local
        detection[unit] = blurred[:, :TX] * lax.rsqrt(local)
        for begin, end, source, rows, shift in outs:

            @pl.when((unit >= begin) & (unit < end))
            def _():
                target = pl.multiple_of(unit * STEP + shift, HALO)
                for store in stores(unit, source, rows, target):
                    store.start()

    @pl.loop(0, spans)
    def _(unit):
        for begin, end, source, rows, shift in outs:

            @pl.when((unit >= begin) & (unit < end))
            def _():
                for store in stores(unit, source, rows, 0):
                    store.wait()


def stage(plan, mine, taps, between, chunks, lots, held=()):
    fields, _, _ = plan
    spans, tall = fields["spans"], fields["tall"]
    shape = jax.ShapeDtypeStruct((TY, TX), jnp.float32)
    flat = [array for parts in chunks for part in parts for array in part]
    first = 3 + len(flat)
    return pl.pallas_call(
        functools.partial(stage_kernel, plan, lots),
        out_shape=(shape, shape),
        in_specs=[SMEM, SMEM, VMEM] + [VMEM] * len(flat) + [HBM] * len(held),
        out_specs=(HBM, HBM),
        input_output_aliases={first + at: at for at in range(len(held))},
        scratch_shapes=[
            pltpu.VMEM((spans, tall, WIDE), jnp.float32),
            pltpu.VMEM((spans, tall - 2 * HALO, TX), jnp.float32),
            pltpu.VMEM((spans, tall - 2 * HALO, TX), jnp.float32),
            pltpu.SemaphoreType.DMA((spans, 2)),
        ]
        + [pltpu.VMEM((part[0].shape[0], SIDE), jnp.float32) for parts in chunks for part in parts],
        compiler_params=pltpu.CompilerParams(vmem_limit_bytes=56 * MIB),
        cost_estimate=pl.CostEstimate(
            flops=80 * spans * tall * WIDE, bytes_accessed=12 * spans * tall * WIDE, transcendentals=0
        ),
        name="stage",
    )(mine, taps, between, *flat, *held)


def outer_plan(lot):
    fields = dict(visits=2, aliased=0, spans=UNITS + 1, tall=2 * lot, between=(lot - HALO, lot))
    copies = [(0, 1, 0, lot, 0, 0, UNITS, 1), (0, 0, 0, lot, lot, 0, UNITS, 0)]
    rows = lot - HALO
    outs = [
        (0, 1, rows, rows, 0),
        (1, UNITS, 0, 2 * rows, -rows),
        (UNITS, UNITS + 1, 0, rows, -rows),
    ]
    return fields, copies, outs


def inner_plan(lot, inner):
    edge = 2 * HALO
    tall = 2 * inner + 2 * edge
    fields = dict(visits=2, aliased=2, spans=UNITS, tall=tall, between=None)
    copies = [
        (0, 0, lot - edge, edge, 0, 0, UNITS, 0),
        (1, 0, 0, inner, edge, 0, UNITS, 0),
        (1, 1, 0, inner, edge + inner, 0, UNITS, 0),
        (0, 1, 0, edge, edge + 2 * inner, 0, UNITS, 0),
    ]
    return fields, copies, [(0, UNITS, 0, tall - edge, lot - HALO)]


def whole_plan(lot, visits):
    fields = dict(
        visits=visits, aliased=0, spans=UNITS, tall=STEP + 2 * HALO, between=(0, HALO + STEP)
    )
    copies = [(0, visit, 0, lot, HALO + visit * lot, 0, UNITS, 0) for visit in range(visits)]
    copies.append((0, visits - 1, lot - HALO, HALO, 0, 0, UNITS - 1, 1))
    copies.append((0, 0, 0, HALO, HALO + STEP, 1, UNITS, -1))
    return fields, copies, [(0, UNITS, 0, STEP, 0)]


def per_device(
    images, inv_var, good_columns, warp_rows, warp_cols, block_visit, dest_tile, offsets, psf_taps
):
    tiles = lax.axis_size("py") * lax.axis_size("px")
    visits = lax.axis_size("visit")
    plan = shares(visits)
    lots = [rows for rows, _ in plan]
    mine = lax.axis_index("visit").astype(jnp.int32).reshape(1)
    dtype = jnp.bfloat16 if visits == 2 else jnp.float32

    def make(chunk):
        return warp(
            tiles, plan[chunk], chunk == 0, block_visit, dest_tile[:, 0], offsets.reshape(-1),
            good_columns, warp_rows, warp_cols, inv_var, images,
        )

    def send(blocks):
        return lax.all_to_all(blocks, EVERY, split_axis=0, concat_axis=0, tiled=True)

    arrived = send(make(0))
    if len(plan) == 1:
        code = codes(arrived)
        coadd, strip, edge = place(code, arrived, lots[0], dtype)
        parts = spread(coadd, strip)
        if visits > 1:
            edges = lax.all_gather(edge, "visit")
            edge = (edges[visits - 1], edges[0])
        else:
            edge = (edge, edge)
        between = rows_between(edge, parts)
        return stage(whole_plan(lots[0], visits), mine, psf_taps, between, [parts], lots)

    later = make(1)
    arrived, later = lax.optimization_barrier((arrived, later))
    second = send(later)
    code = codes(arrived)
    coadd, strip, edge = place(code, arrived, lots[0], dtype)
    parts = spread(coadd, strip)
    between = rows_between(edge, parts)
    held = stage(outer_plan(lots[0]), mine, psf_taps, between, [parts], lots[:1])
    second, held = lax.optimization_barrier((second, held))
    coadd, strip, _ = place(code, second, lots[1], dtype)
    more = spread(coadd, strip)
    return stage(inner_plan(*lots), mine, psf_taps, between, [parts, more], lots, held)


def codes(arrived):
    note = arrived[:, arrived.shape[1] - NOTE, :: SIDE // CAP]
    return note.astype(jnp.float32).astype(jnp.int32).reshape(-1)


def solution(mesh):
    in_specs = (
        P(EVERY, None, None),
        P(EVERY, None, None),
        P("visit", None),
        P("visit", None, None),
        P("visit", None, None),
        P(EVERY),
        P(EVERY, None),
        P(EVERY, None),
        P(),
    )
    out_specs = (P("py", "px"), P("py", "px"))
    return jax.shard_map(
        per_device, mesh=mesh, in_specs=in_specs, out_specs=out_specs, check_vma=False
    )
```

```python
import functools

import jax
import jax.numpy as jnp
from jax import lax
from jax.experimental import pallas as pl
from jax.experimental.pallas import tpu as pltpu
from jax.sharding import PartitionSpec as P

TY = 1024
TX = 1024
STEP = 128
CAP = 2
UNITS = TY // STEP
HALO = 8
EDGE = 16
SIDE = 128
WIDE = TX + SIDE
GROUP = 4
NOTE = 16
MIB = 1 << 20
EVERY = ("visit", "py", "px")
HBM = pl.BlockSpec(memory_space=pltpu.HBM)
SMEM = pl.BlockSpec(memory_space=pltpu.SMEM)
VMEM = pl.BlockSpec(memory_space=pltpu.VMEM)


def shares(visits):
    if visits == 2:
        edge, inner = 48, 16
        return [(edge, (0, STEP - edge)), (inner, (edge, edge + inner))]
    rows = STEP // visits
    return [(rows, tuple(visit * rows for visit in range(visits)))]


def warp_kernel(
    tiles, share, noted, visit_ref, tile_ref, offset_ref, good_ref, rows_hbm, cols_hbm, var_hbm,
    image_hbm, out_hbm, rows, cols, var, image, done, note, count, table_sems, sems, out_sems,
):
    blocks, side, _ = var.shape
    some, firsts = share
    groups = blocks // GROUP
    slot_rows = done.shape[2]
    tables = [
        pltpu.make_async_copy(rows_hbm, rows, table_sems.at[0]),
        pltpu.make_async_copy(cols_hbm, cols, table_sems.at[1]),
    ]

    def loads(group):
        span = pl.ds(group * GROUP, GROUP)
        return (
            pltpu.make_async_copy(var_hbm.at[span], var.at[span], sems.at[group, 0]),
            pltpu.make_async_copy(image_hbm.at[span], image.at[span], sems.at[group, 1]),
        )

    for load in tables:
        load.start()
    for group in range(groups):
        for load in loads(group):
            load.start()

    @pl.loop(0, tiles)
    def _(tile):
        count[tile] = 0

    if noted:
        note[...] = jnp.full(note.shape, -1, jnp.bfloat16)
        slot_of_lane = lax.broadcasted_iota(jnp.int32, (NOTE, SIDE), 1) // (SIDE // CAP)

    for load in tables:
        load.wait()

    strips = [first + strip * STEP for first in firsts for strip in range(side // STEP)]
    tall = some * len(strips)
    part = tall // len(firsts)

    @pl.loop(0, groups)
    def _(group):
        for load in loads(group):
            load.wait()
        visits = [visit_ref[group * GROUP + ahead] for ahead in range(GROUP)]
        planes, turned, warped = [], [], []
        for ahead in range(GROUP):
            block = group * GROUP + ahead
            good = good_ref[pl.ds(visits[ahead], 1), :].astype(jnp.float32)
            weight = var[block].astype(jnp.float32) * good
            data = weight * image[block].astype(jnp.float32)
            planes.append(
                jnp.concatenate([data.astype(jnp.bfloat16), weight.astype(jnp.bfloat16)], axis=1)
            )
        for ahead in range(GROUP):
            matrix = jnp.concatenate(
                [rows[visits[ahead], first : first + some, :] for first in strips], axis=0
            )
            turned.append(
                jnp.dot(matrix, planes[ahead], preferred_element_type=jnp.float32).astype(jnp.bfloat16)
            )
        for ahead in range(GROUP):
            both = jnp.concatenate([turned[ahead][:, :side], turned[ahead][:, side:]], axis=0)
            warped.append(
                lax.dot_general(
                    both,
                    cols[visits[ahead]],
                    (((1,), (1,)), ((), ())),
                    preferred_element_type=jnp.float32,
                ).astype(jnp.bfloat16)
            )
        for ahead in range(GROUP):
            block = group * GROUP + ahead
            for visit in range(len(firsts)):
                for half in range(side // SIDE):
                    for plane in range(2):
                        start = plane * tall + visit * part
                        into = (2 * half + plane) * part
                        done[block, visit, into : into + part, :] = warped[ahead][
                            start : start + part, half * SIDE : (half + 1) * SIDE
                        ]
        for ahead in range(GROUP):
            block = group * GROUP + ahead
            tile = tile_ref[block]
            rank = count[tile]
            count[tile] = rank + 1
            for visit in range(len(firsts)):
                target = visit * tiles + tile
                pltpu.make_async_copy(
                    done.at[block, visit],
                    out_hbm.at[target, pl.ds(pl.multiple_of(rank * slot_rows, NOTE), slot_rows)],
                    out_sems.at[block, visit],
                ).start()
                if noted:
                    code = offset_ref[0, block] * 8 + offset_ref[1, block]
                    note[target] = jnp.where(
                        slot_of_lane == rank, code.astype(jnp.float32), note[target].astype(jnp.float32)
                    ).astype(jnp.bfloat16)

    if noted:
        notes = pltpu.make_async_copy(
            note, out_hbm.at[:, pl.ds(CAP * slot_rows, NOTE)], table_sems.at[0]
        )
        notes.start()

    @pl.loop(0, blocks)
    def _(block):
        for visit in range(len(firsts)):
            pltpu.make_async_copy(
                done.at[block, visit], out_hbm.at[0, pl.ds(0, slot_rows)], out_sems.at[block, visit]
            ).wait()

    if noted:
        notes.wait()


def warp(tiles, share, noted, visit, tile, offset, good, rows, cols, var, image):
    blocks, side, _ = var.shape
    some, firsts = share
    slot_rows = 2 * (side // STEP) * some * (side // SIDE)
    visits = len(firsts)
    return pl.pallas_call(
        functools.partial(warp_kernel, tiles, share, noted),
        out_shape=jax.ShapeDtypeStruct(
            (visits * tiles, CAP * slot_rows + noted * NOTE, SIDE), jnp.bfloat16
        ),
        in_specs=[SMEM, SMEM, SMEM, VMEM, HBM, HBM, HBM, HBM],
        out_specs=HBM,
        scratch_shapes=[
            pltpu.VMEM(rows.shape, jnp.bfloat16),
            pltpu.VMEM(cols.shape, jnp.bfloat16),
            pltpu.VMEM(var.shape, jnp.bfloat16),
            pltpu.VMEM(var.shape, jnp.bfloat16),
            pltpu.VMEM((blocks, visits, slot_rows, SIDE), jnp.bfloat16),
            pltpu.VMEM((visits * tiles, NOTE, SIDE), jnp.bfloat16),
            pltpu.SMEM((tiles,), jnp.int32),
            pltpu.SemaphoreType.DMA((2,)),
            pltpu.SemaphoreType.DMA((blocks // GROUP, 2)),
            pltpu.SemaphoreType.DMA((blocks, visits)),
        ],
        compiler_params=pltpu.CompilerParams(vmem_limit_bytes=60 * MIB),
        cost_estimate=pl.CostEstimate(
            flops=8 * blocks * side**3, bytes_accessed=8 * blocks * side**2, transcendentals=0
        ),
        name="warp",
    )(visit, tile, offset, good, rows, cols, var, image)


def place_kernel(part, code_ref, blocks_ref, coadd_ref, strip_ref, edge_ref, data, weight):
    step = pl.program_id(0)
    some = blocks_ref.shape[0]
    height = data.shape[0]
    lot = height // UNITS

    @pl.when(step == 0)
    def _():
        data[...] = jnp.zeros_like(data)
        weight[...] = jnp.zeros_like(weight)

    for block in range(some):
        for slot in range(CAP):
            code = code_ref[(step * some + block) * CAP + slot]

            @pl.when(code >= 0)
            def _():
                row = pl.multiple_of((code // 8) * lot, lot)
                for half in range(2):
                    col = pl.multiple_of((code % 8 + half) * STEP, STEP)
                    cells = (pl.ds(row, part), pl.ds(col, STEP))
                    first = (slot * 2 + half) * 2 * part
                    data[cells] += blocks_ref[block, first : first + part].astype(jnp.float32)
                    weight[cells] += blocks_ref[block, first + part : first + 2 * part].astype(
                        jnp.float32
                    )

    @pl.when(step == pl.num_programs(0) - 1)
    def _():
        coadd = data[...] / jnp.maximum(weight[...], 1.0)
        coadd_ref[...] = coadd.astype(coadd_ref.dtype)
        strip_ref[:HALO] = coadd[:, :SIDE].T[:HALO]
        strip_ref[HALO:] = coadd[:, TX - SIDE :].T[SIDE - HALO :]
        edge_ref[:HALO] = coadd[:HALO]
        edge_ref[HALO:] = coadd[height - HALO :]


def place(code, blocks, lot):
    count, tall, side = blocks.shape
    some = 4
    height = lot * UNITS
    shapes = [((height, TX), jnp.bfloat16), ((2 * HALO, height), jnp.float32), ((2 * HALO, TX), jnp.float32)]
    return pl.pallas_call(
        functools.partial(place_kernel, 2 * lot),
        grid_spec=pltpu.PrefetchScalarGridSpec(
            num_scalar_prefetch=1,
            grid=(count // some,),
            in_specs=[pl.BlockSpec((some, tall, side), lambda step, code: (step, 0, 0))],
            out_specs=[pl.BlockSpec(shape, lambda step, code: (0, 0)) for shape, _ in shapes],
            scratch_shapes=[pltpu.VMEM((height, TX), jnp.float32)] * 2,
        ),
        out_shape=[jax.ShapeDtypeStruct(*shape) for shape in shapes],
        compiler_params=pltpu.CompilerParams(vmem_limit_bytes=32 * MIB),
        cost_estimate=pl.CostEstimate(
            flops=count * tall * side, bytes_accessed=count * tall * side * 2, transcendentals=0
        ),
        name="place",
    )(code, blocks)


def beside(axis):
    count = lax.axis_size(axis)
    up = [(i, i + 1) for i in range(count - 1)]
    return up, [(j, i) for i, j in up]


def neighbours(first, last, axis):
    up, down = beside(axis)
    return lax.ppermute(last, axis, up), lax.ppermute(first, axis, down)


def spread(coadd, strip):
    visits = lax.axis_size("visit")
    first, last = strip[:HALO], strip[HALO:]
    if visits == 2:
        other = lax.ppermute(coadd, "visit", [(0, 1), (1, 0)])
        count = lax.axis_size("px")
        up, down = beside("px")

        def crossed(pairs):
            return [(v * count + i, (1 - v) * count + j) for v in range(2) for i, j in pairs]

        left, right = neighbours(first, last, "px")
        other_left = lax.ppermute(last, ("visit", "px"), crossed(up))
        other_right = lax.ppermute(first, ("visit", "px"), crossed(down))
        return [(coadd, left, right), (other, other_left, other_right)]
    one = (coadd, *neighbours(first, last, "px"))
    if visits == 1:
        return [one]
    every = [lax.all_gather(part, "visit") for part in one]
    return [tuple(part[visit] for part in every) for visit in range(visits)]


def widened(rows, left, right):
    gap = jnp.zeros((HALO, SIDE - 2 * HALO), jnp.float32)
    return jnp.concatenate([rows, right.T, gap, left.T], axis=1)


def rows_between(edge, parts):
    visits = len(parts)
    height = parts[0][1].shape[1]
    none = jnp.zeros((EDGE - HALO, WIDE), jnp.float32)
    if visits != 2:
        last = widened(edge[0][HALO:], *[side[:, height - HALO :] for side in parts[-1][1:]])
        first = widened(edge[1][:HALO], *[side[:, :HALO] for side in parts[0][1:]])
        above, below = neighbours(first, last, "py")
        return jnp.concatenate([none, above, below, none], axis=0).astype(jnp.bfloat16)
    lower = lax.axis_index("visit") == 0
    mine = widened(
        jnp.where(lower, edge[:HALO], edge[HALO:]),
        *[jnp.where(lower, side[:, :HALO], side[:, height - HALO :]) for side in parts[0][1:]],
    )
    count = lax.axis_size("py")
    up, down = beside("py")

    def pairs(cross):
        return [(i, j + cross * count) for i, j in down] + [
            (count + i, j + (1 - cross) * count) for i, j in up
        ]

    straight = lax.ppermute(mine, ("visit", "py"), pairs(0))
    crossed = lax.ppermute(mine, ("visit", "py"), pairs(1))
    above, below = jnp.where(lower, crossed, straight), jnp.where(lower, straight, crossed)
    return jnp.concatenate([none, above, below, none], axis=0).astype(jnp.bfloat16)


def bands(plan, taps):
    fields = plan[0]
    tall, margin = fields["tall"], fields["margin"]
    row = jnp.arange(tall, dtype=jnp.int32)
    out = jnp.arange(tall - 2 * margin, dtype=jnp.int32) + margin
    three = (jnp.abs(row[:, None] - row[None, :]) <= 1).astype(jnp.bfloat16)
    nine = (jnp.abs(out[:, None] - row[None, :]) <= 4).astype(jnp.bfloat16)
    count = taps.shape[0]
    ahead = row[None, :] - out[:, None] + count // 2
    blur = sum(jnp.where(ahead == tap, taps[tap], 0.0) for tap in range(count))
    coarse = blur.astype(jnp.bfloat16)
    fine = (blur - coarse.astype(jnp.float32)).astype(jnp.bfloat16)
    return jnp.concatenate([three, coarse, fine], axis=0), nine


def stage_kernel(plan, lots, *refs):
    mine_ref, taps_ref, between_ref, sums_ref, nine_ref = refs[:5]
    fields, copies, outs = plan
    visits, margin = fields["visits"], fields["margin"]
    at = 5
    chunks = []
    for lot in lots:
        parts = []
        for _ in range(visits):
            parts.append(refs[at : at + 3])
            at += 3
        chunks.append(parts)
    at += fields["aliased"]
    detection_hbm, variance_hbm = refs[at : at + 2]
    field, detection, variance, sems = refs[at + 2 : at + 6]
    sides = refs[at + 6 :]
    spans, tall, _ = field.shape
    short = tall - 2 * margin

    which = 0
    held = []
    for parts in chunks:
        group = []
        for cells, left, right in parts:
            side = sides[which]
            which += 1
            height = cells.shape[0]
            side[...] = jnp.concatenate(
                [right[...], jnp.zeros((SIDE - 2 * HALO, height), jnp.float32), left[...]], axis=0
            ).T.astype(jnp.bfloat16)
            group.append((cells, side))
        held.append(group)

    for span, first, rows in fields["blank"]:
        field[span, first : first + rows, :] = jnp.zeros((rows, WIDE), jnp.bfloat16)

    def assemble(order):
        for chunk, visit, first, rows, at_row, begin, end, shift in copies:
            cells, side = held[chunk][order[visit]]
            lot = lots[chunk]

            @pl.loop(begin, end)
            def _(unit):
                start = pl.multiple_of(unit * lot + first, EDGE)
                into = pl.ds(at_row, rows)
                field[unit + shift, into, :TX] = cells[pl.ds(start, rows), :]
                field[unit + shift, into, TX:] = side[pl.ds(start, rows), :]

    if visits == 2:
        for flip in range(2):

            @pl.when(mine_ref[0] == flip)
            def _():
                assemble((0, 1) if flip == 0 else (1, 0))

    else:
        assemble(tuple(range(visits)))
    if fields["between"]:
        above_at, below_at = fields["between"]
        field[0, above_at : above_at + EDGE, :] = between_ref[:EDGE, :]
        field[spans - 1, below_at : below_at + EDGE, :] = between_ref[EDGE:, :]

    taps = [taps_ref[tap] for tap in range(7)]

    def across(value, by):
        return value if by == 0 else pltpu.roll(value, by % WIDE, 1)

    def three(value, by):
        return value + across(value, by) + across(value, -by)

    def stores(unit, source, rows, target):
        return [
            pltpu.make_async_copy(
                scratch.at[unit, pl.ds(source, rows)], hbm.at[pl.ds(target, rows)], sems.at[unit, at]
            )
            for at, (scratch, hbm) in enumerate(
                ((detection, detection_hbm), (variance, variance_hbm))
            )
        ]

    @pl.loop(0, spans)
    def _(unit):
        value = field[unit]
        sums = jnp.dot(sums_ref[...], value, preferred_element_type=jnp.float32)
        resid = value.astype(jnp.float32) - three(sums[:tall], 1) * (1.0 / 9.0)
        square = resid * resid
        coarse = square.astype(jnp.bfloat16)
        fine = (square - coarse.astype(jnp.float32)).astype(jnp.bfloat16)
        tower = jnp.dot(nine_ref[...], coarse, preferred_element_type=jnp.float32) + jnp.dot(
            nine_ref[...], fine, preferred_element_type=jnp.float32
        )
        local = three(three(tower, 1), 3)[:, :TX] * (1.0 / 81.0) + 1e-05
        rowwise = sums[tall : tall + short] + sums[tall + short :]
        blurred = sum(taps[tap] * across(rowwise, 3 - tap) for tap in range(7))
        variance[unit] = local
        detection[unit] = blurred[:, :TX] * lax.rsqrt(local)
        for begin, end, source, rows, shift in outs:

            @pl.when((unit >= begin) & (unit < end))
            def _():
                target = pl.multiple_of(unit * STEP + shift, HALO)
                for store in stores(unit, source, rows, target):
                    store.start()

    @pl.loop(0, spans)
    def _(unit):
        for begin, end, source, rows, shift in outs:

            @pl.when((unit >= begin) & (unit < end))
            def _():
                for store in stores(unit, source, rows, 0):
                    store.wait()


def stage(plan, mine, taps, between, tables, chunks, lots, held=()):
    fields, _, _ = plan
    spans, tall = fields["spans"], fields["tall"]
    shape = jax.ShapeDtypeStruct((TY, TX), jnp.float32)
    flat = [array for parts in chunks for part in parts for array in part]
    first = 5 + len(flat)
    out = pltpu.VMEM((spans, tall - 2 * fields["margin"], TX), jnp.float32)
    return pl.pallas_call(
        functools.partial(stage_kernel, plan, lots),
        out_shape=(shape, shape),
        in_specs=[SMEM, SMEM, VMEM, VMEM, VMEM] + [VMEM] * len(flat) + [HBM] * len(held),
        out_specs=(HBM, HBM),
        input_output_aliases={first + at: at for at in range(len(held))},
        scratch_shapes=[
            pltpu.VMEM((spans, tall, WIDE), jnp.bfloat16),
            out,
            out,
            pltpu.SemaphoreType.DMA((spans, 2)),
        ]
        + [pltpu.VMEM((part[0].shape[0], SIDE), jnp.bfloat16) for parts in chunks for part in parts],
        compiler_params=pltpu.CompilerParams(vmem_limit_bytes=56 * MIB),
        cost_estimate=pl.CostEstimate(
            flops=80 * spans * tall * WIDE, bytes_accessed=12 * spans * tall * WIDE, transcendentals=0
        ),
        name="stage",
    )(mine, taps, between, *tables, *flat, *held)


def outer_plan(lot):
    fields = dict(
        visits=2, aliased=0, spans=UNITS + 1, tall=2 * lot, margin=HALO, between=(lot - EDGE, lot),
        blank=[(0, 0, lot - EDGE), (UNITS, lot + EDGE, lot - EDGE)],
    )
    copies = [(0, 1, 0, lot, 0, 0, UNITS, 1), (0, 0, 0, lot, lot, 0, UNITS, 0)]
    rows = lot - HALO
    outs = [
        (0, 1, rows, rows, 0),
        (1, UNITS, 0, 2 * rows, -rows),
        (UNITS, UNITS + 1, 0, rows, -rows),
    ]
    return fields, copies, outs


def inner_plan(lot, inner):
    tall = 2 * inner + 2 * EDGE
    fields = dict(
        visits=2, aliased=2, spans=UNITS, tall=tall, margin=HALO, between=None, blank=[]
    )
    copies = [
        (0, 0, lot - EDGE, EDGE, 0, 0, UNITS, 0),
        (1, 0, 0, inner, EDGE, 0, UNITS, 0),
        (1, 1, 0, inner, EDGE + inner, 0, UNITS, 0),
        (0, 1, 0, EDGE, EDGE + 2 * inner, 0, UNITS, 0),
    ]
    return fields, copies, [(0, UNITS, 0, tall - 2 * HALO, lot - HALO)]


def whole_plan(lot, visits):
    fields = dict(
        visits=visits, aliased=0, spans=UNITS, tall=STEP + 2 * EDGE, margin=EDGE,
        between=(0, EDGE + STEP), blank=[],
    )
    copies = [(0, visit, 0, lot, EDGE + visit * lot, 0, UNITS, 0) for visit in range(visits)]
    copies.append((0, visits - 1, lot - EDGE, EDGE, 0, 0, UNITS - 1, 1))
    copies.append((0, 0, 0, EDGE, EDGE + STEP, 1, UNITS, -1))
    return fields, copies, [(0, UNITS, 0, STEP, 0)]


def per_device(
    images, inv_var, good_columns, warp_rows, warp_cols, block_visit, dest_tile, offsets, psf_taps
):
    tiles = lax.axis_size("py") * lax.axis_size("px")
    visits = lax.axis_size("visit")
    plan = shares(visits)
    lots = [rows for rows, _ in plan]
    mine = lax.axis_index("visit").astype(jnp.int32).reshape(1)

    def make(chunk, var):
        return warp(
            tiles, plan[chunk], chunk == 0, block_visit, dest_tile[:, 0], offsets.T,
            good_columns, warp_rows, warp_cols, var, images,
        )

    def send(blocks):
        return lax.all_to_all(blocks, EVERY, split_axis=0, concat_axis=0, tiled=True)

    made, psf_taps = lax.optimization_barrier((make(0, inv_var), psf_taps))
    arrived = send(made)
    if len(plan) == 1:
        code = codes(arrived)
        coadd, strip, edge = place(code, arrived, lots[0])
        parts = spread(coadd, strip)
        if visits > 1:
            edges = lax.all_gather(edge, "visit")
            edge = (edges[visits - 1], edges[0])
        else:
            edge = (edge, edge)
        between = rows_between(edge, parts)
        every = whole_plan(lots[0], visits)
        return stage(every, mine, psf_taps, between, bands(every, psf_taps), [parts], lots)

    outer, inner = outer_plan(lots[0]), inner_plan(*lots)
    tables, inv_var = lax.optimization_barrier(
        ([bands(part, psf_taps) for part in (outer, inner)], inv_var)
    )
    arrived, later = lax.optimization_barrier((arrived, make(1, inv_var)))
    second = send(later)
    code = codes(arrived)
    coadd, strip, edge = place(code, arrived, lots[0])
    parts = spread(coadd, strip)
    between = rows_between(edge, parts)
    coadd, strip, _ = place(code, second, lots[1])
    more = spread(coadd, strip)
    (parts, between), _ = lax.optimization_barrier(((parts, between), coadd))
    held = stage(outer, mine, psf_taps, between, tables[0], [parts], lots[:1])
    return stage(inner, mine, psf_taps, between, tables[1], [parts, more], lots, held)


def codes(arrived):
    note = arrived[:, arrived.shape[1] - NOTE, :: SIDE // CAP]
    return note.astype(jnp.float32).astype(jnp.int32).reshape(-1)


def solution(mesh):
    in_specs = (
        P(EVERY, None, None),
        P(EVERY, None, None),
        P("visit", None),
        P("visit", None, None),
        P("visit", None, None),
        P(EVERY),
        P(EVERY, None),
        P(EVERY, None),
        P(),
    )
    out_specs = (P("py", "px"), P("py", "px"))
    return jax.shard_map(
        per_device, mesh=mesh, in_specs=in_specs, out_specs=out_specs, check_vma=False
    )
```

```python
import functools

import jax
import jax.numpy as jnp
from jax import lax
from jax.experimental import pallas as pl
from jax.experimental.pallas import tpu as pltpu
from jax.sharding import PartitionSpec as P

TY = 1024
TX = 1024
STEP = 128
CAP = 2
UNITS = TY // STEP
HALO = 8
EDGE = 16
SIDE = 128
WIDE = TX + SIDE
GROUP = 4
NOTE = 16
MIB = 1 << 20
EVERY = ("visit", "py", "px")
HBM = pl.BlockSpec(memory_space=pltpu.HBM)
SMEM = pl.BlockSpec(memory_space=pltpu.SMEM)
VMEM = pl.BlockSpec(memory_space=pltpu.VMEM)


def shares(visits):
    if visits == 2:
        edge, inner = 32, 32
        return [(edge, (0, STEP - edge)), (inner, (edge, edge + inner))]
    rows = STEP // visits
    return [(rows, tuple(visit * rows for visit in range(visits)))]


def warp_kernel(
    tiles, share, noted, visit_ref, tile_ref, offset_ref, good_ref, rows_hbm, cols_hbm, var_hbm,
    image_hbm, out_hbm, rows, cols, var, image, done, note, count, table_sems, sems, out_sems,
):
    blocks, side, _ = var.shape
    some, firsts = share
    groups = blocks // GROUP
    slot_rows = done.shape[2]
    tables = [
        pltpu.make_async_copy(rows_hbm, rows, table_sems.at[0]),
        pltpu.make_async_copy(cols_hbm, cols, table_sems.at[1]),
    ]

    def loads(group):
        span = pl.ds(group * GROUP, GROUP)
        return (
            pltpu.make_async_copy(var_hbm.at[span], var.at[span], sems.at[group, 0]),
            pltpu.make_async_copy(image_hbm.at[span], image.at[span], sems.at[group, 1]),
        )

    for load in tables:
        load.start()
    for group in range(groups):
        for load in loads(group):
            load.start()

    @pl.loop(0, tiles)
    def _(tile):
        count[tile] = 0

    if noted:
        note[...] = jnp.full(note.shape, -1, jnp.bfloat16)
        slot_of_lane = lax.broadcasted_iota(jnp.int32, (NOTE, SIDE), 1) // (SIDE // CAP)

    for load in tables:
        load.wait()

    strips = [first + strip * STEP for first in firsts for strip in range(side // STEP)]
    tall = some * len(strips)
    part = tall // len(firsts)

    @pl.loop(0, groups)
    def _(group):
        for load in loads(group):
            load.wait()
        visits = [visit_ref[group * GROUP + ahead] for ahead in range(GROUP)]
        planes, turned, warped = [], [], []
        for ahead in range(GROUP):
            block = group * GROUP + ahead
            good = good_ref[pl.ds(visits[ahead], 1), :].astype(jnp.float32)
            weight = var[block].astype(jnp.float32) * good
            data = weight * image[block].astype(jnp.float32)
            planes.append(
                jnp.concatenate([data.astype(jnp.bfloat16), weight.astype(jnp.bfloat16)], axis=1)
            )
        for ahead in range(GROUP):
            matrix = jnp.concatenate(
                [rows[visits[ahead], first : first + some, :] for first in strips], axis=0
            )
            turned.append(
                jnp.dot(matrix, planes[ahead], preferred_element_type=jnp.float32).astype(jnp.bfloat16)
            )
        for ahead in range(GROUP):
            both = jnp.concatenate([turned[ahead][:, :side], turned[ahead][:, side:]], axis=0)
            warped.append(
                lax.dot_general(
                    both,
                    cols[visits[ahead]],
                    (((1,), (1,)), ((), ())),
                    preferred_element_type=jnp.float32,
                ).astype(jnp.bfloat16)
            )
        for ahead in range(GROUP):
            block = group * GROUP + ahead
            for visit in range(len(firsts)):
                for half in range(side // SIDE):
                    for plane in range(2):
                        start = plane * tall + visit * part
                        into = (2 * half + plane) * part
                        done[block, visit, into : into + part, :] = warped[ahead][
                            start : start + part, half * SIDE : (half + 1) * SIDE
                        ]
        for ahead in range(GROUP):
            block = group * GROUP + ahead
            tile = tile_ref[block]
            rank = count[tile]
            count[tile] = rank + 1
            for visit in range(len(firsts)):
                target = visit * tiles + tile
                pltpu.make_async_copy(
                    done.at[block, visit],
                    out_hbm.at[target, pl.ds(pl.multiple_of(rank * slot_rows, NOTE), slot_rows)],
                    out_sems.at[block, visit],
                ).start()
                if noted:
                    code = offset_ref[0, block] * 8 + offset_ref[1, block]
                    note[target] = jnp.where(
                        slot_of_lane == rank, code.astype(jnp.float32), note[target].astype(jnp.float32)
                    ).astype(jnp.bfloat16)

    if noted:
        notes = pltpu.make_async_copy(
            note, out_hbm.at[:, pl.ds(CAP * slot_rows, NOTE)], table_sems.at[0]
        )
        notes.start()

    @pl.loop(0, blocks)
    def _(block):
        for visit in range(len(firsts)):
            pltpu.make_async_copy(
                done.at[block, visit], out_hbm.at[0, pl.ds(0, slot_rows)], out_sems.at[block, visit]
            ).wait()

    if noted:
        notes.wait()


def warp(tiles, share, noted, visit, tile, offset, good, rows, cols, var, image):
    blocks, side, _ = var.shape
    some, firsts = share
    slot_rows = 2 * (side // STEP) * some * (side // SIDE)
    visits = len(firsts)
    return pl.pallas_call(
        functools.partial(warp_kernel, tiles, share, noted),
        out_shape=jax.ShapeDtypeStruct(
            (visits * tiles, CAP * slot_rows + noted * NOTE, SIDE), jnp.bfloat16
        ),
        in_specs=[SMEM, SMEM, SMEM, VMEM, HBM, HBM, HBM, HBM],
        out_specs=HBM,
        scratch_shapes=[
            pltpu.VMEM(rows.shape, jnp.bfloat16),
            pltpu.VMEM(cols.shape, jnp.bfloat16),
            pltpu.VMEM(var.shape, jnp.bfloat16),
            pltpu.VMEM(var.shape, jnp.bfloat16),
            pltpu.VMEM((blocks, visits, slot_rows, SIDE), jnp.bfloat16),
            pltpu.VMEM((visits * tiles, NOTE, SIDE), jnp.bfloat16),
            pltpu.SMEM((tiles,), jnp.int32),
            pltpu.SemaphoreType.DMA((2,)),
            pltpu.SemaphoreType.DMA((blocks // GROUP, 2)),
            pltpu.SemaphoreType.DMA((blocks, visits)),
        ],
        compiler_params=pltpu.CompilerParams(vmem_limit_bytes=60 * MIB),
        cost_estimate=pl.CostEstimate(
            flops=8 * blocks * side**3, bytes_accessed=8 * blocks * side**2, transcendentals=0
        ),
        name="warp",
    )(visit, tile, offset, good, rows, cols, var, image)


def place_kernel(part, code_ref, blocks_ref, coadd_ref, strip_ref, edge_ref, data, weight):
    step = pl.program_id(0)
    some = blocks_ref.shape[0]
    height = data.shape[0]
    lot = height // UNITS

    @pl.when(step == 0)
    def _():
        data[...] = jnp.zeros_like(data)
        weight[...] = jnp.zeros_like(weight)

    for block in range(some):
        for slot in range(CAP):
            code = code_ref[(step * some + block) * CAP + slot]

            @pl.when(code >= 0)
            def _():
                row = pl.multiple_of((code // 8) * lot, lot)
                for half in range(2):
                    col = pl.multiple_of((code % 8 + half) * STEP, STEP)
                    cells = (pl.ds(row, part), pl.ds(col, STEP))
                    first = (slot * 2 + half) * 2 * part
                    data[cells] += blocks_ref[block, first : first + part].astype(jnp.float32)
                    weight[cells] += blocks_ref[block, first + part : first + 2 * part].astype(
                        jnp.float32
                    )

    @pl.when(step == pl.num_programs(0) - 1)
    def _():
        coadd = data[...] / jnp.maximum(weight[...], 1.0)
        coadd_ref[...] = coadd.astype(coadd_ref.dtype)
        strip_ref[:HALO] = coadd[:, :SIDE].T[:HALO]
        strip_ref[HALO:] = coadd[:, TX - SIDE :].T[SIDE - HALO :]
        edge_ref[:HALO] = coadd[:HALO]
        edge_ref[HALO:] = coadd[height - HALO :]


def place(code, blocks, lot):
    count, tall, side = blocks.shape
    some = 4
    height = lot * UNITS
    shapes = [((height, TX), jnp.bfloat16), ((2 * HALO, height), jnp.float32), ((2 * HALO, TX), jnp.float32)]
    return pl.pallas_call(
        functools.partial(place_kernel, 2 * lot),
        grid_spec=pltpu.PrefetchScalarGridSpec(
            num_scalar_prefetch=1,
            grid=(count // some,),
            in_specs=[pl.BlockSpec((some, tall, side), lambda step, code: (step, 0, 0))],
            out_specs=[pl.BlockSpec(shape, lambda step, code: (0, 0)) for shape, _ in shapes],
            scratch_shapes=[pltpu.VMEM((height, TX), jnp.float32)] * 2,
        ),
        out_shape=[jax.ShapeDtypeStruct(*shape) for shape in shapes],
        compiler_params=pltpu.CompilerParams(vmem_limit_bytes=32 * MIB),
        cost_estimate=pl.CostEstimate(
            flops=count * tall * side, bytes_accessed=count * tall * side * 2, transcendentals=0
        ),
        name="place",
    )(code, blocks)


def beside(axis):
    count = lax.axis_size(axis)
    up = [(i, i + 1) for i in range(count - 1)]
    return up, [(j, i) for i, j in up]


def neighbours(first, last, axis):
    up, down = beside(axis)
    return lax.ppermute(last, axis, up), lax.ppermute(first, axis, down)


def spread(coadd, strip):
    visits = lax.axis_size("visit")
    first, last = strip[:HALO], strip[HALO:]
    if visits == 2:
        swap = [(0, 1), (1, 0)]
        other = lax.ppermute(coadd, "visit", swap)
        left, right = neighbours(first, last, "px")
        far = lax.ppermute(jnp.concatenate([left, right], axis=0), "visit", swap)
        return [(coadd, left, right), (other, far[:HALO], far[HALO:])]
    one = (coadd, *neighbours(first, last, "px"))
    if visits == 1:
        return [one]
    every = [lax.all_gather(part, "visit") for part in one]
    return [tuple(part[visit] for part in every) for visit in range(visits)]


def widened(rows, left, right):
    gap = jnp.zeros((HALO, SIDE - 2 * HALO), jnp.float32)
    return jnp.concatenate([rows, right.T, gap, left.T], axis=1)


def rows_between(edge, parts):
    visits = len(parts)
    height = parts[0][1].shape[1]
    none = jnp.zeros((EDGE - HALO, WIDE), jnp.float32)
    if visits != 2:
        last = widened(edge[0][HALO:], *[side[:, height - HALO :] for side in parts[-1][1:]])
        first = widened(edge[1][:HALO], *[side[:, :HALO] for side in parts[0][1:]])
        above, below = neighbours(first, last, "py")
        return jnp.concatenate([none, above, below, none], axis=0).astype(jnp.bfloat16)
    lower = lax.axis_index("visit") == 0
    mine = widened(
        jnp.where(lower, edge[:HALO], edge[HALO:]),
        *[jnp.where(lower, side[:, :HALO], side[:, height - HALO :]) for side in parts[0][1:]],
    )
    count = lax.axis_size("py")
    up, down = beside("py")

    def pairs(cross):
        return [(i, j + cross * count) for i, j in down] + [
            (count + i, j + (1 - cross) * count) for i, j in up
        ]

    straight = lax.ppermute(mine, ("visit", "py"), pairs(0))
    crossed = lax.ppermute(mine, ("visit", "py"), pairs(1))
    above, below = jnp.where(lower, crossed, straight), jnp.where(lower, straight, crossed)
    return jnp.concatenate([none, above, below, none], axis=0).astype(jnp.bfloat16)


def bands(plan, taps):
    fields = plan[0]
    tall, margin = fields["tall"], fields["margin"]
    row = jnp.arange(tall, dtype=jnp.int32)
    out = jnp.arange(tall - 2 * margin, dtype=jnp.int32) + margin
    three = (jnp.abs(row[:, None] - row[None, :]) <= 1).astype(jnp.bfloat16)
    nine = (jnp.abs(out[:, None] - row[None, :]) <= 4).astype(jnp.bfloat16)
    count = taps.shape[0]
    ahead = row[None, :] - out[:, None] + count // 2
    blur = sum(jnp.where(ahead == tap, taps[tap], 0.0) for tap in range(count))
    coarse = blur.astype(jnp.bfloat16)
    fine = (blur - coarse.astype(jnp.float32)).astype(jnp.bfloat16)
    return jnp.concatenate([three, coarse, fine], axis=0), nine


def stage_kernel(plan, lots, *refs):
    mine_ref, taps_ref, between_ref, sums_ref, nine_ref = refs[:5]
    fields, copies, outs = plan
    visits, margin = fields["visits"], fields["margin"]
    at = 5
    chunks = []
    for lot in lots:
        parts = []
        for _ in range(visits):
            parts.append(refs[at : at + 3])
            at += 3
        chunks.append(parts)
    at += fields["aliased"]
    detection_hbm, variance_hbm = refs[at : at + 2]
    field, detection, variance, sems = refs[at + 2 : at + 6]
    sides = refs[at + 6 :]
    spans, tall, _ = field.shape
    short = tall - 2 * margin

    which = 0
    held = []
    for parts in chunks:
        group = []
        for cells, left, right in parts:
            side = sides[which]
            which += 1
            height = cells.shape[0]
            side[...] = jnp.concatenate(
                [right[...], jnp.zeros((SIDE - 2 * HALO, height), jnp.float32), left[...]], axis=0
            ).T.astype(jnp.bfloat16)
            group.append((cells, side))
        held.append(group)

    for span, first, rows in fields["blank"]:
        field[span, first : first + rows, :] = jnp.zeros((rows, WIDE), jnp.bfloat16)

    def assemble(order):
        for chunk, visit, first, rows, at_row, begin, end, shift in copies:
            cells, side = held[chunk][order[visit]]
            lot = lots[chunk]

            @pl.loop(begin, end)
            def _(unit):
                start = pl.multiple_of(unit * lot + first, EDGE)
                into = pl.ds(at_row, rows)
                field[unit + shift, into, :TX] = cells[pl.ds(start, rows), :]
                field[unit + shift, into, TX:] = side[pl.ds(start, rows), :]

    if visits == 2:
        for flip in range(2):

            @pl.when(mine_ref[0] == flip)
            def _():
                assemble((0, 1) if flip == 0 else (1, 0))

    else:
        assemble(tuple(range(visits)))
    if fields["between"]:
        above_at, below_at = fields["between"]
        field[0, above_at : above_at + EDGE, :] = between_ref[:EDGE, :]
        field[spans - 1, below_at : below_at + EDGE, :] = between_ref[EDGE:, :]

    taps = [taps_ref[tap] for tap in range(7)]

    def across(value, by):
        return value if by == 0 else pltpu.roll(value, by % WIDE, 1)

    def three(value, by):
        return value + across(value, by) + across(value, -by)

    def stores(unit, source, rows, target):
        return [
            pltpu.make_async_copy(
                scratch.at[unit, pl.ds(source, rows)], hbm.at[pl.ds(target, rows)], sems.at[unit, at]
            )
            for at, (scratch, hbm) in enumerate(
                ((detection, detection_hbm), (variance, variance_hbm))
            )
        ]

    @pl.loop(0, spans)
    def _(unit):
        value = field[unit]
        sums = jnp.dot(sums_ref[...], value, preferred_element_type=jnp.float32)
        resid = value.astype(jnp.float32) - three(sums[:tall], 1) * (1.0 / 9.0)
        square = resid * resid
        coarse = square.astype(jnp.bfloat16)
        fine = (square - coarse.astype(jnp.float32)).astype(jnp.bfloat16)
        tower = jnp.dot(nine_ref[...], coarse, preferred_element_type=jnp.float32) + jnp.dot(
            nine_ref[...], fine, preferred_element_type=jnp.float32
        )
        local = three(three(tower, 1), 3)[:, :TX] * (1.0 / 81.0) + 1e-05
        rowwise = sums[tall : tall + short] + sums[tall + short :]
        blurred = sum(taps[tap] * across(rowwise, 3 - tap) for tap in range(7))
        variance[unit] = local
        detection[unit] = blurred[:, :TX] * lax.rsqrt(local)
        for begin, end, source, rows, shift in outs:

            @pl.when((unit >= begin) & (unit < end))
            def _():
                target = pl.multiple_of(unit * STEP + shift, HALO)
                for store in stores(unit, source, rows, target):
                    store.start()

    @pl.loop(0, spans)
    def _(unit):
        for begin, end, source, rows, shift in outs:

            @pl.when((unit >= begin) & (unit < end))
            def _():
                for store in stores(unit, source, rows, 0):
                    store.wait()


def stage(plan, mine, taps, between, tables, chunks, lots, held=()):
    fields, _, _ = plan
    spans, tall = fields["spans"], fields["tall"]
    shape = jax.ShapeDtypeStruct((TY, TX), jnp.float32)
    flat = [array for parts in chunks for part in parts for array in part]
    first = 5 + len(flat)
    out = pltpu.VMEM((spans, tall - 2 * fields["margin"], TX), jnp.float32)
    return pl.pallas_call(
        functools.partial(stage_kernel, plan, lots),
        out_shape=(shape, shape),
        in_specs=[SMEM, SMEM, VMEM, VMEM, VMEM] + [VMEM] * len(flat) + [HBM] * len(held),
        out_specs=(HBM, HBM),
        input_output_aliases={first + at: at for at in range(len(held))},
        scratch_shapes=[
            pltpu.VMEM((spans, tall, WIDE), jnp.bfloat16),
            out,
            out,
            pltpu.SemaphoreType.DMA((spans, 2)),
        ]
        + [pltpu.VMEM((part[0].shape[0], SIDE), jnp.bfloat16) for parts in chunks for part in parts],
        compiler_params=pltpu.CompilerParams(vmem_limit_bytes=56 * MIB),
        cost_estimate=pl.CostEstimate(
            flops=80 * spans * tall * WIDE, bytes_accessed=12 * spans * tall * WIDE, transcendentals=0
        ),
        name="stage",
    )(mine, taps, between, *tables, *flat, *held)


def outer_plan(lot):
    fields = dict(
        visits=2, aliased=0, spans=UNITS + 1, tall=2 * lot, margin=HALO, between=(lot - EDGE, lot),
        blank=[(0, 0, lot - EDGE), (UNITS, lot + EDGE, lot - EDGE)],
    )
    copies = [(0, 1, 0, lot, 0, 0, UNITS, 1), (0, 0, 0, lot, lot, 0, UNITS, 0)]
    rows = lot - HALO
    outs = [
        (0, 1, rows, rows, 0),
        (1, UNITS, 0, 2 * rows, -rows),
        (UNITS, UNITS + 1, 0, rows, -rows),
    ]
    return fields, copies, outs


def inner_plan(lot, inner):
    tall = 2 * inner + 2 * EDGE
    fields = dict(
        visits=2, aliased=2, spans=UNITS, tall=tall, margin=HALO, between=None, blank=[]
    )
    copies = [
        (0, 0, lot - EDGE, EDGE, 0, 0, UNITS, 0),
        (1, 0, 0, inner, EDGE, 0, UNITS, 0),
        (1, 1, 0, inner, EDGE + inner, 0, UNITS, 0),
        (0, 1, 0, EDGE, EDGE + 2 * inner, 0, UNITS, 0),
    ]
    return fields, copies, [(0, UNITS, 0, tall - 2 * HALO, lot - HALO)]


def whole_plan(lot, visits):
    fields = dict(
        visits=visits, aliased=0, spans=UNITS, tall=STEP + 2 * EDGE, margin=EDGE,
        between=(0, EDGE + STEP), blank=[],
    )
    copies = [(0, visit, 0, lot, EDGE + visit * lot, 0, UNITS, 0) for visit in range(visits)]
    copies.append((0, visits - 1, lot - EDGE, EDGE, 0, 0, UNITS - 1, 1))
    copies.append((0, 0, 0, EDGE, EDGE + STEP, 1, UNITS, -1))
    return fields, copies, [(0, UNITS, 0, STEP, 0)]


def per_device(
    images, inv_var, good_columns, warp_rows, warp_cols, block_visit, dest_tile, offsets, psf_taps
):
    tiles = lax.axis_size("py") * lax.axis_size("px")
    visits = lax.axis_size("visit")
    plan = shares(visits)
    lots = [rows for rows, _ in plan]
    mine = lax.axis_index("visit").astype(jnp.int32).reshape(1)

    def make(chunk, var):
        return warp(
            tiles, plan[chunk], chunk == 0, block_visit, dest_tile[:, 0], offsets.T,
            good_columns, warp_rows, warp_cols, var, images,
        )

    def send(blocks):
        return lax.all_to_all(blocks, EVERY, split_axis=0, concat_axis=0, tiled=True)

    made, psf_taps = lax.optimization_barrier((make(0, inv_var), psf_taps))
    arrived = send(made)
    if len(plan) == 1:
        code = codes(arrived)
        coadd, strip, edge = place(code, arrived, lots[0])
        parts = spread(coadd, strip)
        if visits > 1:
            edges = lax.all_gather(edge, "visit")
            edge = (edges[visits - 1], edges[0])
        else:
            edge = (edge, edge)
        between = rows_between(edge, parts)
        every = whole_plan(lots[0], visits)
        return stage(every, mine, psf_taps, between, bands(every, psf_taps), [parts], lots)

    outer, inner = outer_plan(lots[0]), inner_plan(*lots)
    tables, inv_var = lax.optimization_barrier(
        ([bands(part, psf_taps) for part in (outer, inner)], inv_var)
    )
    arrived, later = lax.optimization_barrier((arrived, make(1, inv_var)))
    second = send(later)
    code = codes(arrived)
    coadd, strip, edge = place(code, arrived, lots[0])
    parts = spread(coadd, strip)
    between = rows_between(edge, parts)
    held = stage(outer, mine, psf_taps, between, tables[0], [parts], lots[:1])
    second, held = lax.optimization_barrier((second, held))
    coadd, strip, _ = place(code, second, lots[1])
    more = spread(coadd, strip)
    return stage(inner, mine, psf_taps, between, tables[1], [parts, more], lots, held)


def codes(arrived):
    note = arrived[:, arrived.shape[1] - NOTE, :: SIDE // CAP]
    return note.astype(jnp.float32).astype(jnp.int32).reshape(-1)


def solution(mesh):
    in_specs = (
        P(EVERY, None, None),
        P(EVERY, None, None),
        P("visit", None),
        P("visit", None, None),
        P("visit", None, None),
        P(EVERY),
        P(EVERY, None),
        P(EVERY, None),
        P(),
    )
    out_specs = (P("py", "px"), P("py", "px"))
    return jax.shard_map(
        per_device, mesh=mesh, in_specs=in_specs, out_specs=out_specs, check_vma=False
    )
```

```python
import functools

import jax
import jax.numpy as jnp
from jax import lax
from jax.experimental import pallas as pl
from jax.experimental.pallas import tpu as pltpu
from jax.sharding import PartitionSpec as P

TY = 1024
TX = 1024
STEP = 128
CAP = 2
UNITS = TY // STEP
HALO = 8
EDGE = 16
SIDE = 128
WIDE = TX + SIDE
GROUP = 4
NOTE = 16
MIB = 1 << 20
EVERY = ("visit", "py", "px")
HBM = pl.BlockSpec(memory_space=pltpu.HBM)
SMEM = pl.BlockSpec(memory_space=pltpu.SMEM)
VMEM = pl.BlockSpec(memory_space=pltpu.VMEM)


def shares(visits):
    if visits == 2:
        edge, inner = 48, 16
        return [(edge, (0, STEP - edge)), (inner, (edge, edge + inner))]
    rows = STEP // visits
    return [(rows, tuple(visit * rows for visit in range(visits)))]


def warp_kernel(
    tiles, share, noted, visit_ref, tile_ref, offset_ref, good_ref, rows_hbm, cols_hbm, var_hbm,
    image_hbm, out_hbm, rows, cols, var, image, done, note, count, table_sems, sems, out_sems,
):
    blocks, side, _ = var.shape
    some, firsts = share
    groups = blocks // GROUP
    slot_rows = done.shape[2]
    tables = [
        pltpu.make_async_copy(rows_hbm, rows, table_sems.at[0]),
        pltpu.make_async_copy(cols_hbm, cols, table_sems.at[1]),
    ]

    def loads(group):
        span = pl.ds(group * GROUP, GROUP)
        return (
            pltpu.make_async_copy(var_hbm.at[span], var.at[span], sems.at[group, 0]),
            pltpu.make_async_copy(image_hbm.at[span], image.at[span], sems.at[group, 1]),
        )

    for load in tables:
        load.start()
    for group in range(groups):
        for load in loads(group):
            load.start()

    @pl.loop(0, tiles)
    def _(tile):
        count[tile] = 0

    if noted:
        note[...] = jnp.full(note.shape, -1, jnp.bfloat16)
        slot_of_lane = lax.broadcasted_iota(jnp.int32, (NOTE, SIDE), 1) // (SIDE // CAP)

    for load in tables:
        load.wait()

    strips = [first + strip * STEP for first in firsts for strip in range(side // STEP)]
    tall = some * len(strips)
    part = tall // len(firsts)

    @pl.loop(0, groups)
    def _(group):
        for load in loads(group):
            load.wait()
        visits = [visit_ref[group * GROUP + ahead] for ahead in range(GROUP)]
        planes, turned, warped = [], [], []
        for ahead in range(GROUP):
            block = group * GROUP + ahead
            good = good_ref[pl.ds(visits[ahead], 1), :].astype(jnp.float32)
            weight = var[block].astype(jnp.float32) * good
            data = weight * image[block].astype(jnp.float32)
            planes.append(
                jnp.concatenate([data.astype(jnp.bfloat16), weight.astype(jnp.bfloat16)], axis=1)
            )
        for ahead in range(GROUP):
            matrix = jnp.concatenate(
                [rows[visits[ahead], first : first + some, :] for first in strips], axis=0
            )
            turned.append(
                jnp.dot(matrix, planes[ahead], preferred_element_type=jnp.float32).astype(jnp.bfloat16)
            )
        for ahead in range(GROUP):
            both = jnp.concatenate([turned[ahead][:, :side], turned[ahead][:, side:]], axis=0)
            warped.append(
                lax.dot_general(
                    both,
                    cols[visits[ahead]],
                    (((1,), (1,)), ((), ())),
                    preferred_element_type=jnp.float32,
                ).astype(jnp.bfloat16)
            )
        for ahead in range(GROUP):
            block = group * GROUP + ahead
            for visit in range(len(firsts)):
                for half in range(side // SIDE):
                    for plane in range(2):
                        start = plane * tall + visit * part
                        into = (2 * half + plane) * part
                        done[block, visit, into : into + part, :] = warped[ahead][
                            start : start + part, half * SIDE : (half + 1) * SIDE
                        ]
        for ahead in range(GROUP):
            block = group * GROUP + ahead
            tile = tile_ref[block]
            rank = count[tile]
            count[tile] = rank + 1
            for visit in range(len(firsts)):
                target = visit * tiles + tile
                pltpu.make_async_copy(
                    done.at[block, visit],
                    out_hbm.at[target, pl.ds(pl.multiple_of(rank * slot_rows, NOTE), slot_rows)],
                    out_sems.at[block, visit],
                ).start()
                if noted:
                    code = offset_ref[0, block] * 8 + offset_ref[1, block]
                    note[target] = jnp.where(
                        slot_of_lane == rank, code.astype(jnp.float32), note[target].astype(jnp.float32)
                    ).astype(jnp.bfloat16)

    if noted:
        notes = pltpu.make_async_copy(
            note, out_hbm.at[:, pl.ds(CAP * slot_rows, NOTE)], table_sems.at[0]
        )
        notes.start()

    @pl.loop(0, blocks)
    def _(block):
        for visit in range(len(firsts)):
            pltpu.make_async_copy(
                done.at[block, visit], out_hbm.at[0, pl.ds(0, slot_rows)], out_sems.at[block, visit]
            ).wait()

    if noted:
        notes.wait()


def warp(tiles, share, noted, visit, tile, offset, good, rows, cols, var, image):
    blocks, side, _ = var.shape
    some, firsts = share
    slot_rows = 2 * (side // STEP) * some * (side // SIDE)
    visits = len(firsts)
    return pl.pallas_call(
        functools.partial(warp_kernel, tiles, share, noted),
        out_shape=jax.ShapeDtypeStruct(
            (visits * tiles, CAP * slot_rows + noted * NOTE, SIDE), jnp.bfloat16
        ),
        in_specs=[SMEM, SMEM, SMEM, VMEM, HBM, HBM, HBM, HBM],
        out_specs=HBM,
        scratch_shapes=[
            pltpu.VMEM(rows.shape, jnp.bfloat16),
            pltpu.VMEM(cols.shape, jnp.bfloat16),
            pltpu.VMEM(var.shape, jnp.bfloat16),
            pltpu.VMEM(var.shape, jnp.bfloat16),
            pltpu.VMEM((blocks, visits, slot_rows, SIDE), jnp.bfloat16),
            pltpu.VMEM((visits * tiles, NOTE, SIDE), jnp.bfloat16),
            pltpu.SMEM((tiles,), jnp.int32),
            pltpu.SemaphoreType.DMA((2,)),
            pltpu.SemaphoreType.DMA((blocks // GROUP, 2)),
            pltpu.SemaphoreType.DMA((blocks, visits)),
        ],
        compiler_params=pltpu.CompilerParams(vmem_limit_bytes=60 * MIB),
        cost_estimate=pl.CostEstimate(
            flops=8 * blocks * side**3, bytes_accessed=8 * blocks * side**2, transcendentals=0
        ),
        name="warp",
    )(visit, tile, offset, good, rows, cols, var, image)


def place_kernel(part, code_ref, blocks_ref, coadd_ref, strip_ref, edge_ref, data, weight):
    step = pl.program_id(0)
    some = blocks_ref.shape[0]
    height = data.shape[0]
    lot = height // UNITS

    @pl.when(step == 0)
    def _():
        data[...] = jnp.zeros_like(data)
        weight[...] = jnp.zeros_like(weight)

    for block in range(some):
        for slot in range(CAP):
            code = code_ref[(step * some + block) * CAP + slot]

            @pl.when(code >= 0)
            def _():
                row = pl.multiple_of((code // 8) * lot, lot)
                for half in range(2):
                    col = pl.multiple_of((code % 8 + half) * STEP, STEP)
                    cells = (pl.ds(row, part), pl.ds(col, STEP))
                    first = (slot * 2 + half) * 2 * part
                    data[cells] += blocks_ref[block, first : first + part].astype(jnp.float32)
                    weight[cells] += blocks_ref[block, first + part : first + 2 * part].astype(
                        jnp.float32
                    )

    @pl.when(step == pl.num_programs(0) - 1)
    def _():
        coadd = data[...] / jnp.maximum(weight[...], 1.0)
        coadd_ref[...] = coadd.astype(coadd_ref.dtype)
        strip_ref[:HALO] = coadd[:, :SIDE].T[:HALO]
        strip_ref[HALO:] = coadd[:, TX - SIDE :].T[SIDE - HALO :]
        edge_ref[:HALO] = coadd[:HALO]
        edge_ref[HALO:] = coadd[height - HALO :]


def place(code, blocks, lot):
    count, tall, side = blocks.shape
    some = 4
    height = lot * UNITS
    shapes = [((height, TX), jnp.bfloat16), ((2 * HALO, height), jnp.float32), ((2 * HALO, TX), jnp.float32)]
    return pl.pallas_call(
        functools.partial(place_kernel, 2 * lot),
        grid_spec=pltpu.PrefetchScalarGridSpec(
            num_scalar_prefetch=1,
            grid=(count // some,),
            in_specs=[pl.BlockSpec((some, tall, side), lambda step, code: (step, 0, 0))],
            out_specs=[pl.BlockSpec(shape, lambda step, code: (0, 0)) for shape, _ in shapes],
            scratch_shapes=[pltpu.VMEM((height, TX), jnp.float32)] * 2,
        ),
        out_shape=[jax.ShapeDtypeStruct(*shape) for shape in shapes],
        compiler_params=pltpu.CompilerParams(vmem_limit_bytes=32 * MIB),
        cost_estimate=pl.CostEstimate(
            flops=count * tall * side, bytes_accessed=count * tall * side * 2, transcendentals=0
        ),
        name="place",
    )(code, blocks)


def beside(axis):
    count = lax.axis_size(axis)
    up = [(i, i + 1) for i in range(count - 1)]
    return up, [(j, i) for i, j in up]


def neighbours(first, last, axis):
    up, down = beside(axis)
    return lax.ppermute(last, axis, up), lax.ppermute(first, axis, down)


def swapped(array):
    return lax.ppermute(array, "visit", [(0, 1), (1, 0)])


def beyond(strips, above, below):
    first = [strip[:HALO] for strip in strips] + [rows[:, :SIDE] for rows in (above, below)]
    last = [strip[HALO:] for strip in strips] + [rows[:, TX - SIDE :] for rows in (above, below)]
    return neighbours(jnp.concatenate(first, axis=1), jnp.concatenate(last, axis=1), "px")


def straight_to_both(strip):
    first, last = strip[:HALO], strip[HALO:]
    count = lax.axis_size("px")
    up, down = beside("px")

    def crossed(pairs):
        return [(v * count + i, (1 - v) * count + j) for v in range(2) for i, j in pairs]

    own = neighbours(first, last, "px")
    return own, (
        lax.ppermute(last, ("visit", "px"), crossed(up)),
        lax.ppermute(first, ("visit", "px"), crossed(down)),
    )


def rows_between(edge):
    lower = lax.axis_index("visit") == 0
    mine = jnp.where(lower, edge[:HALO], edge[HALO:])
    count = lax.axis_size("py")
    up, down = beside("py")

    def pairs(cross):
        return [(i, j + cross * count) for i, j in down] + [
            (count + i, j + (1 - cross) * count) for i, j in up
        ]

    straight = lax.ppermute(mine, ("visit", "py"), pairs(0))
    crossed = lax.ppermute(mine, ("visit", "py"), pairs(1))
    return jnp.where(lower, crossed, straight), jnp.where(lower, straight, crossed)


def bands(plan, taps):
    tall, margin = plan[0]["tall"], plan[0]["margin"]
    row = jnp.arange(tall, dtype=jnp.int32)
    out = jnp.arange(tall - 2 * margin, dtype=jnp.int32) + margin
    three = (jnp.abs(row[:, None] - row[None, :]) <= 1).astype(jnp.bfloat16)
    nine = (jnp.abs(out[:, None] - row[None, :]) <= 4).astype(jnp.bfloat16)
    count = taps.shape[0]
    ahead = row[None, :] - out[:, None] + count // 2
    coarse, fine = split(sum(jnp.where(ahead == tap, taps[tap], 0.0) for tap in range(count)))
    lane = jnp.arange(4 * SIDE, dtype=jnp.int32)
    across = jnp.abs(lane[:, None] - lane[None, SIDE : 3 * SIDE]) <= 4
    return (
        jnp.concatenate([three] * 2, axis=1),
        jnp.concatenate([nine] * 2, axis=1),
        jnp.concatenate([coarse, coarse, fine], axis=1),
        across.astype(jnp.bfloat16),
    )


def split(value):
    coarse = value.astype(jnp.bfloat16)
    return coarse, (value - coarse.astype(jnp.float32)).astype(jnp.bfloat16)


def filtered(value, taps, tables, margin):
    three, nine, blur, across = [table[...] for table in tables]
    tall = value.shape[0]
    short = tall - 2 * margin

    def product(matrix, terms):
        return jnp.dot(matrix, jnp.concatenate(terms, axis=0), preferred_element_type=jnp.float32)

    moved = {
        by: (pltpu.roll(value, -by % WIDE, 1) if by else value).astype(jnp.float32)
        for by in range(-3, 4)
    }
    rowwise = sum(taps[tap] * moved[tap - 3] for tap in range(7))[:, :TX]
    resid = moved[0] - product(three, split(moved[-1] + moved[0] + moved[1])) * (1.0 / 9.0)
    tower = jnp.concatenate(split(product(nine, split(resid * resid))), axis=0)
    windows = [jnp.concatenate([tower[:, TX:], tower[:, : 3 * SIDE]], axis=1)]
    for start in range(2 * SIDE, TX, 2 * SIDE):
        windows.append(tower[:, start - SIDE : start + 3 * SIDE])
    boxes = jnp.dot(jnp.concatenate(windows, axis=0), across, preferred_element_type=jnp.float32)
    box = jnp.concatenate(
        [
            boxes[2 * at * short : (2 * at + 1) * short] + boxes[(2 * at + 1) * short : (2 * at + 2) * short]
            for at in range(len(windows))
        ],
        axis=1,
    )
    local = box * (1.0 / 81.0) + 1e-05
    coarse, fine = split(rowwise)
    return product(blur, (coarse, fine, coarse)) * lax.rsqrt(local), local


def stage_kernel(plan, lots, *refs):
    mine_ref, taps_ref, above_ref, below_ref = refs[:4]
    tables = refs[4:8]
    fields, copies, outs = plan
    visits, margin = fields["visits"], fields["margin"]
    at = 8
    chunks = []
    for lot in lots:
        parts = []
        for _ in range(visits):
            parts.append(refs[at : at + 3])
            at += 3
        chunks.append(parts)
    at += fields["aliased"]
    detection_hbm, variance_hbm = refs[at : at + 2]
    field, detection, variance, sems = refs[at + 2 : at + 6]
    sides = refs[at + 6 :]
    spans, tall, _ = field.shape

    which = 0
    held = []
    for parts in chunks:
        group = []
        for number, (cells, left, right) in enumerate(parts):
            side = sides[which]
            which += 1
            height = cells.shape[0]
            first = number * height if left.shape[1] > height else 0
            here = slice(first, first + height)
            gap = jnp.zeros((SIDE - 2 * HALO, height), jnp.float32)
            side[...] = jnp.concatenate([right[:, here], gap, left[:, here]], axis=0).T.astype(
                jnp.bfloat16
            )
            group.append((cells, side))
        held.append(group)

    for span, first, rows in fields["blank"]:
        field[span, first : first + rows, :] = jnp.zeros((rows, WIDE), jnp.bfloat16)

    def assemble(order):
        for chunk, visit, first, rows, at_row, begin, end, shift in copies:
            cells, side = held[chunk][order[visit]]
            lot = lots[chunk]

            @pl.loop(begin, end)
            def _(unit):
                start = pl.multiple_of(unit * lot + first, EDGE)
                into = pl.ds(at_row, rows)
                field[unit + shift, into, :TX] = cells[pl.ds(start, rows), :]
                field[unit + shift, into, TX:] = side[pl.ds(start, rows), :]

    if visits == 2:
        for flip in range(2):

            @pl.when(mine_ref[0] == flip)
            def _():
                assemble((0, 1) if flip == 0 else (1, 0))

    else:
        assemble(tuple(range(visits)))

    if fields["between"]:
        _, left, right = chunks[0][0]
        corners = left.shape[1] - 2 * SIDE
        from_left = lax.broadcasted_iota(jnp.int32, (HALO, SIDE), 1) >= SIDE // 2
        none = jnp.zeros((EDGE - HALO, WIDE), jnp.float32)
        for number, (span, first, rows) in enumerate(
            zip((0, spans - 1), fields["between"], (above_ref, below_ref))
        ):
            here = slice(corners + number * SIDE, corners + (number + 1) * SIDE)
            wide = jnp.concatenate(
                [rows[...], jnp.where(from_left, left[:, here], right[:, here])], axis=1
            )
            strip = [none, wide] if number == 0 else [wide, none]
            field[span, first : first + EDGE, :] = jnp.concatenate(strip, axis=0).astype(jnp.bfloat16)

    taps = [taps_ref[tap] for tap in range(7)]

    def stores(unit, source, rows, target):
        return [
            pltpu.make_async_copy(
                scratch.at[unit, pl.ds(source, rows)], hbm.at[pl.ds(target, rows)], sems.at[unit, at]
            )
            for at, (scratch, hbm) in enumerate(
                ((detection, detection_hbm), (variance, variance_hbm))
            )
        ]

    some = next(count for count in (4, 3, 2, 1) if spans % count == 0 and count * tall <= 320)

    @pl.loop(0, spans, step=some)
    def _(first):
        for ahead in range(some):
            unit = first + ahead
            detection[unit], variance[unit] = filtered(field[unit], taps, tables, margin)
        for ahead in range(some):
            unit = first + ahead
            for begin, end, source, rows, shift in outs:

                @pl.when((unit >= begin) & (unit < end))
                def _():
                    target = pl.multiple_of(unit * STEP + shift, HALO)
                    for store in stores(unit, source, rows, target):
                        store.start()

    @pl.loop(0, spans)
    def _(unit):
        for begin, end, source, rows, shift in outs:

            @pl.when((unit >= begin) & (unit < end))
            def _():
                for store in stores(unit, source, rows, 0):
                    store.wait()


def stage(plan, mine, taps, between, tables, chunks, lots, held=()):
    fields, _, _ = plan
    spans, tall = fields["spans"], fields["tall"]
    shape = jax.ShapeDtypeStruct((TY, TX), jnp.float32)
    flat = [array for parts in chunks for part in parts for array in part]
    first = 8 + len(flat)
    out = pltpu.VMEM((spans, tall - 2 * fields["margin"], TX), jnp.float32)
    return pl.pallas_call(
        functools.partial(stage_kernel, plan, lots),
        out_shape=(shape, shape),
        in_specs=[SMEM, SMEM] + [VMEM] * (6 + len(flat)) + [HBM] * len(held),
        out_specs=(HBM, HBM),
        input_output_aliases={first + at: at for at in range(len(held))},
        scratch_shapes=[
            pltpu.VMEM((spans, tall, WIDE), jnp.bfloat16),
            out,
            out,
            pltpu.SemaphoreType.DMA((spans, 2)),
        ]
        + [pltpu.VMEM((part[0].shape[0], SIDE), jnp.bfloat16) for parts in chunks for part in parts],
        compiler_params=pltpu.CompilerParams(vmem_limit_bytes=56 * MIB),
        cost_estimate=pl.CostEstimate(
            flops=80 * spans * tall * WIDE, bytes_accessed=12 * spans * tall * WIDE, transcendentals=0
        ),
        name="stage",
    )(mine, taps, *between, *tables, *flat, *held)


def outer_plan(lot):
    fields = dict(
        visits=2, aliased=0, spans=UNITS + 1, tall=2 * lot, margin=HALO, between=(lot - EDGE, lot),
        blank=[(0, 0, lot - EDGE), (UNITS, lot + EDGE, lot - EDGE)],
    )
    copies = [(0, 1, 0, lot, 0, 0, UNITS, 1), (0, 0, 0, lot, lot, 0, UNITS, 0)]
    rows = lot - HALO
    outs = [
        (0, 1, rows, rows, 0),
        (1, UNITS, 0, 2 * rows, -rows),
        (UNITS, UNITS + 1, 0, rows, -rows),
    ]
    return fields, copies, outs


def inner_plan(lot, inner):
    tall = 2 * inner + 2 * EDGE
    fields = dict(
        visits=2, aliased=2, spans=UNITS, tall=tall, margin=HALO, between=None, blank=[]
    )
    copies = [
        (0, 0, lot - EDGE, EDGE, 0, 0, UNITS, 0),
        (1, 0, 0, inner, EDGE, 0, UNITS, 0),
        (1, 1, 0, inner, EDGE + inner, 0, UNITS, 0),
        (0, 1, 0, EDGE, EDGE + 2 * inner, 0, UNITS, 0),
    ]
    return fields, copies, [(0, UNITS, 0, tall - 2 * HALO, lot - HALO)]


def whole_plan(lot, visits):
    fields = dict(
        visits=visits, aliased=0, spans=UNITS, tall=STEP + 2 * EDGE, margin=EDGE,
        between=(0, EDGE + STEP), blank=[],
    )
    copies = [(0, visit, 0, lot, EDGE + visit * lot, 0, UNITS, 0) for visit in range(visits)]
    copies.append((0, visits - 1, lot - EDGE, EDGE, 0, 0, UNITS - 1, 1))
    copies.append((0, 0, 0, EDGE, EDGE + STEP, 1, UNITS, -1))
    return fields, copies, [(0, UNITS, 0, STEP, 0)]


def per_device(
    images, inv_var, good_columns, warp_rows, warp_cols, block_visit, dest_tile, offsets, psf_taps
):
    tiles = lax.axis_size("py") * lax.axis_size("px")
    visits = lax.axis_size("visit")
    plan = shares(visits)
    lots = [rows for rows, _ in plan]
    mine = lax.axis_index("visit").astype(jnp.int32).reshape(1)

    def make(chunk, var):
        return warp(
            tiles, plan[chunk], chunk == 0, block_visit, dest_tile[:, 0], offsets.T,
            good_columns, warp_rows, warp_cols, var, images,
        )

    def send(blocks):
        return lax.all_to_all(blocks, EVERY, split_axis=0, concat_axis=0, tiled=True)

    made, psf_taps = lax.optimization_barrier((make(0, inv_var), psf_taps))
    arrived = send(made)
    if len(plan) == 1:
        every = whole_plan(lots[0], visits)
        coadd, strip, edge = place(codes(arrived), arrived, lots[0])
        all_of = [lax.all_gather(part, "visit") for part in (coadd, strip, edge)]
        between = neighbours(all_of[2][0, :HALO], all_of[2][visits - 1, HALO:], "py")
        sides = beyond([all_of[1][visit] for visit in range(visits)], *between)
        parts = [(all_of[0][visit], *sides) for visit in range(visits)]
        return stage(every, mine, psf_taps, between, bands(every, psf_taps), [parts], lots)

    outer, inner = outer_plan(lots[0]), inner_plan(*lots)
    tables, inv_var = lax.optimization_barrier(
        ([bands(part, psf_taps) for part in (outer, inner)], inv_var)
    )
    arrived, later = lax.optimization_barrier((arrived, make(1, inv_var)))
    second = send(later)
    code = codes(arrived)
    coadd, strip, edge = place(code, arrived, lots[0])
    other = swapped(coadd)
    between = rows_between(edge)
    sides = beyond([strip, swapped(strip)], *between)
    parts = [(coadd, *sides), (other, *sides)]
    coadd, strip, _ = place(code, second, lots[1])
    own_sides, other_sides = straight_to_both(strip)
    more = [(coadd, *own_sides), (swapped(coadd), *other_sides)]
    (parts, between), _ = lax.optimization_barrier(((parts, between), coadd))
    held = stage(outer, mine, psf_taps, between, tables[0], [parts], lots[:1])
    return stage(inner, mine, psf_taps, between, tables[1], [parts, more], lots, held)


def codes(arrived):
    note = arrived[:, arrived.shape[1] - NOTE, :: SIDE // CAP]
    return note.astype(jnp.float32).astype(jnp.int32).reshape(-1)


def solution(mesh):
    in_specs = (
        P(EVERY, None, None),
        P(EVERY, None, None),
        P("visit", None),
        P("visit", None, None),
        P("visit", None, None),
        P(EVERY),
        P(EVERY, None),
        P(EVERY, None),
        P(),
    )
    out_specs = (P("py", "px"), P("py", "px"))
    return jax.shard_map(
        per_device, mesh=mesh, in_specs=in_specs, out_specs=out_specs, check_vma=False
    )
```

```python
import functools

import jax
import jax.numpy as jnp
from jax import lax
from jax.experimental import pallas as pl
from jax.experimental.pallas import tpu as pltpu
from jax.sharding import PartitionSpec as P

TY = 1024
TX = 1024
STEP = 128
CAP = 2
UNITS = TY // STEP
HALO = 8
EDGE = 16
SIDE = 128
WIDE = TX + SIDE
GROUP = 4
NOTE = 16
MIB = 1 << 20
EVERY = ("visit", "py", "px")
HBM = pl.BlockSpec(memory_space=pltpu.HBM)
SMEM = pl.BlockSpec(memory_space=pltpu.SMEM)
VMEM = pl.BlockSpec(memory_space=pltpu.VMEM)


def shares(visits):
    if visits == 2:
        edge, inner = 48, 16
        return [(edge, (0, STEP - edge)), (inner, (edge, edge + inner))]
    rows = STEP // visits
    return [(rows, tuple(visit * rows for visit in range(visits)))]


def warp_kernel(
    tiles, share, noted, visit_ref, tile_ref, offset_ref, good_ref, rows_hbm, cols_hbm, var_hbm,
    image_hbm, out_hbm, rows, cols, var, image, done, note, count, table_sems, sems, out_sems,
):
    blocks, side, _ = var.shape
    some, firsts = share
    groups = blocks // GROUP
    slot_rows = done.shape[2]
    tables = [
        pltpu.make_async_copy(rows_hbm, rows, table_sems.at[0]),
        pltpu.make_async_copy(cols_hbm, cols, table_sems.at[1]),
    ]

    def loads(group):
        span = pl.ds(group * GROUP, GROUP)
        return (
            pltpu.make_async_copy(var_hbm.at[span], var.at[span], sems.at[group, 0]),
            pltpu.make_async_copy(image_hbm.at[span], image.at[span], sems.at[group, 1]),
        )

    for load in tables:
        load.start()
    for group in range(groups):
        for load in loads(group):
            load.start()

    @pl.loop(0, tiles)
    def _(tile):
        count[tile] = 0

    if noted:
        note[...] = jnp.full(note.shape, -1, jnp.bfloat16)
        slot_of_lane = lax.broadcasted_iota(jnp.int32, (NOTE, SIDE), 1) // (SIDE // CAP)

    for load in tables:
        load.wait()

    strips = [first + strip * STEP for first in firsts for strip in range(side // STEP)]
    tall = some * len(strips)
    part = tall // len(firsts)

    @pl.loop(0, groups)
    def _(group):
        for load in loads(group):
            load.wait()
        visits = [visit_ref[group * GROUP + ahead] for ahead in range(GROUP)]
        planes, turned, warped = [], [], []
        for ahead in range(GROUP):
            block = group * GROUP + ahead
            good = good_ref[pl.ds(visits[ahead], 1), :].astype(jnp.float32)
            weight = var[block].astype(jnp.float32) * good
            data = weight * image[block].astype(jnp.float32)
            planes.append(
                jnp.concatenate([data.astype(jnp.bfloat16), weight.astype(jnp.bfloat16)], axis=1)
            )
        for ahead in range(GROUP):
            matrix = jnp.concatenate(
                [rows[visits[ahead], first : first + some, :] for first in strips], axis=0
            )
            turned.append(
                jnp.dot(matrix, planes[ahead], preferred_element_type=jnp.float32).astype(jnp.bfloat16)
            )
        for ahead in range(GROUP):
            both = jnp.concatenate([turned[ahead][:, :side], turned[ahead][:, side:]], axis=0)
            warped.append(
                lax.dot_general(
                    both,
                    cols[visits[ahead]],
                    (((1,), (1,)), ((), ())),
                    preferred_element_type=jnp.float32,
                ).astype(jnp.bfloat16)
            )
        for ahead in range(GROUP):
            block = group * GROUP + ahead
            for visit in range(len(firsts)):
                for half in range(side // SIDE):
                    for plane in range(2):
                        start = plane * tall + visit * part
                        into = (2 * half + plane) * part
                        done[block, visit, into : into + part, :] = warped[ahead][
                            start : start + part, half * SIDE : (half + 1) * SIDE
                        ]
        for ahead in range(GROUP):
            block = group * GROUP + ahead
            tile = tile_ref[block]
            rank = count[tile]
            count[tile] = rank + 1
            for visit in range(len(firsts)):
                target = visit * tiles + tile
                pltpu.make_async_copy(
                    done.at[block, visit],
                    out_hbm.at[target, pl.ds(pl.multiple_of(rank * slot_rows, NOTE), slot_rows)],
                    out_sems.at[block, visit],
                ).start()
                if noted:
                    code = offset_ref[0, block] * 8 + offset_ref[1, block]
                    note[target] = jnp.where(
                        slot_of_lane == rank, code.astype(jnp.float32), note[target].astype(jnp.float32)
                    ).astype(jnp.bfloat16)

    if noted:
        notes = pltpu.make_async_copy(
            note, out_hbm.at[:, pl.ds(CAP * slot_rows, NOTE)], table_sems.at[0]
        )
        notes.start()

    @pl.loop(0, blocks)
    def _(block):
        for visit in range(len(firsts)):
            pltpu.make_async_copy(
                done.at[block, visit], out_hbm.at[0, pl.ds(0, slot_rows)], out_sems.at[block, visit]
            ).wait()

    if noted:
        notes.wait()


def warp(tiles, share, noted, visit, tile, offset, good, rows, cols, var, image):
    blocks, side, _ = var.shape
    some, firsts = share
    slot_rows = 2 * (side // STEP) * some * (side // SIDE)
    visits = len(firsts)
    return pl.pallas_call(
        functools.partial(warp_kernel, tiles, share, noted),
        out_shape=jax.ShapeDtypeStruct(
            (visits * tiles, CAP * slot_rows + noted * NOTE, SIDE), jnp.bfloat16
        ),
        in_specs=[SMEM, SMEM, SMEM, VMEM, HBM, HBM, HBM, HBM],
        out_specs=HBM,
        scratch_shapes=[
            pltpu.VMEM(rows.shape, jnp.bfloat16),
            pltpu.VMEM(cols.shape, jnp.bfloat16),
            pltpu.VMEM(var.shape, jnp.bfloat16),
            pltpu.VMEM(var.shape, jnp.bfloat16),
            pltpu.VMEM((blocks, visits, slot_rows, SIDE), jnp.bfloat16),
            pltpu.VMEM((visits * tiles, NOTE, SIDE), jnp.bfloat16),
            pltpu.SMEM((tiles,), jnp.int32),
            pltpu.SemaphoreType.DMA((2,)),
            pltpu.SemaphoreType.DMA((blocks // GROUP, 2)),
            pltpu.SemaphoreType.DMA((blocks, visits)),
        ],
        compiler_params=pltpu.CompilerParams(vmem_limit_bytes=60 * MIB),
        cost_estimate=pl.CostEstimate(
            flops=8 * blocks * side**3, bytes_accessed=8 * blocks * side**2, transcendentals=0
        ),
        name="warp",
    )(visit, tile, offset, good, rows, cols, var, image)


def place_kernel(part, code_ref, blocks_ref, coadd_ref, strip_ref, edge_ref, data, weight):
    step = pl.program_id(0)
    some = blocks_ref.shape[0]
    height = data.shape[0]
    lot = height // UNITS

    @pl.when(step == 0)
    def _():
        data[...] = jnp.zeros_like(data)
        weight[...] = jnp.zeros_like(weight)

    for block in range(some):
        for slot in range(CAP):
            code = code_ref[(step * some + block) * CAP + slot]

            @pl.when(code >= 0)
            def _():
                row = pl.multiple_of((code // 8) * lot, lot)
                for half in range(2):
                    col = pl.multiple_of((code % 8 + half) * STEP, STEP)
                    cells = (pl.ds(row, part), pl.ds(col, STEP))
                    first = (slot * 2 + half) * 2 * part
                    data[cells] += blocks_ref[block, first : first + part].astype(jnp.float32)
                    weight[cells] += blocks_ref[block, first + part : first + 2 * part].astype(
                        jnp.float32
                    )

    @pl.when(step == pl.num_programs(0) - 1)
    def _():
        coadd = data[...] / jnp.maximum(weight[...], 1.0)
        coadd_ref[...] = coadd.astype(coadd_ref.dtype)
        strip_ref[:HALO] = coadd[:, :SIDE].T[:HALO]
        strip_ref[HALO:] = coadd[:, TX - SIDE :].T[SIDE - HALO :]
        edge_ref[:HALO] = coadd[:HALO]
        edge_ref[HALO:] = coadd[height - HALO :]


def place(code, blocks, lot):
    count, tall, side = blocks.shape
    some = 4
    height = lot * UNITS
    shapes = [((height, TX), jnp.bfloat16), ((2 * HALO, height), jnp.float32), ((2 * HALO, TX), jnp.float32)]
    return pl.pallas_call(
        functools.partial(place_kernel, 2 * lot),
        grid_spec=pltpu.PrefetchScalarGridSpec(
            num_scalar_prefetch=1,
            grid=(count // some,),
            in_specs=[pl.BlockSpec((some, tall, side), lambda step, code: (step, 0, 0))],
            out_specs=[pl.BlockSpec(shape, lambda step, code: (0, 0)) for shape, _ in shapes],
            scratch_shapes=[pltpu.VMEM((height, TX), jnp.float32)] * 2,
        ),
        out_shape=[jax.ShapeDtypeStruct(*shape) for shape in shapes],
        compiler_params=pltpu.CompilerParams(vmem_limit_bytes=32 * MIB),
        cost_estimate=pl.CostEstimate(
            flops=count * tall * side, bytes_accessed=count * tall * side * 2, transcendentals=0
        ),
        name="place",
    )(code, blocks)


def beside(axis):
    count = lax.axis_size(axis)
    up = [(i, i + 1) for i in range(count - 1)]
    return up, [(j, i) for i, j in up]


def neighbours(first, last, axis):
    up, down = beside(axis)
    return lax.ppermute(last, axis, up), lax.ppermute(first, axis, down)


def swapped(array):
    return lax.ppermute(array, "visit", [(0, 1), (1, 0)])


def beyond(strips, above, below):
    first = [strip[:HALO] for strip in strips] + [rows[:, :SIDE] for rows in (above, below)]
    last = [strip[HALO:] for strip in strips] + [rows[:, TX - SIDE :] for rows in (above, below)]
    return neighbours(jnp.concatenate(first, axis=1), jnp.concatenate(last, axis=1), "px")


def straight_to_both(strip):
    first, last = strip[:HALO], strip[HALO:]
    count = lax.axis_size("px")
    up, down = beside("px")

    def crossed(pairs):
        return [(v * count + i, (1 - v) * count + j) for v in range(2) for i, j in pairs]

    own = neighbours(first, last, "px")
    return own, (
        lax.ppermute(last, ("visit", "px"), crossed(up)),
        lax.ppermute(first, ("visit", "px"), crossed(down)),
    )


def rows_between(edge):
    lower = lax.axis_index("visit") == 0
    mine = jnp.where(lower, edge[:HALO], edge[HALO:])
    count = lax.axis_size("py")
    up, down = beside("py")

    def pairs(cross):
        return [(i, j + cross * count) for i, j in down] + [
            (count + i, j + (1 - cross) * count) for i, j in up
        ]

    straight = lax.ppermute(mine, ("visit", "py"), pairs(0))
    crossed = lax.ppermute(mine, ("visit", "py"), pairs(1))
    return jnp.where(lower, crossed, straight), jnp.where(lower, straight, crossed)


def bands(plan, taps):
    tall, margin = plan[0]["tall"], plan[0]["margin"]
    row = jnp.arange(tall, dtype=jnp.int32)
    out = jnp.arange(tall - 2 * margin, dtype=jnp.int32) + margin
    three = (jnp.abs(row[:, None] - row[None, :]) <= 1).astype(jnp.bfloat16)
    nine = (jnp.abs(out[:, None] - row[None, :]) <= 4).astype(jnp.bfloat16)
    count = taps.shape[0]
    ahead = row[None, :] - out[:, None] + count // 2
    coarse, fine = split(sum(jnp.where(ahead == tap, taps[tap], 0.0) for tap in range(count)))
    lane = jnp.arange(4 * SIDE, dtype=jnp.int32)
    across = jnp.abs(lane[:, None] - lane[None, SIDE : 3 * SIDE]) <= 4
    return (
        jnp.concatenate([three] * 2, axis=1),
        jnp.concatenate([nine] * 2, axis=1),
        jnp.concatenate([coarse, coarse, fine], axis=1),
        across.astype(jnp.bfloat16),
    )


def split(value):
    coarse = value.astype(jnp.bfloat16)
    return coarse, (value - coarse.astype(jnp.float32)).astype(jnp.bfloat16)


def filtered(value, taps, tables, margin):
    three, nine, blur, across = [table[...] for table in tables]
    tall = value.shape[0]
    short = tall - 2 * margin

    def product(matrix, terms):
        return jnp.dot(matrix, jnp.concatenate(terms, axis=0), preferred_element_type=jnp.float32)

    moved = {
        by: (pltpu.roll(value, -by % WIDE, 1) if by else value).astype(jnp.float32)
        for by in range(-3, 4)
    }
    rowwise = sum(taps[tap] * moved[tap - 3] for tap in range(7))[:, :TX]
    resid = moved[0] - product(three, split(moved[-1] + moved[0] + moved[1])) * (1.0 / 9.0)
    tower = jnp.concatenate(split(product(nine, split(resid * resid))), axis=0)
    windows = [jnp.concatenate([tower[:, TX:], tower[:, : 3 * SIDE]], axis=1)]
    for start in range(2 * SIDE, TX, 2 * SIDE):
        windows.append(tower[:, start - SIDE : start + 3 * SIDE])
    boxes = jnp.dot(jnp.concatenate(windows, axis=0), across, preferred_element_type=jnp.float32)
    box = jnp.concatenate(
        [
            boxes[2 * at * short : (2 * at + 1) * short] + boxes[(2 * at + 1) * short : (2 * at + 2) * short]
            for at in range(len(windows))
        ],
        axis=1,
    )
    local = box * (1.0 / 81.0) + 1e-05
    coarse, fine = split(rowwise)
    return product(blur, (coarse, fine, coarse)) * lax.rsqrt(local), local


def stage_kernel(plan, mend, lots, *refs):
    mine_ref, taps_ref, above_ref, below_ref = refs[:4]
    fields, copies, outs = plan
    visits, bare = fields["visits"], fields["bare"]
    tables, at = refs[4:8], 8
    if mend:
        mend_tables, at = refs[8:12], 12
    chunks = []
    for lot in lots:
        parts = []
        for _ in range(visits):
            parts.append(refs[at : at + (1 if bare else 3)])
            at += len(parts[-1])
        chunks.append(parts)
    held_hbm = refs[at : at + (2 if mend else 0)]
    at += len(held_hbm)
    out_hbm = refs[at : at + 2]
    field, detection, variance, sems = refs[at + 2 : at + 6]
    at += 6
    if mend:
        rim, columns, column_sems = refs[at : at + 3]
        at += 3
    sides = refs[at:]
    results = (detection, variance)
    spans, tall, _ = field.shape

    def column_copies(hbm, back):
        found = []
        for number, ref in enumerate(hbm):
            for edge in range(2):
                far = ref.at[:, pl.ds(edge * (TX - SIDE), SIDE)]
                near = columns.at[number, edge]
                source, target = (near, far) if back else (far, near)
                found.append(pltpu.make_async_copy(source, target, column_sems.at[number, edge]))
        return found

    if mend:
        for copy in column_copies(held_hbm, False):
            copy.start()

    which = 0
    held = []
    for parts in chunks:
        group = []
        for number, part in enumerate(parts):
            cells, side = part[0], None
            if not bare:
                _, left, right = part
                side = sides[which]
                which += 1
                height = cells.shape[0]
                first = number * height if left.shape[1] > height else 0
                here = slice(first, first + height)
                gap = jnp.zeros((SIDE - 2 * HALO, height), jnp.float32)
                side[...] = jnp.concatenate([right[:, here], gap, left[:, here]], axis=0).T.astype(
                    jnp.bfloat16
                )
            group.append((cells, side))
        held.append(group)

    def whole_rows(span, into, cells, side, rows):
        field[span, into, :TX] = cells[rows, :]
        if not bare:
            field[span, into, TX:] = side[rows, :]

    def rim_rows(span, into, cells, side, rows):
        rim[span, into, :SIDE] = cells[rows, :SIDE]
        rim[span, into, SIDE : 2 * SIDE] = cells[rows, TX - SIDE :]
        rim[span, into, 2 * SIDE :] = side[rows, :]

    def assemble(order, copies, put):
        for chunk, visit, first, rows, at_row, begin, end, shift in copies:
            cells, side = held[chunk][order[visit]]

            @pl.loop(begin, end)
            def _(unit):
                start = pl.multiple_of(unit * lots[chunk] + first, EDGE)
                put(unit + shift, pl.ds(at_row, rows), cells, side, pl.ds(start, rows))

    def assemble_all(order):
        assemble(order, copies, whole_rows)
        if mend:
            assemble(order, mend[1], rim_rows)

    if bare:
        field[:, :, TX:] = jnp.zeros((spans, tall, SIDE), jnp.bfloat16)
    for span, first, rows in fields["blank"]:
        field[span, first : first + rows, :] = jnp.zeros((rows, WIDE), jnp.bfloat16)
    if mend:
        for span, first, rows in mend[0]["blank"]:
            rim[span, first : first + rows, :] = jnp.zeros((rows, 3 * SIDE), jnp.bfloat16)
    if visits == 2:
        for flip in range(2):

            @pl.when(mine_ref[0] == flip)
            def _():
                assemble_all((0, 1) if flip == 0 else (1, 0))

    else:
        assemble_all(tuple(range(visits)))

    between = (mend or plan)[0]["between"]
    if between:
        from_left = lax.broadcasted_iota(jnp.int32, (HALO, SIDE), 1) >= SIDE // 2
        for number, rows in enumerate((above_ref, below_ref)):
            corner = jnp.zeros((HALO, SIDE), jnp.float32)
            if not bare:
                _, left, right = chunks[0][0]
                first = left.shape[1] + (number - 2) * SIDE
                here = slice(first, first + SIDE)
                corner = jnp.where(from_left, left[:, here], right[:, here])
            if mend:
                wide = jnp.concatenate([rows[:, :SIDE], rows[:, TX - SIDE :], corner], axis=1)
            else:
                wide = jnp.concatenate([rows[...], corner], axis=1)
            strip = [jnp.zeros_like(wide), wide] if number == 0 else [wide, jnp.zeros_like(wide)]
            strip = jnp.concatenate(strip, axis=0).astype(jnp.bfloat16)
            into = slice(between[number], between[number] + EDGE)
            if mend:
                rim[number * (rim.shape[0] - 1), into, :] = strip
            else:
                field[number * (spans - 1), into, :] = strip

    taps = [taps_ref[tap] for tap in range(7)]
    lane = lax.broadcasted_iota(jnp.int32, (1, SIDE), 1)

    if mend:
        for copy in column_copies(held_hbm, False):
            copy.wait()
        count = rim.shape[0]
        tiles = []
        for tile in range(WIDE // SIDE):
            pair = jnp.zeros(rim.shape[1:2] + (SIDE,), jnp.bfloat16)
            for span in range(2 * tile, min(2 * tile + 2, count)):
                base = (span % 2) * (SIDE // 2)
                near, far, halo = (rim[span, :, at * SIDE : (at + 1) * SIDE] for at in range(3))
                for value, first, last, by in (
                    (halo, 0, 8, 8), (near, 8, 32, 8), (far, 32, 56, 56), (halo, 56, 64, 56),
                ):
                    inside = (lane >= base + first) & (lane < base + last)
                    pair = jnp.where(inside, pltpu.roll(value, (base + by) % SIDE, 1), pair)
            tiles.append(pair)
        mended = filtered(jnp.concatenate(tiles, axis=1), taps, mend_tables, mend[0]["margin"])
        for begin, end, source, rows, shift in mend[2]:
            for span in range(begin, end):
                base = (span % 2) * (SIDE // 2)
                tile = slice((span // 2) * SIDE, (span // 2 + 1) * SIDE)
                target = slice(span * STEP + shift, span * STEP + shift + rows)
                for number in range(2):
                    value = mended[number][source : source + rows, tile]
                    for edge, by, good in ((0, -base - 8, lane < 8), (1, 72 - base, lane >= 120)):
                        columns[number, edge, target, :] = jnp.where(
                            good, pltpu.roll(value, by % SIDE, 1), columns[number, edge, target, :]
                        )

    lanes = pl.ds(SIDE, TX - 2 * SIDE) if mend else pl.ds(0, TX)

    def stores(unit, source, rows, target):
        return [
            pltpu.make_async_copy(
                scratch.at[unit, pl.ds(source, rows), lanes],
                hbm.at[pl.ds(target, rows), lanes],
                sems.at[unit, at],
            )
            for at, (scratch, hbm) in enumerate(zip(results, out_hbm))
        ]

    some = next(count for count in (4, 3, 2, 1) if spans % count == 0 and count * tall <= 320)

    @pl.loop(0, spans, step=some)
    def _(first):
        for ahead in range(some):
            unit = first + ahead
            detection[unit], variance[unit] = filtered(field[unit], taps, tables, fields["margin"])
        for ahead in range(some):
            unit = first + ahead
            for begin, end, source, rows, shift in outs:

                @pl.when((unit >= begin) & (unit < end))
                def _():
                    target = pl.multiple_of(unit * STEP + shift, HALO)
                    for store in stores(unit, source, rows, target):
                        store.start()
                    if mend:
                        for number in range(2):
                            for edge in range(2):
                                columns[number, edge, pl.ds(target, rows), :] = results[number][
                                    unit, source : source + rows, pl.ds(edge * (TX - SIDE), SIDE)
                                ]

    if mend:
        for copy in column_copies(out_hbm, True):
            copy.start()

    @pl.loop(0, spans)
    def _(unit):
        for begin, end, source, rows, shift in outs:

            @pl.when((unit >= begin) & (unit < end))
            def _():
                for store in stores(unit, source, rows, 0):
                    store.wait()

    if mend:
        for copy in column_copies(out_hbm, True):
            copy.wait()


def stage(plan, mine, taps, between, tables, chunks, lots, mend=None, mend_tables=(), held=()):
    fields = plan[0]
    spans, tall = fields["spans"], fields["tall"]
    shape = jax.ShapeDtypeStruct((TY, TX), jnp.float32)
    flat = [array for parts in chunks for part in parts for array in part]
    vmems = [*between, *tables, *mend_tables, *flat]
    out = pltpu.VMEM((spans, tall - 2 * fields["margin"], TX), jnp.float32)
    scratch = [pltpu.VMEM((spans, tall, WIDE), jnp.bfloat16), out, out, pltpu.SemaphoreType.DMA((spans, 2))]
    if mend:
        scratch += [
            pltpu.VMEM((mend[0]["spans"], mend[0]["tall"], 3 * SIDE), jnp.bfloat16),
            pltpu.VMEM((2, 2, TY, SIDE), jnp.float32),
            pltpu.SemaphoreType.DMA((2, 2)),
        ]
    if not fields["bare"]:
        scratch += [
            pltpu.VMEM((part[0].shape[0], SIDE), jnp.bfloat16) for parts in chunks for part in parts
        ]
    return pl.pallas_call(
        functools.partial(stage_kernel, plan, mend, lots),
        out_shape=(shape, shape),
        in_specs=[SMEM, SMEM] + [VMEM] * len(vmems) + [HBM] * len(held),
        out_specs=(HBM, HBM),
        input_output_aliases={2 + len(vmems) + at: at for at in range(len(held))},
        scratch_shapes=scratch,
        compiler_params=pltpu.CompilerParams(vmem_limit_bytes=56 * MIB),
        cost_estimate=pl.CostEstimate(
            flops=80 * spans * tall * WIDE, bytes_accessed=12 * spans * tall * WIDE, transcendentals=0
        ),
        name="stage",
    )(mine, taps, *vmems, *held)


def outer_plan(lot):
    fields = dict(
        visits=2, bare=True, spans=UNITS + 1, tall=2 * lot, margin=HALO, between=(lot - EDGE, lot),
        blank=[(0, 0, lot - EDGE), (UNITS, lot + EDGE, lot - EDGE)],
    )
    copies = [(0, 1, 0, lot, 0, 0, UNITS, 1), (0, 0, 0, lot, lot, 0, UNITS, 0)]
    rows = lot - HALO
    outs = [
        (0, 1, rows, rows, 0),
        (1, UNITS, 0, 2 * rows, -rows),
        (UNITS, UNITS + 1, 0, rows, -rows),
    ]
    return fields, copies, outs


def inner_plan(lot, inner):
    tall = 2 * inner + 2 * EDGE
    fields = dict(
        visits=2, bare=False, spans=UNITS, tall=tall, margin=HALO, between=None, blank=[]
    )
    copies = [
        (0, 0, lot - EDGE, EDGE, 0, 0, UNITS, 0),
        (1, 0, 0, inner, EDGE, 0, UNITS, 0),
        (1, 1, 0, inner, EDGE + inner, 0, UNITS, 0),
        (0, 1, 0, EDGE, EDGE + 2 * inner, 0, UNITS, 0),
    ]
    return fields, copies, [(0, UNITS, 0, tall - 2 * HALO, lot - HALO)]


def whole_plan(lot, visits):
    fields = dict(
        visits=visits, bare=False, spans=UNITS, tall=STEP + 2 * EDGE, margin=EDGE,
        between=(0, EDGE + STEP), blank=[],
    )
    copies = [(0, visit, 0, lot, EDGE + visit * lot, 0, UNITS, 0) for visit in range(visits)]
    copies.append((0, visits - 1, lot - EDGE, EDGE, 0, 0, UNITS - 1, 1))
    copies.append((0, 0, 0, EDGE, EDGE + STEP, 1, UNITS, -1))
    return fields, copies, [(0, UNITS, 0, STEP, 0)]


def per_device(
    images, inv_var, good_columns, warp_rows, warp_cols, block_visit, dest_tile, offsets, psf_taps
):
    tiles = lax.axis_size("py") * lax.axis_size("px")
    visits = lax.axis_size("visit")
    plan = shares(visits)
    lots = [rows for rows, _ in plan]
    mine = lax.axis_index("visit").astype(jnp.int32).reshape(1)

    def make(chunk, var):
        return warp(
            tiles, plan[chunk], chunk == 0, block_visit, dest_tile[:, 0], offsets.T,
            good_columns, warp_rows, warp_cols, var, images,
        )

    def send(blocks):
        return lax.all_to_all(blocks, EVERY, split_axis=0, concat_axis=0, tiled=True)

    made, psf_taps = lax.optimization_barrier((make(0, inv_var), psf_taps))
    arrived = send(made)
    if len(plan) == 1:
        every = whole_plan(lots[0], visits)
        coadd, strip, edge = place(codes(arrived), arrived, lots[0])
        all_of = [lax.all_gather(part, "visit") for part in (coadd, strip, edge)]
        between = neighbours(all_of[2][0, :HALO], all_of[2][visits - 1, HALO:], "py")
        sides = beyond([all_of[1][visit] for visit in range(visits)], *between)
        parts = [(all_of[0][visit], *sides) for visit in range(visits)]
        return stage(every, mine, psf_taps, between, bands(every, psf_taps), [parts], lots)

    outer, inner = outer_plan(lots[0]), inner_plan(*lots)
    tables, inv_var = lax.optimization_barrier(
        ([bands(part, psf_taps) for part in (outer, inner)], inv_var)
    )
    arrived, later = lax.optimization_barrier((arrived, make(1, inv_var)))
    second = send(later)
    code = codes(arrived)
    coadd, strip, edge = place(code, arrived, lots[0])
    other = swapped(coadd)
    between = rows_between(edge)
    sides = beyond([strip, swapped(strip)], *between)
    parts = [(coadd, *sides), (other, *sides)]
    held = stage(outer, mine, psf_taps, between, tables[0], [[(coadd,), (other,)]], lots[:1])
    second, held = lax.optimization_barrier((second, held))
    coadd, strip, _ = place(code, second, lots[1])
    own_sides, other_sides = straight_to_both(strip)
    more = [(coadd, *own_sides), (swapped(coadd), *other_sides)]
    return stage(
        inner, mine, psf_taps, between, tables[1], [parts, more], lots, outer, tables[0], held
    )


def codes(arrived):
    note = arrived[:, arrived.shape[1] - NOTE, :: SIDE // CAP]
    return note.astype(jnp.float32).astype(jnp.int32).reshape(-1)


def solution(mesh):
    in_specs = (
        P(EVERY, None, None),
        P(EVERY, None, None),
        P("visit", None),
        P("visit", None, None),
        P("visit", None, None),
        P(EVERY),
        P(EVERY, None),
        P(EVERY, None),
        P(),
    )
    out_specs = (P("py", "px"), P("py", "px"))
    return jax.shard_map(
        per_device, mesh=mesh, in_specs=in_specs, out_specs=out_specs, check_vma=False
    )
```

```python
import functools

import jax
import jax.numpy as jnp
from jax import lax
from jax.experimental import pallas as pl
from jax.experimental.pallas import tpu as pltpu
from jax.sharding import PartitionSpec as P

TY = 1024
TX = 1024
STEP = 128
CAP = 2
UNITS = TY // STEP
HALO = 8
EDGE = 16
SIDE = 128
WIDE = TX + SIDE
GROUP = 4
CUT = 6
NOTE = 16
MIB = 1 << 20
EVERY = ("visit", "py", "px")
HBM = pl.BlockSpec(memory_space=pltpu.HBM)
SMEM = pl.BlockSpec(memory_space=pltpu.SMEM)
VMEM = pl.BlockSpec(memory_space=pltpu.VMEM)


def shares(visits):
    if visits == 2:
        edge, inner = 48, 16
        return [(edge, (0, STEP - edge)), (inner, (edge, edge + inner))]
    rows = STEP // visits
    return [(rows, tuple(visit * rows for visit in range(visits)))]


def warp_kernel(
    tiles, share, noted, visit_ref, tile_ref, offset_ref, good_ref, rows_hbm, cols_hbm, var_hbm,
    image_hbm, out_hbm, rows, cols, var, image, done, note, count, table_sems, sems, out_sems,
):
    blocks, side, _ = var.shape
    some, firsts = share
    groups = blocks // GROUP
    slot_rows = done.shape[2]
    tables = [
        pltpu.make_async_copy(rows_hbm, rows, table_sems.at[0]),
        pltpu.make_async_copy(cols_hbm, cols, table_sems.at[1]),
    ]

    def loads(group):
        span = pl.ds(group * GROUP, GROUP)
        return (
            pltpu.make_async_copy(var_hbm.at[span], var.at[span], sems.at[group, 0]),
            pltpu.make_async_copy(image_hbm.at[span], image.at[span], sems.at[group, 1]),
        )

    for load in tables:
        load.start()
    for group in range(groups):
        for load in loads(group):
            load.start()

    @pl.loop(0, tiles)
    def _(tile):
        count[tile] = 0

    if noted:
        note[...] = jnp.full(note.shape, -1, jnp.bfloat16)
        slot_of_lane = lax.broadcasted_iota(jnp.int32, (NOTE, SIDE), 1) // (SIDE // CAP)

    for load in tables:
        load.wait()

    strips = [first + strip * STEP for first in firsts for strip in range(side // STEP)]
    tall = some * len(strips)
    part = tall // len(firsts)

    @pl.loop(0, groups)
    def _(group):
        for load in loads(group):
            load.wait()
        visits = [visit_ref[group * GROUP + ahead] for ahead in range(GROUP)]
        planes, turned, warped = [], [], []
        for ahead in range(GROUP):
            block = group * GROUP + ahead
            good = good_ref[pl.ds(visits[ahead], 1), :].astype(jnp.float32)
            weight = var[block].astype(jnp.float32) * good
            data = weight * image[block].astype(jnp.float32)
            planes.append(
                jnp.concatenate([data.astype(jnp.bfloat16), weight.astype(jnp.bfloat16)], axis=1)
            )
        for ahead in range(GROUP):
            matrix = jnp.concatenate(
                [rows[visits[ahead], first : first + some, :] for first in strips], axis=0
            )
            turned.append(
                jnp.dot(matrix, planes[ahead], preferred_element_type=jnp.float32).astype(jnp.bfloat16)
            )
        for ahead in range(GROUP):
            both = jnp.concatenate([turned[ahead][:, :side], turned[ahead][:, side:]], axis=0)
            warped.append(
                lax.dot_general(
                    both,
                    cols[visits[ahead]],
                    (((1,), (1,)), ((), ())),
                    preferred_element_type=jnp.float32,
                ).astype(jnp.bfloat16)
            )
        for ahead in range(GROUP):
            block = group * GROUP + ahead
            for visit in range(len(firsts)):
                for half in range(side // SIDE):
                    for plane in range(2):
                        start = plane * tall + visit * part
                        into = (2 * half + plane) * part
                        done[block, visit, into : into + part, :] = warped[ahead][
                            start : start + part, half * SIDE : (half + 1) * SIDE
                        ]
        for ahead in range(GROUP):
            block = group * GROUP + ahead
            tile = tile_ref[block]
            rank = count[tile]
            count[tile] = rank + 1
            for visit in range(len(firsts)):
                target = visit * tiles + tile
                pltpu.make_async_copy(
                    done.at[block, visit],
                    out_hbm.at[target, pl.ds(pl.multiple_of(rank * slot_rows, NOTE), slot_rows)],
                    out_sems.at[block, visit],
                ).start()
                if noted:
                    code = offset_ref[0, block] * 8 + offset_ref[1, block]
                    note[target] = jnp.where(
                        slot_of_lane == rank, code.astype(jnp.float32), note[target].astype(jnp.float32)
                    ).astype(jnp.bfloat16)

    if noted:
        notes = pltpu.make_async_copy(
            note, out_hbm.at[:, pl.ds(CAP * slot_rows, NOTE)], table_sems.at[0]
        )
        notes.start()

    @pl.loop(0, blocks)
    def _(block):
        for visit in range(len(firsts)):
            pltpu.make_async_copy(
                done.at[block, visit], out_hbm.at[0, pl.ds(0, slot_rows)], out_sems.at[block, visit]
            ).wait()

    if noted:
        notes.wait()


def warp(tiles, share, noted, visit, tile, offset, good, rows, cols, var, image):
    blocks, side, _ = var.shape
    some, firsts = share
    slot_rows = 2 * (side // STEP) * some * (side // SIDE)
    visits = len(firsts)
    return pl.pallas_call(
        functools.partial(warp_kernel, tiles, share, noted),
        out_shape=jax.ShapeDtypeStruct(
            (visits * tiles, CAP * slot_rows + noted * NOTE, SIDE), jnp.bfloat16
        ),
        in_specs=[SMEM, SMEM, SMEM, VMEM, HBM, HBM, HBM, HBM],
        out_specs=HBM,
        scratch_shapes=[
            pltpu.VMEM(rows.shape, jnp.bfloat16),
            pltpu.VMEM(cols.shape, jnp.bfloat16),
            pltpu.VMEM(var.shape, jnp.bfloat16),
            pltpu.VMEM(var.shape, jnp.bfloat16),
            pltpu.VMEM((blocks, visits, slot_rows, SIDE), jnp.bfloat16),
            pltpu.VMEM((visits * tiles, NOTE, SIDE), jnp.bfloat16),
            pltpu.SMEM((tiles,), jnp.int32),
            pltpu.SemaphoreType.DMA((2,)),
            pltpu.SemaphoreType.DMA((blocks // GROUP, 2)),
            pltpu.SemaphoreType.DMA((blocks, visits)),
        ],
        compiler_params=pltpu.CompilerParams(vmem_limit_bytes=60 * MIB),
        cost_estimate=pl.CostEstimate(
            flops=8 * blocks * side**3, bytes_accessed=8 * blocks * side**2, transcendentals=0
        ),
        name="warp",
    )(visit, tile, offset, good, rows, cols, var, image)


def place_kernel(part, pieces, code_ref, blocks_ref, *refs):
    coadd_refs, (strip_ref, edge_ref, data, weight) = refs[: len(pieces)], refs[len(pieces) :]
    step = pl.program_id(0)
    some = blocks_ref.shape[0]
    height = data.shape[0]
    lot = height // UNITS

    @pl.when(step == 0)
    def _():
        data[...] = jnp.zeros_like(data)
        weight[...] = jnp.zeros_like(weight)

    for block in range(some):
        for slot in range(CAP):
            code = code_ref[(step * some + block) * CAP + slot]

            @pl.when(code >= 0)
            def _():
                row = pl.multiple_of((code // 8) * lot, lot)
                for half in range(2):
                    col = pl.multiple_of((code % 8 + half) * STEP, STEP)
                    cells = (pl.ds(row, part), pl.ds(col, STEP))
                    first = (slot * 2 + half) * 2 * part
                    data[cells] += blocks_ref[block, first : first + part].astype(jnp.float32)
                    weight[cells] += blocks_ref[block, first + part : first + 2 * part].astype(
                        jnp.float32
                    )

    @pl.when(step == pl.num_programs(0) - 1)
    def _():
        coadd = data[...] / jnp.maximum(weight[...], 1.0)
        for (first, last), coadd_ref in zip(pieces, coadd_refs):
            coadd_ref[...] = coadd[first * lot : last * lot].astype(jnp.bfloat16)
        strip_ref[:HALO] = coadd[:, :SIDE].T[:HALO]
        strip_ref[HALO:] = coadd[:, TX - SIDE :].T[SIDE - HALO :]
        edge_ref[:HALO] = coadd[:HALO]
        edge_ref[HALO:] = coadd[height - HALO :]


def place(code, blocks, lot, pieces=((0, UNITS),)):
    count, tall, side = blocks.shape
    some = 4
    height = lot * UNITS
    shapes = [(((last - first) * lot, TX), jnp.bfloat16) for first, last in pieces] + [((2 * HALO, height), jnp.float32), ((2 * HALO, TX), jnp.float32)]
    return pl.pallas_call(
        functools.partial(place_kernel, 2 * lot, pieces),
        grid_spec=pltpu.PrefetchScalarGridSpec(
            num_scalar_prefetch=1,
            grid=(count // some,),
            in_specs=[pl.BlockSpec((some, tall, side), lambda step, code: (step, 0, 0))],
            out_specs=[pl.BlockSpec(shape, lambda step, code: (0, 0)) for shape, _ in shapes],
            scratch_shapes=[pltpu.VMEM((height, TX), jnp.float32)] * 2,
        ),
        out_shape=[jax.ShapeDtypeStruct(*shape) for shape in shapes],
        compiler_params=pltpu.CompilerParams(vmem_limit_bytes=32 * MIB),
        cost_estimate=pl.CostEstimate(
            flops=count * tall * side, bytes_accessed=count * tall * side * 2, transcendentals=0
        ),
        name="place",
    )(code, blocks)


def beside(axis):
    count = lax.axis_size(axis)
    up = [(i, i + 1) for i in range(count - 1)]
    return up, [(j, i) for i, j in up]


def neighbours(first, last, axis):
    up, down = beside(axis)
    return lax.ppermute(last, axis, up), lax.ppermute(first, axis, down)


def swapped(array):
    return lax.ppermute(array, "visit", [(0, 1), (1, 0)])


def beyond(strips, above, below):
    first = [strip[:HALO] for strip in strips] + [rows[:, :SIDE] for rows in (above, below)]
    last = [strip[HALO:] for strip in strips] + [rows[:, TX - SIDE :] for rows in (above, below)]
    return neighbours(jnp.concatenate(first, axis=1), jnp.concatenate(last, axis=1), "px")


def rows_between(edge):
    lower = lax.axis_index("visit") == 0
    mine = jnp.where(lower, edge[:HALO], edge[HALO:])
    count = lax.axis_size("py")
    up, down = beside("py")

    def pairs(cross):
        return [(i, j + cross * count) for i, j in down] + [
            (count + i, j + (1 - cross) * count) for i, j in up
        ]

    straight = lax.ppermute(mine, ("visit", "py"), pairs(0))
    crossed = lax.ppermute(mine, ("visit", "py"), pairs(1))
    return jnp.where(lower, crossed, straight), jnp.where(lower, straight, crossed)


def bands(plan, taps):
    tall, margin = plan[0]["tall"], plan[0]["margin"]
    row = jnp.arange(tall, dtype=jnp.int32)
    out = jnp.arange(tall - 2 * margin, dtype=jnp.int32) + margin
    three = (jnp.abs(row[:, None] - row[None, :]) <= 1).astype(jnp.bfloat16)
    nine = (jnp.abs(out[:, None] - row[None, :]) <= 4).astype(jnp.bfloat16)
    count = taps.shape[0]
    ahead = row[None, :] - out[:, None] + count // 2
    coarse, fine = split(sum(jnp.where(ahead == tap, taps[tap], 0.0) for tap in range(count)))
    lane = jnp.arange(4 * SIDE, dtype=jnp.int32)
    across = jnp.abs(lane[:, None] - lane[None, SIDE : 3 * SIDE]) <= 4
    return (
        jnp.concatenate([three] * 2, axis=1),
        jnp.concatenate([nine] * 2, axis=1),
        jnp.concatenate([coarse, coarse, fine], axis=1),
        across.astype(jnp.bfloat16),
    )


def split(value):
    coarse = value.astype(jnp.bfloat16)
    return coarse, (value - coarse.astype(jnp.float32)).astype(jnp.bfloat16)


def filtered(value, taps, tables, margin):
    three, nine, blur, across = [table[...] for table in tables]
    tall = value.shape[0]
    short = tall - 2 * margin

    def product(matrix, terms):
        return jnp.dot(matrix, jnp.concatenate(terms, axis=0), preferred_element_type=jnp.float32)

    moved = {
        by: (pltpu.roll(value, -by % WIDE, 1) if by else value).astype(jnp.float32)
        for by in range(-3, 4)
    }
    rowwise = sum(taps[tap] * moved[tap - 3] for tap in range(7))[:, :TX]
    resid = moved[0] - product(three, split(moved[-1] + moved[0] + moved[1])) * (1.0 / 9.0)
    tower = jnp.concatenate(split(product(nine, split(resid * resid))), axis=0)
    windows = [jnp.concatenate([tower[:, TX:], tower[:, : 3 * SIDE]], axis=1)]
    for start in range(2 * SIDE, TX, 2 * SIDE):
        windows.append(tower[:, start - SIDE : start + 3 * SIDE])
    boxes = jnp.dot(jnp.concatenate(windows, axis=0), across, preferred_element_type=jnp.float32)
    box = jnp.concatenate(
        [
            boxes[2 * at * short : (2 * at + 1) * short] + boxes[(2 * at + 1) * short : (2 * at + 2) * short]
            for at in range(len(windows))
        ],
        axis=1,
    )
    local = box * (1.0 / 81.0) + 1e-05
    coarse, fine = split(rowwise)
    return product(blur, (coarse, fine, coarse)) * lax.rsqrt(local), local


def stage_kernel(plan, mend, chunks, heights, *refs):
    mine_ref, taps_ref, above_ref, below_ref = refs[:4]
    fields, copies, outs = plan
    visits = fields["visits"]
    bare = not heights
    tables, at = refs[4:8], 8
    if mend:
        mend_tables, at = refs[8:12], 12
    if not bare:
        left, right = refs[at : at + 2]
        at += 2
    cells_of = [refs[at + visits * chunk : at + visits * (chunk + 1)] for chunk in range(len(chunks))]
    at += visits * len(chunks) + fields["held"]
    held_hbm = refs[at - 2 : at] if mend else ()
    out_hbm = refs[at : at + 2]
    field, detection, variance, sems = refs[at + 2 : at + 6]
    at += 6
    if mend:
        rim, columns, column_sems = refs[at : at + 3]
        at += 3
    sides = refs[at:]
    results = (detection, variance)
    spans, tall, _ = field.shape

    def column_copies(hbm, back):
        found = []
        for number, ref in enumerate(hbm):
            for edge in range(2):
                far = ref.at[:, pl.ds(edge * (TX - SIDE), SIDE)]
                near = columns.at[number, edge]
                source, target = (near, far) if back else (far, near)
                found.append(pltpu.make_async_copy(source, target, column_sems.at[number, edge]))
        return found

    if mend:
        for copy in column_copies(held_hbm, False):
            copy.start()

    first = 0
    for lot, height in enumerate(heights):
        for visit in range(visits):
            here = slice(first, first + height)
            first += height
            gap = jnp.zeros((SIDE - 2 * HALO, height), jnp.float32)
            sides[lot * visits + visit][...] = jnp.concatenate(
                [right[:, here], gap, left[:, here]], axis=0
            ).T.astype(jnp.bfloat16)
    corners = first

    def whole_rows(span, into, cells, rows, side, side_rows):
        field[span, into, :TX] = cells[rows, :]
        if not bare:
            field[span, into, TX:] = side[side_rows, :]

    def rim_rows(span, into, cells, rows, side, side_rows):
        rim[span, into, :SIDE] = cells[rows, :SIDE]
        rim[span, into, SIDE : 2 * SIDE] = cells[rows, TX - SIDE :]
        rim[span, into, 2 * SIDE :] = side[side_rows, :]

    def assemble(order, copies, put):
        for chunk, visit, first, rows, at_row, begin, end, shift in copies:
            tall_of, base, lot = chunks[chunk]
            cells = cells_of[chunk][order[visit]]
            side = None if bare else sides[lot * visits + order[visit]]

            @pl.loop(begin, end)
            def _(unit):
                start = pl.multiple_of((unit - base) * tall_of + first, EDGE)
                beside = pl.multiple_of(unit * tall_of + first, EDGE)
                put(
                    unit + shift, pl.ds(at_row, rows), cells, pl.ds(start, rows), side,
                    pl.ds(beside, rows),
                )

    def assemble_all(order):
        assemble(order, copies, whole_rows)
        if mend:
            assemble(order, mend[1], rim_rows)

    if bare:
        field[:, :, TX:] = jnp.zeros((spans, tall, SIDE), jnp.bfloat16)
    for span, first, rows in fields["blank"]:
        field[span, first : first + rows, :] = jnp.zeros((rows, WIDE), jnp.bfloat16)
    if mend:
        for span, first, rows in mend[0]["blank"]:
            rim[span, first : first + rows, :] = jnp.zeros((rows, 3 * SIDE), jnp.bfloat16)
    if visits == 2:
        for flip in range(2):

            @pl.when(mine_ref[0] == flip)
            def _():
                assemble_all((0, 1) if flip == 0 else (1, 0))

    else:
        assemble_all(tuple(range(visits)))

    between = (mend or plan)[0]["between"]
    if between:
        from_left = lax.broadcasted_iota(jnp.int32, (HALO, SIDE), 1) >= SIDE // 2
        for number, rows in enumerate((above_ref, below_ref)):
            if between[number] is None:
                continue
            corner = jnp.zeros((HALO, SIDE), jnp.float32)
            if not bare:
                here = slice(corners + number * SIDE, corners + (number + 1) * SIDE)
                corner = jnp.where(from_left, left[:, here], right[:, here])
            if mend:
                wide = jnp.concatenate([rows[:, :SIDE], rows[:, TX - SIDE :], corner], axis=1)
            else:
                wide = jnp.concatenate([rows[...], corner], axis=1)
            strip = [jnp.zeros_like(wide), wide] if number == 0 else [wide, jnp.zeros_like(wide)]
            strip = jnp.concatenate(strip, axis=0).astype(jnp.bfloat16)
            into = slice(between[number], between[number] + EDGE)
            if mend:
                rim[number * (rim.shape[0] - 1), into, :] = strip
            else:
                field[number * (spans - 1), into, :] = strip

    taps = [taps_ref[tap] for tap in range(7)]
    lane = lax.broadcasted_iota(jnp.int32, (1, SIDE), 1)

    if mend:
        for copy in column_copies(held_hbm, False):
            copy.wait()
        count = rim.shape[0]
        tiles = []
        for tile in range(WIDE // SIDE):
            pair = jnp.zeros(rim.shape[1:2] + (SIDE,), jnp.bfloat16)
            for span in range(2 * tile, min(2 * tile + 2, count)):
                base = (span % 2) * (SIDE // 2)
                near, far, halo = (rim[span, :, at * SIDE : (at + 1) * SIDE] for at in range(3))
                for value, first, last, by in (
                    (halo, 0, 8, 8), (near, 8, 32, 8), (far, 32, 56, 56), (halo, 56, 64, 56),
                ):
                    inside = (lane >= base + first) & (lane < base + last)
                    pair = jnp.where(inside, pltpu.roll(value, (base + by) % SIDE, 1), pair)
            tiles.append(pair)
        mended = filtered(jnp.concatenate(tiles, axis=1), taps, mend_tables, mend[0]["margin"])
        for begin, end, source, rows, shift in mend[2]:
            for span in range(begin, end):
                base = (span % 2) * (SIDE // 2)
                tile = slice((span // 2) * SIDE, (span // 2 + 1) * SIDE)
                target = slice(span * STEP + shift, span * STEP + shift + rows)
                for number in range(2):
                    value = mended[number][source : source + rows, tile]
                    for edge, by, good in ((0, -base - 8, lane < 8), (1, 72 - base, lane >= 120)):
                        columns[number, edge, target, :] = jnp.where(
                            good, pltpu.roll(value, by % SIDE, 1), columns[number, edge, target, :]
                        )

    lanes = pl.ds(SIDE, TX - 2 * SIDE) if mend else pl.ds(0, TX)

    def stores(unit, source, rows, target):
        return [
            pltpu.make_async_copy(
                scratch.at[unit, pl.ds(source, rows), lanes],
                hbm.at[pl.ds(target, rows), lanes],
                sems.at[unit, at],
            )
            for at, (scratch, hbm) in enumerate(zip(results, out_hbm))
        ]

    some = next(count for count in (4, 3, 2, 1) if spans % count == 0 and count * tall <= 320)

    @pl.loop(0, spans, step=some)
    def _(first):
        for ahead in range(some):
            unit = first + ahead
            detection[unit], variance[unit] = filtered(field[unit], taps, tables, fields["margin"])
        for ahead in range(some):
            unit = first + ahead
            for begin, end, source, rows, shift in outs:

                @pl.when((unit >= begin) & (unit < end))
                def _():
                    target = pl.multiple_of(unit * STEP + shift, HALO)
                    for store in stores(unit, source, rows, target):
                        store.start()
                    if mend:
                        for number in range(2):
                            for edge in range(2):
                                columns[number, edge, pl.ds(target, rows), :] = results[number][
                                    unit, source : source + rows, pl.ds(edge * (TX - SIDE), SIDE)
                                ]

    if mend:
        for copy in column_copies(out_hbm, True):
            copy.start()

    @pl.loop(0, spans)
    def _(unit):
        for begin, end, source, rows, shift in outs:

            @pl.when((unit >= begin) & (unit < end))
            def _():
                for store in stores(unit, source, rows, 0):
                    store.wait()

    if mend:
        for copy in column_copies(out_hbm, True):
            copy.wait()


def stage(plan, mine, taps, between, tables, chunks, cells, beside=(), heights=(), mend=None, mend_tables=(), held=()):
    fields = plan[0]
    spans, tall = fields["spans"], fields["tall"]
    shape = jax.ShapeDtypeStruct((TY, TX), jnp.float32)
    vmems = [*between, *tables, *mend_tables, *beside, *[array for parts in cells for array in parts]]
    out = pltpu.VMEM((spans, tall - 2 * fields["margin"], TX), jnp.float32)
    scratch = [pltpu.VMEM((spans, tall, WIDE), jnp.bfloat16), out, out, pltpu.SemaphoreType.DMA((spans, 2))]
    if mend:
        scratch += [
            pltpu.VMEM((mend[0]["spans"], mend[0]["tall"], 3 * SIDE), jnp.bfloat16),
            pltpu.VMEM((2, 2, TY, SIDE), jnp.float32),
            pltpu.SemaphoreType.DMA((2, 2)),
        ]
    for height in heights:
        scratch += [pltpu.VMEM((height, SIDE), jnp.bfloat16)] * fields["visits"]
    return pl.pallas_call(
        functools.partial(stage_kernel, plan, mend, chunks, heights),
        out_shape=(shape, shape),
        in_specs=[SMEM, SMEM] + [VMEM] * len(vmems) + [HBM] * len(held),
        out_specs=(HBM, HBM),
        input_output_aliases={2 + len(vmems) + at: at for at in range(len(held))},
        scratch_shapes=scratch,
        compiler_params=pltpu.CompilerParams(vmem_limit_bytes=56 * MIB),
        cost_estimate=pl.CostEstimate(
            flops=80 * spans * tall * WIDE, bytes_accessed=12 * spans * tall * WIDE, transcendentals=0
        ),
        name="stage",
    )(mine, taps, *vmems, *held)


def outer_plan(lot, begin, end, pieces):
    fields = dict(
        visits=2, spans=end - begin, tall=2 * lot, margin=HALO, held=0 if begin == 0 else 2,
        between=(lot - EDGE if begin == 0 else None, lot if end == UNITS + 1 else None),
        blank=([(0, 0, lot - EDGE)] if begin == 0 else [])
        + ([(end - begin - 1, lot + EDGE, lot - EDGE)] if end == UNITS + 1 else []),
    )
    copies = []
    for chunk, first, last in pieces:
        copies.append((chunk, 1, 0, lot, 0, max(first, begin - 1), min(last, end - 1), 1 - begin))
        copies.append((chunk, 0, 0, lot, lot, max(first, begin), min(last, end), -begin))
    rows = lot - HALO
    outs = []
    if begin == 0:
        outs.append((0, 1, rows, rows, 0))
    outs.append((max(begin, 1) - begin, min(end, UNITS) - begin, 0, 2 * rows, begin * STEP - rows))
    if end == UNITS + 1:
        outs.append((UNITS - begin, end - begin, 0, rows, begin * STEP - rows))
    return fields, [copy for copy in copies if copy[5] < copy[6]], outs


def inner_plan(lot, inner, pieces):
    tall = 2 * inner + 2 * EDGE
    fields = dict(visits=2, spans=UNITS, tall=tall, margin=HALO, between=None, blank=[], held=2)
    copies = [
        (len(pieces), 0, 0, inner, EDGE, 0, UNITS, 0),
        (len(pieces), 1, 0, inner, EDGE + inner, 0, UNITS, 0),
    ]
    for chunk, first, last in pieces:
        copies.append((chunk, 0, lot - EDGE, EDGE, 0, first, last, 0))
        copies.append((chunk, 1, 0, EDGE, EDGE + 2 * inner, first, last, 0))
    return fields, copies, [(0, UNITS, 0, tall - 2 * HALO, lot - HALO)]


def whole_plan(lot, visits):
    fields = dict(
        visits=visits, spans=UNITS, tall=STEP + 2 * EDGE, margin=EDGE, held=0,
        between=(0, EDGE + STEP), blank=[],
    )
    copies = [(0, visit, 0, lot, EDGE + visit * lot, 0, UNITS, 0) for visit in range(visits)]
    copies.append((0, visits - 1, lot - EDGE, EDGE, 0, 0, UNITS - 1, 1))
    copies.append((0, 0, 0, EDGE, EDGE + STEP, 1, UNITS, -1))
    return fields, copies, [(0, UNITS, 0, STEP, 0)]


def per_device(
    images, inv_var, good_columns, warp_rows, warp_cols, block_visit, dest_tile, offsets, psf_taps
):
    tiles = lax.axis_size("py") * lax.axis_size("px")
    visits = lax.axis_size("visit")
    plan = shares(visits)
    lots = [rows for rows, _ in plan]
    mine = lax.axis_index("visit").astype(jnp.int32).reshape(1)

    def make(chunk, var):
        return warp(
            tiles, plan[chunk], chunk == 0, block_visit, dest_tile[:, 0], offsets.T,
            good_columns, warp_rows, warp_cols, var, images,
        )

    def send(blocks):
        return lax.all_to_all(blocks, EVERY, split_axis=0, concat_axis=0, tiled=True)

    made, psf_taps = lax.optimization_barrier((make(0, inv_var), psf_taps))
    arrived = send(made)
    if len(plan) == 1:
        every = whole_plan(lots[0], visits)
        coadd, strip, edge = place(codes(arrived), arrived, lots[0])
        all_of = [lax.all_gather(part, "visit") for part in (coadd, strip, edge)]
        between = neighbours(all_of[2][0, :HALO], all_of[2][visits - 1, HALO:], "py")
        sides = beyond([all_of[1][visit] for visit in range(visits)], *between)
        cells = [all_of[0][visit] for visit in range(visits)]
        height = lots[0] * UNITS
        return stage(
            every, mine, psf_taps, between, bands(every, psf_taps), [(lots[0], 0, 0)], [cells], sides, [height]
        )

    lot, inner_lot = lots
    ranges = [(0, CUT), (CUT - 1, UNITS)]
    first_part = outer_plan(lot, 0, CUT, [(0, 0, CUT)])
    second_part = outer_plan(lot, CUT, UNITS + 1, [(0, CUT - 1, UNITS)])
    pieces = [(0, 0, CUT), (1, CUT, UNITS)]
    outer, inner = outer_plan(lot, 0, UNITS + 1, pieces), inner_plan(lot, inner_lot, pieces)
    tables, inv_var = lax.optimization_barrier(
        ([bands(part, psf_taps) for part in (outer, inner)], inv_var)
    )
    arrived, later = lax.optimization_barrier((arrived, make(1, inv_var)))
    second = send(later)
    code = codes(arrived)
    *cells, strip, edge = place(code, arrived, lot, ranges)
    cells = [(piece, swapped(piece)) for piece in cells]
    strips = [strip, swapped(strip)]
    between = rows_between(edge)
    held = stage(first_part, mine, psf_taps, between, tables[0], [(lot, 0, 0)], cells[:1])
    held = stage(
        second_part, mine, psf_taps, between, tables[0], [(lot, CUT - 1, 0)], cells[1:], held=held
    )
    second, held = lax.optimization_barrier((second, held))
    coadd, strip, _ = place(code, second, inner_lot)
    sides = beyond([*strips, strip, swapped(strip)], *between)
    return stage(
        inner, mine, psf_taps, between, tables[1], [(lot, 0, 0), (lot, CUT - 1, 0), (inner_lot, 0, 1)],
        [*cells, (coadd, swapped(coadd))], sides, [lot * UNITS, inner_lot * UNITS], outer, tables[0], held,
    )


def codes(arrived):
    note = arrived[:, arrived.shape[1] - NOTE, :: SIDE // CAP]
    return note.astype(jnp.float32).astype(jnp.int32).reshape(-1)


def solution(mesh):
    in_specs = (
        P(EVERY, None, None),
        P(EVERY, None, None),
        P("visit", None),
        P("visit", None, None),
        P("visit", None, None),
        P(EVERY),
        P(EVERY, None),
        P(EVERY, None),
        P(),
    )
    out_specs = (P("py", "px"), P("py", "px"))
    return jax.shard_map(
        per_device, mesh=mesh, in_specs=in_specs, out_specs=out_specs, check_vma=False
    )
```

```python
import functools

import jax
import jax.numpy as jnp
from jax import lax
from jax.experimental import pallas as pl
from jax.experimental.pallas import tpu as pltpu
from jax.sharding import PartitionSpec as P

TY = 1024
TX = 1024
STEP = 128
CAP = 2
UNITS = TY // STEP
HALO = 8
EDGE = 16
SIDE = 128
WIDE = TX + SIDE
GROUP = 4
CUT = 6
NOTE = 16
MIB = 1 << 20
EVERY = ("visit", "py", "px")
HBM = pl.BlockSpec(memory_space=pltpu.HBM)
SMEM = pl.BlockSpec(memory_space=pltpu.SMEM)
VMEM = pl.BlockSpec(memory_space=pltpu.VMEM)


def shares(visits):
    if visits == 2:
        edge, inner = 48, 16
        return [(edge, (0, STEP - edge)), (inner, (edge, edge + inner))]
    rows = STEP // visits
    return [(rows, tuple(visit * rows for visit in range(visits)))]


def warp_kernel(
    tiles, share, noted, visit_ref, tile_ref, offset_ref, good_ref, rows_hbm, cols_hbm, var_hbm,
    image_hbm, out_hbm, rows, cols, var, image, done, note, count, table_sems, sems, out_sems,
):
    blocks, side, _ = var.shape
    some, firsts = share
    groups = blocks // GROUP
    slot_rows = done.shape[2]
    tables = [
        pltpu.make_async_copy(rows_hbm, rows, table_sems.at[0]),
        pltpu.make_async_copy(cols_hbm, cols, table_sems.at[1]),
    ]

    def loads(group):
        span = pl.ds(group * GROUP, GROUP)
        return (
            pltpu.make_async_copy(var_hbm.at[span], var.at[span], sems.at[group, 0]),
            pltpu.make_async_copy(image_hbm.at[span], image.at[span], sems.at[group, 1]),
        )

    for load in tables:
        load.start()
    for group in range(groups):
        for load in loads(group):
            load.start()

    @pl.loop(0, tiles)
    def _(tile):
        count[tile] = 0

    if noted:
        note[...] = jnp.full(note.shape, -1, jnp.bfloat16)
        slot_of_lane = lax.broadcasted_iota(jnp.int32, (NOTE, SIDE), 1) // (SIDE // CAP)

    for load in tables:
        load.wait()

    strips = [first + strip * STEP for first in firsts for strip in range(side // STEP)]
    tall = some * len(strips)
    part = tall // len(firsts)

    @pl.loop(0, groups)
    def _(group):
        for load in loads(group):
            load.wait()
        visits = [visit_ref[group * GROUP + ahead] for ahead in range(GROUP)]
        planes, turned, warped = [], [], []
        for ahead in range(GROUP):
            block = group * GROUP + ahead
            good = good_ref[pl.ds(visits[ahead], 1), :].astype(jnp.float32)
            weight = var[block].astype(jnp.float32) * good
            data = weight * image[block].astype(jnp.float32)
            planes.append(
                jnp.concatenate([data.astype(jnp.bfloat16), weight.astype(jnp.bfloat16)], axis=1)
            )
        for ahead in range(GROUP):
            matrix = jnp.concatenate(
                [rows[visits[ahead], first : first + some, :] for first in strips], axis=0
            )
            turned.append(
                jnp.dot(matrix, planes[ahead], preferred_element_type=jnp.float32).astype(jnp.bfloat16)
            )
        for ahead in range(GROUP):
            both = jnp.concatenate([turned[ahead][:, :side], turned[ahead][:, side:]], axis=0)
            warped.append(
                lax.dot_general(
                    both,
                    cols[visits[ahead]],
                    (((1,), (1,)), ((), ())),
                    preferred_element_type=jnp.float32,
                ).astype(jnp.bfloat16)
            )
        for ahead in range(GROUP):
            block = group * GROUP + ahead
            for visit in range(len(firsts)):
                for half in range(side // SIDE):
                    for plane in range(2):
                        start = plane * tall + visit * part
                        into = (2 * half + plane) * part
                        done[block, visit, into : into + part, :] = warped[ahead][
                            start : start + part, half * SIDE : (half + 1) * SIDE
                        ]
        for ahead in range(GROUP):
            block = group * GROUP + ahead
            tile = tile_ref[block]
            rank = count[tile]
            count[tile] = rank + 1
            for visit in range(len(firsts)):
                target = visit * tiles + tile
                pltpu.make_async_copy(
                    done.at[block, visit],
                    out_hbm.at[target, pl.ds(pl.multiple_of(rank * slot_rows, NOTE), slot_rows)],
                    out_sems.at[block, visit],
                ).start()
                if noted:
                    code = offset_ref[0, block] * 8 + offset_ref[1, block]
                    note[target] = jnp.where(
                        slot_of_lane == rank, code.astype(jnp.float32), note[target].astype(jnp.float32)
                    ).astype(jnp.bfloat16)

    if noted:
        notes = pltpu.make_async_copy(
            note, out_hbm.at[:, pl.ds(CAP * slot_rows, NOTE)], table_sems.at[0]
        )
        notes.start()

    @pl.loop(0, blocks)
    def _(block):
        for visit in range(len(firsts)):
            pltpu.make_async_copy(
                done.at[block, visit], out_hbm.at[0, pl.ds(0, slot_rows)], out_sems.at[block, visit]
            ).wait()

    if noted:
        notes.wait()


def warp(tiles, share, noted, visit, tile, offset, good, rows, cols, var, image):
    blocks, side, _ = var.shape
    some, firsts = share
    slot_rows = 2 * (side // STEP) * some * (side // SIDE)
    visits = len(firsts)
    return pl.pallas_call(
        functools.partial(warp_kernel, tiles, share, noted),
        out_shape=jax.ShapeDtypeStruct(
            (visits * tiles, CAP * slot_rows + noted * NOTE, SIDE), jnp.bfloat16
        ),
        in_specs=[SMEM, SMEM, SMEM, VMEM, HBM, HBM, HBM, HBM],
        out_specs=HBM,
        scratch_shapes=[
            pltpu.VMEM(rows.shape, jnp.bfloat16),
            pltpu.VMEM(cols.shape, jnp.bfloat16),
            pltpu.VMEM(var.shape, jnp.bfloat16),
            pltpu.VMEM(var.shape, jnp.bfloat16),
            pltpu.VMEM((blocks, visits, slot_rows, SIDE), jnp.bfloat16),
            pltpu.VMEM((visits * tiles, NOTE, SIDE), jnp.bfloat16),
            pltpu.SMEM((tiles,), jnp.int32),
            pltpu.SemaphoreType.DMA((2,)),
            pltpu.SemaphoreType.DMA((blocks // GROUP, 2)),
            pltpu.SemaphoreType.DMA((blocks, visits)),
        ],
        compiler_params=pltpu.CompilerParams(vmem_limit_bytes=60 * MIB),
        cost_estimate=pl.CostEstimate(
            flops=8 * blocks * side**3, bytes_accessed=8 * blocks * side**2, transcendentals=0
        ),
        name="warp",
    )(visit, tile, offset, good, rows, cols, var, image)


def place_kernel(part, pieces, code_ref, blocks_ref, *refs):
    coadd_refs, (strip_ref, edge_ref, data, weight) = refs[: len(pieces)], refs[len(pieces) :]
    step = pl.program_id(0)
    some = blocks_ref.shape[0]
    height = data.shape[0]
    lot = height // UNITS

    @pl.when(step == 0)
    def _():
        data[...] = jnp.zeros_like(data)
        weight[...] = jnp.zeros_like(weight)

    for block in range(some):
        for slot in range(CAP):
            code = code_ref[(step * some + block) * CAP + slot]

            @pl.when(code >= 0)
            def _():
                row = pl.multiple_of((code // 8) * lot, lot)
                for half in range(2):
                    col = pl.multiple_of((code % 8 + half) * STEP, STEP)
                    cells = (pl.ds(row, part), pl.ds(col, STEP))
                    first = (slot * 2 + half) * 2 * part
                    data[cells] += blocks_ref[block, first : first + part].astype(jnp.float32)
                    weight[cells] += blocks_ref[block, first + part : first + 2 * part].astype(
                        jnp.float32
                    )

    @pl.when(step == pl.num_programs(0) - 1)
    def _():
        coadd = data[...] / jnp.maximum(weight[...], 1.0)
        for (first, last), coadd_ref in zip(pieces, coadd_refs):
            coadd_ref[...] = coadd[first * lot : last * lot].astype(jnp.bfloat16)
        strip_ref[:HALO] = coadd[:, :SIDE].T[:HALO]
        strip_ref[HALO:] = coadd[:, TX - SIDE :].T[SIDE - HALO :]
        edge_ref[:HALO] = coadd[:HALO]
        edge_ref[HALO:] = coadd[height - HALO :]


def place(code, blocks, lot, pieces=((0, UNITS),)):
    count, tall, side = blocks.shape
    some = 4
    height = lot * UNITS
    shapes = [(((last - first) * lot, TX), jnp.bfloat16) for first, last in pieces] + [((2 * HALO, height), jnp.float32), ((2 * HALO, TX), jnp.float32)]
    return pl.pallas_call(
        functools.partial(place_kernel, 2 * lot, pieces),
        grid_spec=pltpu.PrefetchScalarGridSpec(
            num_scalar_prefetch=1,
            grid=(count // some,),
            in_specs=[pl.BlockSpec((some, tall, side), lambda step, code: (step, 0, 0))],
            out_specs=[pl.BlockSpec(shape, lambda step, code: (0, 0)) for shape, _ in shapes],
            scratch_shapes=[pltpu.VMEM((height, TX), jnp.float32)] * 2,
        ),
        out_shape=[jax.ShapeDtypeStruct(*shape) for shape in shapes],
        compiler_params=pltpu.CompilerParams(vmem_limit_bytes=32 * MIB),
        cost_estimate=pl.CostEstimate(
            flops=count * tall * side, bytes_accessed=count * tall * side * 2, transcendentals=0
        ),
        name="place",
    )(code, blocks)


def beside(axis):
    count = lax.axis_size(axis)
    up = [(i, i + 1) for i in range(count - 1)]
    return up, [(j, i) for i, j in up]


def neighbours(first, last, axis):
    up, down = beside(axis)
    return lax.ppermute(last, axis, up), lax.ppermute(first, axis, down)


def swapped(array):
    return lax.ppermute(array, "visit", [(0, 1), (1, 0)])


def beyond(strips, above, below):
    first = [strip[:HALO] for strip in strips] + [rows[:, :SIDE] for rows in (above, below)]
    last = [strip[HALO:] for strip in strips] + [rows[:, TX - SIDE :] for rows in (above, below)]
    return neighbours(jnp.concatenate(first, axis=1), jnp.concatenate(last, axis=1), "px")


def rows_between(edge):
    lower = lax.axis_index("visit") == 0
    mine = jnp.where(lower, edge[:HALO], edge[HALO:])
    count = lax.axis_size("py")
    up, down = beside("py")

    def pairs(cross):
        return [(i, j + cross * count) for i, j in down] + [
            (count + i, j + (1 - cross) * count) for i, j in up
        ]

    straight = lax.ppermute(mine, ("visit", "py"), pairs(0))
    crossed = lax.ppermute(mine, ("visit", "py"), pairs(1))
    return jnp.where(lower, crossed, straight), jnp.where(lower, straight, crossed)


def bands(plan, taps):
    tall, margin = plan[0]["tall"], plan[0]["margin"]
    row = jnp.arange(tall, dtype=jnp.int32)
    out = jnp.arange(tall - 2 * margin, dtype=jnp.int32) + margin
    three = (jnp.abs(row[:, None] - row[None, :]) <= 1).astype(jnp.bfloat16)
    nine = (jnp.abs(out[:, None] - row[None, :]) <= 4).astype(jnp.bfloat16)
    count = taps.shape[0]
    ahead = row[None, :] - out[:, None] + count // 2
    coarse, fine = split(sum(jnp.where(ahead == tap, taps[tap], 0.0) for tap in range(count)))
    lane = jnp.arange(4 * SIDE, dtype=jnp.int32)
    across = jnp.abs(lane[:, None] - lane[None, SIDE : 3 * SIDE]) <= 4
    return (
        jnp.concatenate([three] * 2, axis=1),
        jnp.concatenate([nine] * 2, axis=1),
        jnp.concatenate([coarse, coarse, fine], axis=1),
        across.astype(jnp.bfloat16),
    )


def split(value):
    coarse = value.astype(jnp.bfloat16)
    return coarse, (value - coarse.astype(jnp.float32)).astype(jnp.bfloat16)


def filtered(value, taps, tables, margin):
    three, nine, blur, across = [table[...] for table in tables]
    tall = value.shape[0]
    short = tall - 2 * margin

    def product(matrix, terms):
        return jnp.dot(matrix, jnp.concatenate(terms, axis=0), preferred_element_type=jnp.float32)

    moved = {
        by: (pltpu.roll(value, -by % WIDE, 1) if by else value).astype(jnp.float32)
        for by in range(-3, 4)
    }
    rowwise = sum(taps[tap] * moved[tap - 3] for tap in range(7))[:, :TX]
    resid = moved[0] - product(three, split(moved[-1] + moved[0] + moved[1])) * (1.0 / 9.0)
    tower = jnp.concatenate(split(product(nine, split(resid * resid))), axis=0)
    windows = [jnp.concatenate([tower[:, TX:], tower[:, : 3 * SIDE]], axis=1)]
    for start in range(2 * SIDE, TX, 2 * SIDE):
        windows.append(tower[:, start - SIDE : start + 3 * SIDE])
    boxes = jnp.dot(jnp.concatenate(windows, axis=0), across, preferred_element_type=jnp.float32)
    box = jnp.concatenate(
        [
            boxes[2 * at * short : (2 * at + 1) * short] + boxes[(2 * at + 1) * short : (2 * at + 2) * short]
            for at in range(len(windows))
        ],
        axis=1,
    )
    local = box * (1.0 / 81.0) + 1e-05
    coarse, fine = split(rowwise)
    return product(blur, (coarse, fine, coarse)) * lax.rsqrt(local), local


def stage_kernel(plan, mend, chunks, heights, *refs):
    mine_ref, taps_ref, above_ref, below_ref = refs[:4]
    fields, copies, outs = plan
    visits = fields["visits"]
    bare = not heights
    tables, at = refs[4:8], 8
    if mend:
        mend_tables, at = refs[8:12], 12
    if not bare:
        left, right = refs[at : at + 2]
        at += 2
    cells_of = [refs[at + visits * chunk : at + visits * (chunk + 1)] for chunk in range(len(chunks))]
    at += visits * len(chunks) + fields["held"]
    held_hbm = refs[at - 2 : at] if mend else ()
    out_hbm = refs[at : at + 2]
    field, detection, variance, sems = refs[at + 2 : at + 6]
    at += 6
    if mend:
        rim, columns, column_sems = refs[at : at + 3]
        at += 3
    sides = refs[at:]
    results = (detection, variance)
    spans, tall, _ = field.shape

    def column_copies(hbm, back):
        found = []
        for number, ref in enumerate(hbm):
            for edge in range(2):
                far = ref.at[:, pl.ds(edge * (TX - SIDE), SIDE)]
                near = columns.at[number, edge]
                source, target = (near, far) if back else (far, near)
                found.append(pltpu.make_async_copy(source, target, column_sems.at[number, edge]))
        return found

    if mend:
        for copy in column_copies(held_hbm, False):
            copy.start()

    first = 0
    for lot, height in enumerate(heights):
        for visit in range(visits):
            here = slice(first, first + height)
            first += height
            gap = jnp.zeros((SIDE - 2 * HALO, height), jnp.float32)
            sides[lot * visits + visit][...] = jnp.concatenate(
                [right[:, here], gap, left[:, here]], axis=0
            ).T.astype(jnp.bfloat16)
    corners = first

    def whole_rows(span, into, cells, rows, side, side_rows):
        field[span, into, :TX] = cells[rows, :]
        if not bare:
            field[span, into, TX:] = side[side_rows, :]

    def rim_rows(span, into, cells, rows, side, side_rows):
        rim[span, into, :SIDE] = cells[rows, :SIDE]
        rim[span, into, SIDE : 2 * SIDE] = cells[rows, TX - SIDE :]
        rim[span, into, 2 * SIDE :] = side[side_rows, :]

    def assemble(order, copies, put):
        for chunk, visit, first, rows, at_row, begin, end, shift in copies:
            tall_of, base, lot = chunks[chunk]
            cells = cells_of[chunk][order[visit]]
            side = None if bare else sides[lot * visits + order[visit]]

            @pl.loop(begin, end)
            def _(unit):
                start = pl.multiple_of((unit - base) * tall_of + first, EDGE)
                beside = pl.multiple_of(unit * tall_of + first, EDGE)
                put(
                    unit + shift, pl.ds(at_row, rows), cells, pl.ds(start, rows), side,
                    pl.ds(beside, rows),
                )

    def assemble_all(order):
        assemble(order, copies, whole_rows)
        if mend:
            assemble(order, mend[1], rim_rows)

    if bare:
        field[:, :, TX:] = jnp.zeros((spans, tall, SIDE), jnp.bfloat16)
    for span, first, rows in fields["blank"]:
        field[span, first : first + rows, :] = jnp.zeros((rows, WIDE), jnp.bfloat16)
    if mend:
        for span, first, rows in mend[0]["blank"]:
            rim[span, first : first + rows, :] = jnp.zeros((rows, 3 * SIDE), jnp.bfloat16)
    if visits == 2:
        for flip in range(2):

            @pl.when(mine_ref[0] == flip)
            def _():
                assemble_all((0, 1) if flip == 0 else (1, 0))

    else:
        assemble_all(tuple(range(visits)))

    between = (mend or plan)[0]["between"]
    if between:
        from_left = lax.broadcasted_iota(jnp.int32, (HALO, SIDE), 1) >= SIDE // 2
        for number, rows in enumerate((above_ref, below_ref)):
            if between[number] is None:
                continue
            corner = jnp.zeros((HALO, SIDE), jnp.float32)
            if not bare:
                here = slice(corners + number * SIDE, corners + (number + 1) * SIDE)
                corner = jnp.where(from_left, left[:, here], right[:, here])
            if mend:
                wide = jnp.concatenate([rows[:, :SIDE], rows[:, TX - SIDE :], corner], axis=1)
            else:
                wide = jnp.concatenate([rows[...], corner], axis=1)
            strip = [jnp.zeros_like(wide), wide] if number == 0 else [wide, jnp.zeros_like(wide)]
            strip = jnp.concatenate(strip, axis=0).astype(jnp.bfloat16)
            into = slice(between[number], between[number] + EDGE)
            if mend:
                rim[number * (rim.shape[0] - 1), into, :] = strip
            else:
                field[number * (spans - 1), into, :] = strip

    taps = [taps_ref[tap] for tap in range(7)]
    lane = lax.broadcasted_iota(jnp.int32, (1, SIDE), 1)

    if mend:
        for copy in column_copies(held_hbm, False):
            copy.wait()
        count = rim.shape[0]
        tiles = []
        for tile in range(WIDE // SIDE):
            pair = jnp.zeros(rim.shape[1:2] + (SIDE,), jnp.bfloat16)
            for span in range(2 * tile, min(2 * tile + 2, count)):
                base = (span % 2) * (SIDE // 2)
                near, far, halo = (rim[span, :, at * SIDE : (at + 1) * SIDE] for at in range(3))
                for value, first, last, by in (
                    (halo, 0, 8, 8), (near, 8, 32, 8), (far, 32, 56, 56), (halo, 56, 64, 56),
                ):
                    inside = (lane >= base + first) & (lane < base + last)
                    pair = jnp.where(inside, pltpu.roll(value, (base + by) % SIDE, 1), pair)
            tiles.append(pair)
        mended = filtered(jnp.concatenate(tiles, axis=1), taps, mend_tables, mend[0]["margin"])
        for begin, end, source, rows, shift in mend[2]:
            for span in range(begin, end):
                base = (span % 2) * (SIDE // 2)
                tile = slice((span // 2) * SIDE, (span // 2 + 1) * SIDE)
                target = slice(span * STEP + shift, span * STEP + shift + rows)
                for number in range(2):
                    value = mended[number][source : source + rows, tile]
                    for edge, by, good in ((0, -base - 8, lane < 8), (1, 72 - base, lane >= 120)):
                        columns[number, edge, target, :] = jnp.where(
                            good, pltpu.roll(value, by % SIDE, 1), columns[number, edge, target, :]
                        )

    lanes = pl.ds(SIDE, TX - 2 * SIDE) if mend else pl.ds(0, TX)

    def stores(unit, source, rows, target):
        return [
            pltpu.make_async_copy(
                scratch.at[unit, pl.ds(source, rows), lanes],
                hbm.at[pl.ds(target, rows), lanes],
                sems.at[unit, at],
            )
            for at, (scratch, hbm) in enumerate(zip(results, out_hbm))
        ]

    some = next(count for count in (4, 3, 2, 1) if spans % count == 0 and count * tall <= 320)

    @pl.loop(0, spans, step=some)
    def _(first):
        for ahead in range(some):
            unit = first + ahead
            detection[unit], variance[unit] = filtered(field[unit], taps, tables, fields["margin"])
        for ahead in range(some):
            unit = first + ahead
            for begin, end, source, rows, shift in outs:

                @pl.when((unit >= begin) & (unit < end))
                def _():
                    target = pl.multiple_of(unit * STEP + shift, HALO)
                    for store in stores(unit, source, rows, target):
                        store.start()
                    if mend:
                        for number in range(2):
                            for edge in range(2):
                                columns[number, edge, pl.ds(target, rows), :] = results[number][
                                    unit, source : source + rows, pl.ds(edge * (TX - SIDE), SIDE)
                                ]

    if mend:
        for copy in column_copies(out_hbm, True):
            copy.start()

    @pl.loop(0, spans)
    def _(unit):
        for begin, end, source, rows, shift in outs:

            @pl.when((unit >= begin) & (unit < end))
            def _():
                for store in stores(unit, source, rows, 0):
                    store.wait()

    if mend:
        for copy in column_copies(out_hbm, True):
            copy.wait()


def stage(plan, mine, taps, between, tables, chunks, cells, beside=(), heights=(), mend=None, mend_tables=(), held=()):
    fields = plan[0]
    spans, tall = fields["spans"], fields["tall"]
    shape = jax.ShapeDtypeStruct((TY, TX), jnp.float32)
    vmems = [*between, *tables, *mend_tables, *beside, *[array for parts in cells for array in parts]]
    out = pltpu.VMEM((spans, tall - 2 * fields["margin"], TX), jnp.float32)
    scratch = [pltpu.VMEM((spans, tall, WIDE), jnp.bfloat16), out, out, pltpu.SemaphoreType.DMA((spans, 2))]
    if mend:
        scratch += [
            pltpu.VMEM((mend[0]["spans"], mend[0]["tall"], 3 * SIDE), jnp.bfloat16),
            pltpu.VMEM((2, 2, TY, SIDE), jnp.float32),
            pltpu.SemaphoreType.DMA((2, 2)),
        ]
    for height in heights:
        scratch += [pltpu.VMEM((height, SIDE), jnp.bfloat16)] * fields["visits"]
    return pl.pallas_call(
        functools.partial(stage_kernel, plan, mend, chunks, heights),
        out_shape=(shape, shape),
        in_specs=[SMEM, SMEM] + [VMEM] * len(vmems) + [HBM] * len(held),
        out_specs=(HBM, HBM),
        input_output_aliases={2 + len(vmems) + at: at for at in range(len(held))},
        scratch_shapes=scratch,
        compiler_params=pltpu.CompilerParams(vmem_limit_bytes=56 * MIB),
        cost_estimate=pl.CostEstimate(
            flops=80 * spans * tall * WIDE, bytes_accessed=12 * spans * tall * WIDE, transcendentals=0
        ),
        name="stage",
    )(mine, taps, *vmems, *held)


def outer_plan(lot, begin, end, pieces):
    fields = dict(
        visits=2, spans=end - begin, tall=2 * lot, margin=HALO, held=0 if begin == 0 else 2,
        between=(lot - EDGE if begin == 0 else None, lot if end == UNITS + 1 else None),
        blank=([(0, 0, lot - EDGE)] if begin == 0 else [])
        + ([(end - begin - 1, lot + EDGE, lot - EDGE)] if end == UNITS + 1 else []),
    )
    copies = []
    for chunk, first, last in pieces:
        copies.append((chunk, 1, 0, lot, 0, max(first, begin - 1), min(last, end - 1), 1 - begin))
        copies.append((chunk, 0, 0, lot, lot, max(first, begin), min(last, end), -begin))
    rows = lot - HALO
    outs = []
    if begin == 0:
        outs.append((0, 1, rows, rows, 0))
    outs.append((max(begin, 1) - begin, min(end, UNITS) - begin, 0, 2 * rows, begin * STEP - rows))
    if end == UNITS + 1:
        outs.append((UNITS - begin, end - begin, 0, rows, begin * STEP - rows))
    return fields, [copy for copy in copies if copy[5] < copy[6]], outs


def inner_plan(lot, inner, pieces):
    tall = 2 * inner + 2 * EDGE
    fields = dict(visits=2, spans=UNITS, tall=tall, margin=HALO, between=None, blank=[], held=2)
    copies = [
        (len(pieces), 0, 0, inner, EDGE, 0, UNITS, 0),
        (len(pieces), 1, 0, inner, EDGE + inner, 0, UNITS, 0),
    ]
    for chunk, first, last in pieces:
        copies.append((chunk, 0, lot - EDGE, EDGE, 0, first, last, 0))
        copies.append((chunk, 1, 0, EDGE, EDGE + 2 * inner, first, last, 0))
    return fields, copies, [(0, UNITS, 0, tall - 2 * HALO, lot - HALO)]


def whole_plan(lot, visits):
    fields = dict(
        visits=visits, spans=UNITS, tall=STEP + 2 * EDGE, margin=EDGE, held=0,
        between=(0, EDGE + STEP), blank=[],
    )
    copies = [(0, visit, 0, lot, EDGE + visit * lot, 0, UNITS, 0) for visit in range(visits)]
    copies.append((0, visits - 1, lot - EDGE, EDGE, 0, 0, UNITS - 1, 1))
    copies.append((0, 0, 0, EDGE, EDGE + STEP, 1, UNITS, -1))
    return fields, copies, [(0, UNITS, 0, STEP, 0)]


def per_device(
    images, inv_var, good_columns, warp_rows, warp_cols, block_visit, dest_tile, offsets, psf_taps
):
    tiles = lax.axis_size("py") * lax.axis_size("px")
    visits = lax.axis_size("visit")
    plan = shares(visits)
    lots = [rows for rows, _ in plan]
    mine = lax.axis_index("visit").astype(jnp.int32).reshape(1)

    def make(chunk, var):
        return warp(
            tiles, plan[chunk], chunk == 0, block_visit, dest_tile[:, 0], offsets.T,
            good_columns, warp_rows, warp_cols, var, images,
        )

    def send(blocks):
        return lax.all_to_all(blocks, EVERY, split_axis=0, concat_axis=0, tiled=True)

    made, psf_taps = lax.optimization_barrier((make(0, inv_var), psf_taps))
    arrived = send(made)
    if len(plan) == 1:
        every = whole_plan(lots[0], visits)
        coadd, strip, edge = place(codes(arrived), arrived, lots[0])
        all_of = [lax.all_gather(part, "visit") for part in (coadd, strip, edge)]
        between = neighbours(all_of[2][0, :HALO], all_of[2][visits - 1, HALO:], "py")
        sides = beyond([all_of[1][visit] for visit in range(visits)], *between)
        cells = [all_of[0][visit] for visit in range(visits)]
        height = lots[0] * UNITS
        return stage(
            every, mine, psf_taps, between, bands(every, psf_taps), [(lots[0], 0, 0)], [cells], sides, [height]
        )

    lot, inner_lot = lots
    ranges = [(0, CUT), (CUT - 1, UNITS)]
    first_part = outer_plan(lot, 0, CUT, [(0, 0, CUT)])
    second_part = outer_plan(lot, CUT, UNITS + 1, [(0, CUT - 1, UNITS)])
    pieces = [(0, 0, CUT), (1, CUT, UNITS)]
    outer, inner = outer_plan(lot, 0, UNITS + 1, pieces), inner_plan(lot, inner_lot, pieces)
    tables, inv_var = lax.optimization_barrier(
        ([bands(part, psf_taps) for part in (outer, inner)], inv_var)
    )
    arrived, later = lax.optimization_barrier((arrived, make(1, inv_var)))
    second = send(later)
    code = codes(arrived)
    *cells, strip, edge = place(code, arrived, lot, ranges)
    cells = [(piece, swapped(piece)) for piece in cells]
    outer_strip = strip
    between = rows_between(edge)
    held = stage(first_part, mine, psf_taps, between, tables[0], [(lot, 0, 0)], cells[:1])
    held = stage(
        second_part, mine, psf_taps, between, tables[0], [(lot, CUT - 1, 0)], cells[1:], held=held
    )
    second, held = lax.optimization_barrier((second, held))
    coadd, strip, _ = place(code, second, inner_lot)
    height = lot * UNITS
    strip = jnp.concatenate([outer_strip, strip], axis=1)
    other = swapped(strip)
    strips = [half[:, span] for span in (slice(height), slice(height, None)) for half in (strip, other)]
    sides = beyond(strips, *between)
    return stage(
        inner, mine, psf_taps, between, tables[1], [(lot, 0, 0), (lot, CUT - 1, 0), (inner_lot, 0, 1)],
        [*cells, (coadd, swapped(coadd))], sides, [lot * UNITS, inner_lot * UNITS], outer, tables[0], held,
    )


def codes(arrived):
    note = arrived[:, arrived.shape[1] - NOTE, :: SIDE // CAP]
    return note.astype(jnp.float32).astype(jnp.int32).reshape(-1)


def solution(mesh):
    in_specs = (
        P(EVERY, None, None),
        P(EVERY, None, None),
        P("visit", None),
        P("visit", None, None),
        P("visit", None, None),
        P(EVERY),
        P(EVERY, None),
        P(EVERY, None),
        P(),
    )
    out_specs = (P("py", "px"), P("py", "px"))
    return jax.shard_map(
        per_device, mesh=mesh, in_specs=in_specs, out_specs=out_specs, check_vma=False
    )
```

```python
import functools

import jax
import jax.numpy as jnp
from jax import lax
from jax.experimental import pallas as pl
from jax.experimental.pallas import tpu as pltpu
from jax.sharding import PartitionSpec as P

TY = 1024
TX = 1024
STEP = 128
CAP = 2
UNITS = TY // STEP
HALO = 8
EDGE = 16
SIDE = 128
WIDE = TX + SIDE
GROUP = 4
NOTE = 16
MIB = 1 << 20
EVERY = ("visit", "py", "px")
HBM = pl.BlockSpec(memory_space=pltpu.HBM)
SMEM = pl.BlockSpec(memory_space=pltpu.SMEM)
VMEM = pl.BlockSpec(memory_space=pltpu.VMEM)


def shares(visits):
    if visits == 2:
        edge, inner = 48, 16
        return [(edge, (0, STEP - edge)), (inner, (edge, edge + inner))]
    rows = STEP // visits
    return [(rows, tuple(visit * rows for visit in range(visits)))]


def warp_kernel(
    tiles, share, noted, visit_ref, tile_ref, offset_ref, good_ref, rows_hbm, cols_hbm, var_hbm,
    image_hbm, out_hbm, rows, cols, var, image, done, note, count, table_sems, sems, out_sems,
):
    blocks, side, _ = var.shape
    some, firsts = share
    groups = blocks // GROUP
    slot_rows = done.shape[2]
    tables = [
        pltpu.make_async_copy(rows_hbm, rows, table_sems.at[0]),
        pltpu.make_async_copy(cols_hbm, cols, table_sems.at[1]),
    ]

    def loads(group):
        span = pl.ds(group * GROUP, GROUP)
        return (
            pltpu.make_async_copy(var_hbm.at[span], var.at[span], sems.at[group, 0]),
            pltpu.make_async_copy(image_hbm.at[span], image.at[span], sems.at[group, 1]),
        )

    for load in tables:
        load.start()
    for group in range(groups):
        for load in loads(group):
            load.start()

    @pl.loop(0, tiles)
    def _(tile):
        count[tile] = 0

    if noted:
        note[...] = jnp.full(note.shape, -1, jnp.bfloat16)
        slot_of_lane = lax.broadcasted_iota(jnp.int32, (NOTE, SIDE), 1) // (SIDE // CAP)

    for load in tables:
        load.wait()

    strips = [first + strip * STEP for first in firsts for strip in range(side // STEP)]
    tall = some * len(strips)
    part = tall // len(firsts)

    @pl.loop(0, groups)
    def _(group):
        for load in loads(group):
            load.wait()
        visits = [visit_ref[group * GROUP + ahead] for ahead in range(GROUP)]
        planes, turned, warped = [], [], []
        for ahead in range(GROUP):
            block = group * GROUP + ahead
            good = good_ref[pl.ds(visits[ahead], 1), :].astype(jnp.float32)
            weight = var[block].astype(jnp.float32) * good
            data = weight * image[block].astype(jnp.float32)
            planes.append(
                jnp.concatenate([data.astype(jnp.bfloat16), weight.astype(jnp.bfloat16)], axis=1)
            )
        for ahead in range(GROUP):
            matrix = jnp.concatenate(
                [rows[visits[ahead], first : first + some, :] for first in strips], axis=0
            )
            turned.append(
                jnp.dot(matrix, planes[ahead], preferred_element_type=jnp.float32).astype(jnp.bfloat16)
            )
        for ahead in range(GROUP):
            both = jnp.concatenate([turned[ahead][:, :side], turned[ahead][:, side:]], axis=0)
            warped.append(
                lax.dot_general(
                    both,
                    cols[visits[ahead]],
                    (((1,), (1,)), ((), ())),
                    preferred_element_type=jnp.float32,
                ).astype(jnp.bfloat16)
            )
        for ahead in range(GROUP):
            block = group * GROUP + ahead
            for visit in range(len(firsts)):
                for half in range(side // SIDE):
                    for plane in range(2):
                        start = plane * tall + visit * part
                        into = (2 * half + plane) * part
                        done[block, visit, into : into + part, :] = warped[ahead][
                            start : start + part, half * SIDE : (half + 1) * SIDE
                        ]
        for ahead in range(GROUP):
            block = group * GROUP + ahead
            tile = tile_ref[block]
            rank = count[tile]
            count[tile] = rank + 1
            for visit in range(len(firsts)):
                target = visit * tiles + tile
                pltpu.make_async_copy(
                    done.at[block, visit],
                    out_hbm.at[target, pl.ds(pl.multiple_of(rank * slot_rows, NOTE), slot_rows)],
                    out_sems.at[block, visit],
                ).start()
                if noted:
                    code = offset_ref[0, block] * 8 + offset_ref[1, block]
                    note[target] = jnp.where(
                        slot_of_lane == rank, code.astype(jnp.float32), note[target].astype(jnp.float32)
                    ).astype(jnp.bfloat16)

    if noted:
        notes = pltpu.make_async_copy(
            note, out_hbm.at[:, pl.ds(CAP * slot_rows, NOTE)], table_sems.at[0]
        )
        notes.start()

    @pl.loop(0, blocks)
    def _(block):
        for visit in range(len(firsts)):
            pltpu.make_async_copy(
                done.at[block, visit], out_hbm.at[0, pl.ds(0, slot_rows)], out_sems.at[block, visit]
            ).wait()

    if noted:
        notes.wait()


def warp(tiles, share, noted, visit, tile, offset, good, rows, cols, var, image):
    blocks, side, _ = var.shape
    some, firsts = share
    slot_rows = 2 * (side // STEP) * some * (side // SIDE)
    visits = len(firsts)
    return pl.pallas_call(
        functools.partial(warp_kernel, tiles, share, noted),
        out_shape=jax.ShapeDtypeStruct(
            (visits * tiles, CAP * slot_rows + noted * NOTE, SIDE), jnp.bfloat16
        ),
        in_specs=[SMEM, SMEM, SMEM, VMEM, HBM, HBM, HBM, HBM],
        out_specs=HBM,
        scratch_shapes=[
            pltpu.VMEM(rows.shape, jnp.bfloat16),
            pltpu.VMEM(cols.shape, jnp.bfloat16),
            pltpu.VMEM(var.shape, jnp.bfloat16),
            pltpu.VMEM(var.shape, jnp.bfloat16),
            pltpu.VMEM((blocks, visits, slot_rows, SIDE), jnp.bfloat16),
            pltpu.VMEM((visits * tiles, NOTE, SIDE), jnp.bfloat16),
            pltpu.SMEM((tiles,), jnp.int32),
            pltpu.SemaphoreType.DMA((2,)),
            pltpu.SemaphoreType.DMA((blocks // GROUP, 2)),
            pltpu.SemaphoreType.DMA((blocks, visits)),
        ],
        compiler_params=pltpu.CompilerParams(vmem_limit_bytes=60 * MIB),
        cost_estimate=pl.CostEstimate(
            flops=8 * blocks * side**3, bytes_accessed=8 * blocks * side**2, transcendentals=0
        ),
        name="warp",
    )(visit, tile, offset, good, rows, cols, var, image)


def place_kernel(part, code_ref, blocks_ref, coadd_ref, strip_ref, edge_ref, data, weight):
    step = pl.program_id(0)
    some = blocks_ref.shape[0]
    height = data.shape[0]
    lot = height // UNITS

    @pl.when(step == 0)
    def _():
        data[...] = jnp.zeros_like(data)
        weight[...] = jnp.zeros_like(weight)

    for block in range(some):
        for slot in range(CAP):
            code = code_ref[(step * some + block) * CAP + slot]

            @pl.when(code >= 0)
            def _():
                row = pl.multiple_of((code // 8) * lot, lot)
                for half in range(2):
                    col = pl.multiple_of((code % 8 + half) * STEP, STEP)
                    cells = (pl.ds(row, part), pl.ds(col, STEP))
                    first = (slot * 2 + half) * 2 * part
                    data[cells] += blocks_ref[block, first : first + part].astype(jnp.float32)
                    weight[cells] += blocks_ref[block, first + part : first + 2 * part].astype(
                        jnp.float32
                    )

    @pl.when(step == pl.num_programs(0) - 1)
    def _():
        coadd = data[...] / jnp.maximum(weight[...], 1.0)
        coadd_ref[...] = coadd.astype(coadd_ref.dtype)
        strip_ref[:HALO] = coadd[:, :SIDE].T[:HALO]
        strip_ref[HALO:] = coadd[:, TX - SIDE :].T[SIDE - HALO :]
        edge_ref[:HALO] = coadd[:HALO]
        edge_ref[HALO:] = coadd[height - HALO :]


def place(code, blocks, lot):
    count, tall, side = blocks.shape
    some = 4
    height = lot * UNITS
    shapes = [((height, TX), jnp.bfloat16), ((2 * HALO, height), jnp.float32), ((2 * HALO, TX), jnp.float32)]
    return pl.pallas_call(
        functools.partial(place_kernel, 2 * lot),
        grid_spec=pltpu.PrefetchScalarGridSpec(
            num_scalar_prefetch=1,
            grid=(count // some,),
            in_specs=[pl.BlockSpec((some, tall, side), lambda step, code: (step, 0, 0))],
            out_specs=[pl.BlockSpec(shape, lambda step, code: (0, 0)) for shape, _ in shapes],
            scratch_shapes=[pltpu.VMEM((height, TX), jnp.float32)] * 2,
        ),
        out_shape=[jax.ShapeDtypeStruct(*shape) for shape in shapes],
        compiler_params=pltpu.CompilerParams(vmem_limit_bytes=32 * MIB),
        cost_estimate=pl.CostEstimate(
            flops=count * tall * side, bytes_accessed=count * tall * side * 2, transcendentals=0
        ),
        name="place",
    )(code, blocks)


def beside(axis):
    count = lax.axis_size(axis)
    up = [(i, i + 1) for i in range(count - 1)]
    return up, [(j, i) for i, j in up]


def neighbours(first, last, axis):
    up, down = beside(axis)
    return lax.ppermute(last, axis, up), lax.ppermute(first, axis, down)


def swapped(array):
    return lax.ppermute(array, "visit", [(0, 1), (1, 0)])


def beyond(strips, above, below):
    first = [strip[:HALO] for strip in strips] + [rows[:, :SIDE] for rows in (above, below)]
    last = [strip[HALO:] for strip in strips] + [rows[:, TX - SIDE :] for rows in (above, below)]
    return neighbours(jnp.concatenate(first, axis=1), jnp.concatenate(last, axis=1), "px")


def rows_between(edge):
    lower = lax.axis_index("visit") == 0
    mine = jnp.where(lower, edge[:HALO], edge[HALO:])
    count = lax.axis_size("py")
    up, down = beside("py")

    def pairs(cross):
        return [(i, j + cross * count) for i, j in down] + [
            (count + i, j + (1 - cross) * count) for i, j in up
        ]

    straight = lax.ppermute(mine, ("visit", "py"), pairs(0))
    crossed = lax.ppermute(mine, ("visit", "py"), pairs(1))
    return jnp.where(lower, crossed, straight), jnp.where(lower, straight, crossed)


def bands(plan, taps):
    tall, margin = plan[0]["tall"], plan[0]["margin"]
    row = jnp.arange(tall, dtype=jnp.int32)
    out = jnp.arange(tall - 2 * margin, dtype=jnp.int32) + margin
    three = (jnp.abs(row[:, None] - row[None, :]) <= 1).astype(jnp.bfloat16)
    nine = (jnp.abs(out[:, None] - row[None, :]) <= 4).astype(jnp.bfloat16)
    count = taps.shape[0]
    ahead = row[None, :] - out[:, None] + count // 2
    coarse, fine = split(sum(jnp.where(ahead == tap, taps[tap], 0.0) for tap in range(count)))
    lane = jnp.arange(4 * SIDE, dtype=jnp.int32)
    across = jnp.abs(lane[:, None] - lane[None, SIDE : 3 * SIDE]) <= 4
    return (
        jnp.concatenate([three] * 2, axis=1),
        jnp.concatenate([nine] * 2, axis=1),
        jnp.concatenate([coarse, coarse, fine], axis=1),
        across.astype(jnp.bfloat16),
    )


def split(value):
    coarse = value.astype(jnp.bfloat16)
    return coarse, (value - coarse.astype(jnp.float32)).astype(jnp.bfloat16)


def filtered(value, taps, tables, margin):
    three, nine, blur, across = [table[...] for table in tables]
    tall = value.shape[0]
    short = tall - 2 * margin

    def product(matrix, terms):
        return jnp.dot(matrix, jnp.concatenate(terms, axis=0), preferred_element_type=jnp.float32)

    moved = {
        by: (pltpu.roll(value, -by % WIDE, 1) if by else value).astype(jnp.float32)
        for by in range(-3, 4)
    }
    rowwise = sum(taps[tap] * moved[tap - 3] for tap in range(7))[:, :TX]
    resid = moved[0] - product(three, split(moved[-1] + moved[0] + moved[1])) * (1.0 / 9.0)
    tower = jnp.concatenate(split(product(nine, split(resid * resid))), axis=0)
    windows = [jnp.concatenate([tower[:, TX:], tower[:, : 3 * SIDE]], axis=1)]
    for start in range(2 * SIDE, TX, 2 * SIDE):
        windows.append(tower[:, start - SIDE : start + 3 * SIDE])
    boxes = jnp.dot(jnp.concatenate(windows, axis=0), across, preferred_element_type=jnp.float32)
    box = jnp.concatenate(
        [
            boxes[2 * at * short : (2 * at + 1) * short] + boxes[(2 * at + 1) * short : (2 * at + 2) * short]
            for at in range(len(windows))
        ],
        axis=1,
    )
    local = box * (1.0 / 81.0) + 1e-05
    coarse, fine = split(rowwise)
    return product(blur, (coarse, fine, coarse)) * lax.rsqrt(local), local


def stage_kernel(plan, lots, *refs):
    mine_ref, taps_ref, above_ref, below_ref = refs[:4]
    tables = refs[4:8]
    fields, copies, outs = plan
    visits, margin = fields["visits"], fields["margin"]
    at = 8
    chunks = []
    for lot in lots:
        parts = []
        for _ in range(visits):
            parts.append(refs[at : at + 3])
            at += 3
        chunks.append(parts)
    at += fields["aliased"]
    detection_hbm, variance_hbm = refs[at : at + 2]
    field, detection, variance, sems = refs[at + 2 : at + 6]
    sides = refs[at + 6 :]
    spans, tall, _ = field.shape

    which = 0
    held = []
    for parts in chunks:
        group = []
        for number, (cells, left, right) in enumerate(parts):
            side = sides[which]
            which += 1
            height = cells.shape[0]
            first = number * height if left.shape[1] > height else 0
            here = slice(first, first + height)
            gap = jnp.zeros((SIDE - 2 * HALO, height), jnp.float32)
            side[...] = jnp.concatenate(
                [right[right.shape[0] - HALO :, here], gap, left[:HALO, here]], axis=0
            ).T.astype(jnp.bfloat16)
            group.append((cells, side))
        held.append(group)

    for span, first, rows in fields["blank"]:
        field[span, first : first + rows, :] = jnp.zeros((rows, WIDE), jnp.bfloat16)

    def assemble(order):
        for chunk, visit, first, rows, at_row, begin, end, shift in copies:
            cells, side = held[chunk][order[visit]]
            lot = lots[chunk]

            @pl.loop(begin, end)
            def _(unit):
                start = pl.multiple_of(unit * lot + first, EDGE)
                into = pl.ds(at_row, rows)
                field[unit + shift, into, :TX] = cells[pl.ds(start, rows), :]
                field[unit + shift, into, TX:] = side[pl.ds(start, rows), :]

    if visits == 2:
        for flip in range(2):

            @pl.when(mine_ref[0] == flip)
            def _():
                assemble((0, 1) if flip == 0 else (1, 0))

    else:
        assemble(tuple(range(visits)))

    if fields["between"]:
        _, left, right = chunks[0][0]
        corners = left.shape[1] - 2 * SIDE
        from_left = lax.broadcasted_iota(jnp.int32, (HALO, SIDE), 1) >= SIDE // 2
        none = jnp.zeros((EDGE - HALO, WIDE), jnp.float32)
        for number, (span, first, rows) in enumerate(
            zip((0, spans - 1), fields["between"], (above_ref, below_ref))
        ):
            here = slice(corners + number * SIDE, corners + (number + 1) * SIDE)
            wide = jnp.concatenate(
                [rows[...], jnp.where(from_left, left[:, here], right[:, here])], axis=1
            )
            strip = [none, wide] if number == 0 else [wide, none]
            field[span, first : first + EDGE, :] = jnp.concatenate(strip, axis=0).astype(jnp.bfloat16)

    taps = [taps_ref[tap] for tap in range(7)]

    def stores(unit, source, rows, target):
        return [
            pltpu.make_async_copy(
                scratch.at[unit, pl.ds(source, rows)], hbm.at[pl.ds(target, rows)], sems.at[unit, at]
            )
            for at, (scratch, hbm) in enumerate(
                ((detection, detection_hbm), (variance, variance_hbm))
            )
        ]

    some = next(count for count in (4, 3, 2, 1) if spans % count == 0 and count * tall <= 320)

    @pl.loop(0, spans, step=some)
    def _(first):
        for ahead in range(some):
            unit = first + ahead
            detection[unit], variance[unit] = filtered(field[unit], taps, tables, margin)
        for ahead in range(some):
            unit = first + ahead
            for begin, end, source, rows, shift in outs:

                @pl.when((unit >= begin) & (unit < end))
                def _():
                    target = pl.multiple_of(unit * STEP + shift, HALO)
                    for store in stores(unit, source, rows, target):
                        store.start()

    @pl.loop(0, spans)
    def _(unit):
        for begin, end, source, rows, shift in outs:

            @pl.when((unit >= begin) & (unit < end))
            def _():
                for store in stores(unit, source, rows, 0):
                    store.wait()


def stage(plan, mine, taps, between, tables, chunks, lots, held=()):
    fields, _, _ = plan
    spans, tall = fields["spans"], fields["tall"]
    shape = jax.ShapeDtypeStruct((TY, TX), jnp.float32)
    flat = [array for parts in chunks for part in parts for array in part]
    first = 8 + len(flat)
    out = pltpu.VMEM((spans, tall - 2 * fields["margin"], TX), jnp.float32)
    return pl.pallas_call(
        functools.partial(stage_kernel, plan, lots),
        out_shape=(shape, shape),
        in_specs=[SMEM, SMEM] + [VMEM] * (6 + len(flat)) + [HBM] * len(held),
        out_specs=(HBM, HBM),
        input_output_aliases={first + at: at for at in range(len(held))},
        scratch_shapes=[
            pltpu.VMEM((spans, tall, WIDE), jnp.bfloat16),
            out,
            out,
            pltpu.SemaphoreType.DMA((spans, 2)),
        ]
        + [pltpu.VMEM((part[0].shape[0], SIDE), jnp.bfloat16) for parts in chunks for part in parts],
        compiler_params=pltpu.CompilerParams(vmem_limit_bytes=56 * MIB),
        cost_estimate=pl.CostEstimate(
            flops=80 * spans * tall * WIDE, bytes_accessed=12 * spans * tall * WIDE, transcendentals=0
        ),
        name="stage",
    )(mine, taps, *between, *tables, *flat, *held)


def outer_plan(lot):
    fields = dict(
        visits=2, aliased=0, spans=UNITS + 1, tall=2 * lot, margin=HALO, between=(lot - EDGE, lot),
        blank=[(0, 0, lot - EDGE), (UNITS, lot + EDGE, lot - EDGE)],
    )
    copies = [(0, 1, 0, lot, 0, 0, UNITS, 1), (0, 0, 0, lot, lot, 0, UNITS, 0)]
    rows = lot - HALO
    outs = [
        (0, 1, rows, rows, 0),
        (1, UNITS, 0, 2 * rows, -rows),
        (UNITS, UNITS + 1, 0, rows, -rows),
    ]
    return fields, copies, outs


def inner_plan(lot, inner):
    tall = 2 * inner + 2 * EDGE
    fields = dict(
        visits=2, aliased=2, spans=UNITS, tall=tall, margin=HALO, between=None, blank=[]
    )
    copies = [
        (0, 0, lot - EDGE, EDGE, 0, 0, UNITS, 0),
        (1, 0, 0, inner, EDGE, 0, UNITS, 0),
        (1, 1, 0, inner, EDGE + inner, 0, UNITS, 0),
        (0, 1, 0, EDGE, EDGE + 2 * inner, 0, UNITS, 0),
    ]
    return fields, copies, [(0, UNITS, 0, tall - 2 * HALO, lot - HALO)]


def whole_plan(lot, visits):
    fields = dict(
        visits=visits, aliased=0, spans=UNITS, tall=STEP + 2 * EDGE, margin=EDGE,
        between=(0, EDGE + STEP), blank=[],
    )
    copies = [(0, visit, 0, lot, EDGE + visit * lot, 0, UNITS, 0) for visit in range(visits)]
    copies.append((0, visits - 1, lot - EDGE, EDGE, 0, 0, UNITS - 1, 1))
    copies.append((0, 0, 0, EDGE, EDGE + STEP, 1, UNITS, -1))
    return fields, copies, [(0, UNITS, 0, STEP, 0)]


def per_device(
    images, inv_var, good_columns, warp_rows, warp_cols, block_visit, dest_tile, offsets, psf_taps
):
    tiles = lax.axis_size("py") * lax.axis_size("px")
    visits = lax.axis_size("visit")
    plan = shares(visits)
    lots = [rows for rows, _ in plan]
    mine = lax.axis_index("visit").astype(jnp.int32).reshape(1)

    def make(chunk, var):
        return warp(
            tiles, plan[chunk], chunk == 0, block_visit, dest_tile[:, 0], offsets.T,
            good_columns, warp_rows, warp_cols, var, images,
        )

    def send(blocks):
        return lax.all_to_all(blocks, EVERY, split_axis=0, concat_axis=0, tiled=True)

    made, psf_taps = lax.optimization_barrier((make(0, inv_var), psf_taps))
    arrived = send(made)
    if len(plan) == 1:
        every = whole_plan(lots[0], visits)
        coadd, strip, edge = place(codes(arrived), arrived, lots[0])
        all_of = [lax.all_gather(part, "visit") for part in (coadd, strip, edge)]
        between = neighbours(all_of[2][0, :HALO], all_of[2][visits - 1, HALO:], "py")
        sides = beyond([all_of[1][visit] for visit in range(visits)], *between)
        parts = [(all_of[0][visit], *sides) for visit in range(visits)]
        return stage(every, mine, psf_taps, between, bands(every, psf_taps), [parts], lots)

    outer, inner = outer_plan(lots[0]), inner_plan(*lots)
    tables, inv_var = lax.optimization_barrier(
        ([bands(part, psf_taps) for part in (outer, inner)], inv_var)
    )
    arrived, later = lax.optimization_barrier((arrived, make(1, inv_var)))
    second = send(later)
    code = codes(arrived)
    coadd, strip, edge = place(code, arrived, lots[0])
    between, other_strip = rows_between(edge), swapped(strip)
    coadd, between, other_strip = lax.optimization_barrier((coadd, between, other_strip))
    sides = beyond([strip, other_strip], *between)
    other = swapped(coadd)
    second, sides, other = lax.optimization_barrier((second, sides, other))
    parts = [(coadd, *sides), (other, *sides)]
    coadd, strip, _ = place(code, second, lots[1])
    other = swapped(coadd)
    near = neighbours(strip[:HALO], strip[HALO:], "px")
    (parts, between), _ = lax.optimization_barrier(((parts, between), coadd))
    held = stage(outer, mine, psf_taps, between, tables[0], [parts], lots[:1])
    far = swapped(jnp.concatenate(near, axis=0))
    more = [(coadd, *near), (other, far, far)]
    return stage(inner, mine, psf_taps, between, tables[1], [parts, more], lots, held)


def codes(arrived):
    note = arrived[:, arrived.shape[1] - NOTE, :: SIDE // CAP]
    return note.astype(jnp.float32).astype(jnp.int32).reshape(-1)


def solution(mesh):
    in_specs = (
        P(EVERY, None, None),
        P(EVERY, None, None),
        P("visit", None),
        P("visit", None, None),
        P("visit", None, None),
        P(EVERY),
        P(EVERY, None),
        P(EVERY, None),
        P(),
    )
    out_specs = (P("py", "px"), P("py", "px"))
    return jax.shard_map(
        per_device, mesh=mesh, in_specs=in_specs, out_specs=out_specs, check_vma=False
    )
```

```python
import functools

import jax
import jax.numpy as jnp
from jax import lax
from jax.experimental import pallas as pl
from jax.experimental.pallas import tpu as pltpu
from jax.sharding import PartitionSpec as P

TY = 1024
TX = 1024
STEP = 128
CAP = 2
UNITS = TY // STEP
HALO = 8
EDGE = 16
SIDE = 128
WIDE = TX + SIDE
GROUP = 8
NOTE = 16
MIB = 1 << 20
EVERY = ("visit", "py", "px")
HBM = pl.BlockSpec(memory_space=pltpu.HBM)
SMEM = pl.BlockSpec(memory_space=pltpu.SMEM)
VMEM = pl.BlockSpec(memory_space=pltpu.VMEM)


def shares(visits):
    if visits == 2:
        edge, inner = 48, 16
        return [(edge, (0, STEP - edge)), (inner, (edge, edge + inner))]
    rows = STEP // visits
    return [(rows, tuple(visit * rows for visit in range(visits)))]


def warp_kernel(
    tiles, share, noted, visit_ref, tile_ref, offset_ref, good_ref, rows_hbm, cols_hbm, var_hbm,
    image_hbm, out_hbm, rows, cols, var, image, done, note, count, table_sems, sems, out_sems,
):
    blocks, side, _ = var.shape
    some, firsts = share
    groups = blocks // GROUP
    slot_rows = done.shape[2]
    tables = [
        pltpu.make_async_copy(rows_hbm, rows, table_sems.at[0]),
        pltpu.make_async_copy(cols_hbm, cols, table_sems.at[1]),
    ]

    def loads(group):
        span = pl.ds(group * GROUP, GROUP)
        return (
            pltpu.make_async_copy(var_hbm.at[span], var.at[span], sems.at[group, 0]),
            pltpu.make_async_copy(image_hbm.at[span], image.at[span], sems.at[group, 1]),
        )

    for load in tables:
        load.start()
    for group in range(groups):
        for load in loads(group):
            load.start()

    @pl.loop(0, tiles)
    def _(tile):
        count[tile] = 0

    if noted:
        note[...] = jnp.full(note.shape, -1, jnp.bfloat16)
        slot_of_lane = lax.broadcasted_iota(jnp.int32, (NOTE, SIDE), 1) // (SIDE // CAP)

    for load in tables:
        load.wait()

    strips = [first + strip * STEP for first in firsts for strip in range(side // STEP)]
    tall = some * len(strips)
    part = tall // len(firsts)

    @pl.loop(0, groups)
    def _(group):
        for load in loads(group):
            load.wait()
        visits = [visit_ref[group * GROUP + ahead] for ahead in range(GROUP)]
        planes, turned, warped = [], [], []
        for ahead in range(GROUP):
            block = group * GROUP + ahead
            good = good_ref[pl.ds(visits[ahead], 1), :].astype(jnp.float32)
            weight = var[block].astype(jnp.float32) * good
            data = weight * image[block].astype(jnp.float32)
            planes.append(
                jnp.concatenate([data.astype(jnp.bfloat16), weight.astype(jnp.bfloat16)], axis=1)
            )
        for ahead in range(GROUP):
            matrix = jnp.concatenate(
                [rows[visits[ahead], first : first + some, :] for first in strips], axis=0
            )
            turned.append(
                jnp.dot(matrix, planes[ahead], preferred_element_type=jnp.float32).astype(jnp.bfloat16)
            )
        for ahead in range(GROUP):
            both = jnp.concatenate([turned[ahead][:, :side], turned[ahead][:, side:]], axis=0)
            warped.append(
                lax.dot_general(
                    both,
                    cols[visits[ahead]],
                    (((1,), (1,)), ((), ())),
                    preferred_element_type=jnp.float32,
                ).astype(jnp.bfloat16)
            )
        for ahead in range(GROUP):
            block = group * GROUP + ahead
            for visit in range(len(firsts)):
                for half in range(side // SIDE):
                    for plane in range(2):
                        start = plane * tall + visit * part
                        into = (2 * half + plane) * part
                        done[block, visit, into : into + part, :] = warped[ahead][
                            start : start + part, half * SIDE : (half + 1) * SIDE
                        ]
        for ahead in range(GROUP):
            block = group * GROUP + ahead
            tile = tile_ref[block]
            rank = count[tile]
            count[tile] = rank + 1
            for visit in range(len(firsts)):
                target = visit * tiles + tile
                pltpu.make_async_copy(
                    done.at[block, visit],
                    out_hbm.at[target, pl.ds(pl.multiple_of(rank * slot_rows, NOTE), slot_rows)],
                    out_sems.at[block, visit],
                ).start()
                if noted:
                    code = offset_ref[0, block] * 8 + offset_ref[1, block]
                    note[target] = jnp.where(
                        slot_of_lane == rank, code.astype(jnp.float32), note[target].astype(jnp.float32)
                    ).astype(jnp.bfloat16)

    if noted:
        notes = pltpu.make_async_copy(
            note, out_hbm.at[:, pl.ds(CAP * slot_rows, NOTE)], table_sems.at[0]
        )
        notes.start()

    @pl.loop(0, blocks)
    def _(block):
        for visit in range(len(firsts)):
            pltpu.make_async_copy(
                done.at[block, visit], out_hbm.at[0, pl.ds(0, slot_rows)], out_sems.at[block, visit]
            ).wait()

    if noted:
        notes.wait()


def warp(tiles, share, noted, visit, tile, offset, good, rows, cols, var, image):
    blocks, side, _ = var.shape
    some, firsts = share
    slot_rows = 2 * (side // STEP) * some * (side // SIDE)
    visits = len(firsts)
    return pl.pallas_call(
        functools.partial(warp_kernel, tiles, share, noted),
        out_shape=jax.ShapeDtypeStruct(
            (visits * tiles, CAP * slot_rows + noted * NOTE, SIDE), jnp.bfloat16
        ),
        in_specs=[SMEM, SMEM, SMEM, VMEM, HBM, HBM, HBM, HBM],
        out_specs=HBM,
        scratch_shapes=[
            pltpu.VMEM(rows.shape, jnp.bfloat16),
            pltpu.VMEM(cols.shape, jnp.bfloat16),
            pltpu.VMEM(var.shape, jnp.bfloat16),
            pltpu.VMEM(var.shape, jnp.bfloat16),
            pltpu.VMEM((blocks, visits, slot_rows, SIDE), jnp.bfloat16),
            pltpu.VMEM((visits * tiles, NOTE, SIDE), jnp.bfloat16),
            pltpu.SMEM((tiles,), jnp.int32),
            pltpu.SemaphoreType.DMA((2,)),
            pltpu.SemaphoreType.DMA((blocks // GROUP, 2)),
            pltpu.SemaphoreType.DMA((blocks, visits)),
        ],
        compiler_params=pltpu.CompilerParams(vmem_limit_bytes=60 * MIB),
        cost_estimate=pl.CostEstimate(
            flops=8 * blocks * side**3, bytes_accessed=8 * blocks * side**2, transcendentals=0
        ),
        name="warp",
    )(visit, tile, offset, good, rows, cols, var, image)


def place_kernel(part, code_ref, blocks_ref, coadd_ref, strip_ref, edge_ref, data, weight):
    step = pl.program_id(0)
    some = blocks_ref.shape[0]
    height = data.shape[0]
    lot = height // UNITS

    @pl.when(step == 0)
    def _():
        data[...] = jnp.zeros_like(data)
        weight[...] = jnp.zeros_like(weight)

    for block in range(some):
        for slot in range(CAP):
            code = code_ref[(step * some + block) * CAP + slot]

            @pl.when(code >= 0)
            def _():
                row = pl.multiple_of((code // 8) * lot, lot)
                for half in range(2):
                    col = pl.multiple_of((code % 8 + half) * STEP, STEP)
                    cells = (pl.ds(row, part), pl.ds(col, STEP))
                    first = (slot * 2 + half) * 2 * part
                    data[cells] += blocks_ref[block, first : first + part].astype(jnp.float32)
                    weight[cells] += blocks_ref[block, first + part : first + 2 * part].astype(
                        jnp.float32
                    )

    @pl.when(step == pl.num_programs(0) - 1)
    def _():
        coadd = data[...] / jnp.maximum(weight[...], 1.0)
        coadd_ref[...] = coadd.astype(coadd_ref.dtype)
        strip_ref[:HALO] = coadd[:, :SIDE].T[:HALO]
        strip_ref[HALO:] = coadd[:, TX - SIDE :].T[SIDE - HALO :]
        edge_ref[:HALO] = coadd[:HALO]
        edge_ref[HALO:] = coadd[height - HALO :]


def place(code, blocks, lot):
    count, tall, side = blocks.shape
    some = 4
    height = lot * UNITS
    shapes = [((height, TX), jnp.bfloat16), ((2 * HALO, height), jnp.float32), ((2 * HALO, TX), jnp.float32)]
    return pl.pallas_call(
        functools.partial(place_kernel, 2 * lot),
        grid_spec=pltpu.PrefetchScalarGridSpec(
            num_scalar_prefetch=1,
            grid=(count // some,),
            in_specs=[pl.BlockSpec((some, tall, side), lambda step, code: (step, 0, 0))],
            out_specs=[pl.BlockSpec(shape, lambda step, code: (0, 0)) for shape, _ in shapes],
            scratch_shapes=[pltpu.VMEM((height, TX), jnp.float32)] * 2,
        ),
        out_shape=[jax.ShapeDtypeStruct(*shape) for shape in shapes],
        compiler_params=pltpu.CompilerParams(vmem_limit_bytes=32 * MIB),
        cost_estimate=pl.CostEstimate(
            flops=count * tall * side, bytes_accessed=count * tall * side * 2, transcendentals=0
        ),
        name="place",
    )(code, blocks)


def beside(axis):
    count = lax.axis_size(axis)
    up = [(i, i + 1) for i in range(count - 1)]
    return up, [(j, i) for i, j in up]


def neighbours(first, last, axis):
    up, down = beside(axis)
    return lax.ppermute(last, axis, up), lax.ppermute(first, axis, down)


def swapped(array):
    return lax.ppermute(array, "visit", [(0, 1), (1, 0)])


def beyond(strips, above, below):
    first = [strip[:HALO] for strip in strips] + [rows[:, :SIDE] for rows in (above, below)]
    last = [strip[HALO:] for strip in strips] + [rows[:, TX - SIDE :] for rows in (above, below)]
    return neighbours(jnp.concatenate(first, axis=1), jnp.concatenate(last, axis=1), "px")


def rows_between(edge):
    lower = lax.axis_index("visit") == 0
    mine = jnp.where(lower, edge[:HALO], edge[HALO:])
    count = lax.axis_size("py")
    up, down = beside("py")

    def pairs(cross):
        return [(i, j + cross * count) for i, j in down] + [
            (count + i, j + (1 - cross) * count) for i, j in up
        ]

    straight = lax.ppermute(mine, ("visit", "py"), pairs(0))
    crossed = lax.ppermute(mine, ("visit", "py"), pairs(1))
    return jnp.where(lower, crossed, straight), jnp.where(lower, straight, crossed)


def bands(plan, taps):
    tall, margin = plan[0]["tall"], plan[0]["margin"]
    row = jnp.arange(tall, dtype=jnp.int32)
    out = jnp.arange(tall - 2 * margin, dtype=jnp.int32) + margin
    three = (jnp.abs(row[:, None] - row[None, :]) <= 1).astype(jnp.bfloat16)
    nine = (jnp.abs(out[:, None] - row[None, :]) <= 4).astype(jnp.bfloat16)
    count = taps.shape[0]
    ahead = row[None, :] - out[:, None] + count // 2
    coarse, fine = split(sum(jnp.where(ahead == tap, taps[tap], 0.0) for tap in range(count)))
    lane = jnp.arange(4 * SIDE, dtype=jnp.int32)
    across = jnp.abs(lane[:, None] - lane[None, SIDE : 3 * SIDE]) <= 4
    return (
        three,
        nine,
        jnp.concatenate([coarse, coarse, fine], axis=1),
        across.astype(jnp.bfloat16),
    )


def split(value):
    coarse = value.astype(jnp.bfloat16)
    return coarse, (value - coarse.astype(jnp.float32)).astype(jnp.bfloat16)


def filtered(value, taps, tables, margin):
    three, nine, blur, across = [table[...] for table in tables]
    tall = value.shape[0]
    short = tall - 2 * margin

    def product(matrix, terms):
        return jnp.dot(matrix, jnp.concatenate(terms, axis=0), preferred_element_type=jnp.float32)

    moved = {
        by: (pltpu.roll(value, -by % WIDE, 1) if by else value).astype(jnp.float32)
        for by in range(-3, 4)
    }
    rowwise = sum(taps[tap] * moved[tap - 3] for tap in range(7))[:, :TX]
    resid = moved[0] - product(three, [(moved[-1] + moved[0] + moved[1]).astype(jnp.bfloat16)]) * (1.0 / 9.0)
    tower = product(nine, [(resid * resid).astype(jnp.bfloat16)]).astype(jnp.bfloat16)
    windows = [jnp.concatenate([tower[:, TX:], tower[:, : 3 * SIDE]], axis=1)]
    for start in range(2 * SIDE, TX, 2 * SIDE):
        windows.append(tower[:, start - SIDE : start + 3 * SIDE])
    boxes = jnp.dot(jnp.concatenate(windows, axis=0), across, preferred_element_type=jnp.float32)
    box = jnp.concatenate(
        [boxes[at * short : (at + 1) * short] for at in range(len(windows))], axis=1
    )
    local = box * (1.0 / 81.0) + 1e-05
    coarse, fine = split(rowwise)
    return product(blur, (coarse, fine, coarse)) * lax.rsqrt(local), local


def stage_kernel(plan, lots, *refs):
    mine_ref, taps_ref, above_ref, below_ref = refs[:4]
    tables = refs[4:8]
    fields, copies, outs = plan
    visits, margin = fields["visits"], fields["margin"]
    at = 8
    chunks = []
    for lot in lots:
        parts = []
        for _ in range(visits):
            parts.append(refs[at : at + 3])
            at += 3
        chunks.append(parts)
    at += fields["aliased"]
    detection_hbm, variance_hbm = refs[at : at + 2]
    field, detection, variance, sems = refs[at + 2 : at + 6]
    sides = refs[at + 6 :]
    spans, tall, _ = field.shape

    which = 0
    held = []
    for parts in chunks:
        group = []
        for number, (cells, left, right) in enumerate(parts):
            side = sides[which]
            which += 1
            height = cells.shape[0]
            first = number * height if left.shape[1] > height else 0
            here = slice(first, first + height)
            gap = jnp.zeros((SIDE - 2 * HALO, height), jnp.float32)
            side[...] = jnp.concatenate(
                [right[right.shape[0] - HALO :, here], gap, left[:HALO, here]], axis=0
            ).T.astype(jnp.bfloat16)
            group.append((cells, side))
        held.append(group)

    for span, first, rows in fields["blank"]:
        field[span, first : first + rows, :] = jnp.zeros((rows, WIDE), jnp.bfloat16)

    def assemble(order):
        for chunk, visit, first, rows, at_row, begin, end, shift in copies:
            cells, side = held[chunk][order[visit]]
            lot = lots[chunk]

            @pl.loop(begin, end)
            def _(unit):
                start = pl.multiple_of(unit * lot + first, EDGE)
                into = pl.ds(at_row, rows)
                field[unit + shift, into, :TX] = cells[pl.ds(start, rows), :]
                field[unit + shift, into, TX:] = side[pl.ds(start, rows), :]

    if visits == 2:
        for flip in range(2):

            @pl.when(mine_ref[0] == flip)
            def _():
                assemble((0, 1) if flip == 0 else (1, 0))

    else:
        assemble(tuple(range(visits)))

    if fields["between"]:
        _, left, right = chunks[0][0]
        corners = left.shape[1] - 2 * SIDE
        from_left = lax.broadcasted_iota(jnp.int32, (HALO, SIDE), 1) >= SIDE // 2
        none = jnp.zeros((EDGE - HALO, WIDE), jnp.float32)
        for number, (span, first, rows) in enumerate(
            zip((0, spans - 1), fields["between"], (above_ref, below_ref))
        ):
            here = slice(corners + number * SIDE, corners + (number + 1) * SIDE)
            wide = jnp.concatenate(
                [rows[...], jnp.where(from_left, left[:, here], right[:, here])], axis=1
            )
            strip = [none, wide] if number == 0 else [wide, none]
            field[span, first : first + EDGE, :] = jnp.concatenate(strip, axis=0).astype(jnp.bfloat16)

    taps = [taps_ref[tap] for tap in range(7)]

    def stores(unit, source, rows, target):
        return [
            pltpu.make_async_copy(
                scratch.at[unit, pl.ds(source, rows)], hbm.at[pl.ds(target, rows)], sems.at[unit, at]
            )
            for at, (scratch, hbm) in enumerate(
                ((detection, detection_hbm), (variance, variance_hbm))
            )
        ]

    some = next(count for count in (4, 3, 2, 1) if spans % count == 0 and count * tall <= 320)

    @pl.loop(0, spans, step=some)
    def _(first):
        for ahead in range(some):
            unit = first + ahead
            detection[unit], variance[unit] = filtered(field[unit], taps, tables, margin)
        for ahead in range(some):
            unit = first + ahead
            for begin, end, source, rows, shift in outs:

                @pl.when((unit >= begin) & (unit < end))
                def _():
                    target = pl.multiple_of(unit * STEP + shift, HALO)
                    for store in stores(unit, source, rows, target):
                        store.start()

    @pl.loop(0, spans)
    def _(unit):
        for begin, end, source, rows, shift in outs:

            @pl.when((unit >= begin) & (unit < end))
            def _():
                for store in stores(unit, source, rows, 0):
                    store.wait()


def stage(plan, mine, taps, between, tables, chunks, lots, held=()):
    fields, _, _ = plan
    spans, tall = fields["spans"], fields["tall"]
    shape = jax.ShapeDtypeStruct((TY, TX), jnp.float32)
    flat = [array for parts in chunks for part in parts for array in part]
    first = 8 + len(flat)
    out = pltpu.VMEM((spans, tall - 2 * fields["margin"], TX), jnp.float32)
    return pl.pallas_call(
        functools.partial(stage_kernel, plan, lots),
        out_shape=(shape, shape),
        in_specs=[SMEM, SMEM] + [VMEM] * (6 + len(flat)) + [HBM] * len(held),
        out_specs=(HBM, HBM),
        input_output_aliases={first + at: at for at in range(len(held))},
        scratch_shapes=[
            pltpu.VMEM((spans, tall, WIDE), jnp.bfloat16),
            out,
            out,
            pltpu.SemaphoreType.DMA((spans, 2)),
        ]
        + [pltpu.VMEM((part[0].shape[0], SIDE), jnp.bfloat16) for parts in chunks for part in parts],
        compiler_params=pltpu.CompilerParams(vmem_limit_bytes=32 * MIB),
        cost_estimate=pl.CostEstimate(
            flops=80 * spans * tall * WIDE, bytes_accessed=12 * spans * tall * WIDE, transcendentals=0
        ),
        name="stage",
    )(mine, taps, *between, *tables, *flat, *held)


def outer_plan(lot):
    fields = dict(
        visits=2, aliased=0, spans=UNITS + 1, tall=2 * lot, margin=HALO, between=(lot - EDGE, lot),
        blank=[(0, 0, lot - EDGE), (UNITS, lot + EDGE, lot - EDGE)],
    )
    copies = [(0, 1, 0, lot, 0, 0, UNITS, 1), (0, 0, 0, lot, lot, 0, UNITS, 0)]
    rows = lot - HALO
    outs = [
        (0, 1, rows, rows, 0),
        (1, UNITS, 0, 2 * rows, -rows),
        (UNITS, UNITS + 1, 0, rows, -rows),
    ]
    return fields, copies, outs


def inner_plan(lot, inner):
    tall = 2 * inner + 2 * EDGE
    fields = dict(
        visits=2, aliased=2, spans=UNITS, tall=tall, margin=HALO, between=None, blank=[]
    )
    copies = [
        (0, 0, lot - EDGE, EDGE, 0, 0, UNITS, 0),
        (1, 0, 0, inner, EDGE, 0, UNITS, 0),
        (1, 1, 0, inner, EDGE + inner, 0, UNITS, 0),
        (0, 1, 0, EDGE, EDGE + 2 * inner, 0, UNITS, 0),
    ]
    return fields, copies, [(0, UNITS, 0, tall - 2 * HALO, lot - HALO)]


def whole_plan(lot, visits):
    fields = dict(
        visits=visits, aliased=0, spans=UNITS, tall=STEP + 2 * EDGE, margin=EDGE,
        between=(0, EDGE + STEP), blank=[],
    )
    copies = [(0, visit, 0, lot, EDGE + visit * lot, 0, UNITS, 0) for visit in range(visits)]
    copies.append((0, visits - 1, lot - EDGE, EDGE, 0, 0, UNITS - 1, 1))
    copies.append((0, 0, 0, EDGE, EDGE + STEP, 1, UNITS, -1))
    return fields, copies, [(0, UNITS, 0, STEP, 0)]


def per_device(
    images, inv_var, good_columns, warp_rows, warp_cols, block_visit, dest_tile, offsets, psf_taps
):
    tiles = lax.axis_size("py") * lax.axis_size("px")
    visits = lax.axis_size("visit")
    plan = shares(visits)
    lots = [rows for rows, _ in plan]
    mine = lax.axis_index("visit").astype(jnp.int32).reshape(1)

    def make(chunk, var):
        return warp(
            tiles, plan[chunk], chunk == 0, block_visit, dest_tile[:, 0], offsets.T,
            good_columns, warp_rows, warp_cols, var, images,
        )

    def send(blocks):
        return lax.all_to_all(blocks, EVERY, split_axis=0, concat_axis=0, tiled=True)

    made, psf_taps = lax.optimization_barrier((make(0, inv_var), psf_taps))
    arrived = send(made)
    if len(plan) == 1:
        every = whole_plan(lots[0], visits)
        coadd, strip, edge = place(codes(arrived), arrived, lots[0])
        all_of = [lax.all_gather(part, "visit") for part in (coadd, strip, edge)]
        between = neighbours(all_of[2][0, :HALO], all_of[2][visits - 1, HALO:], "py")
        sides = beyond([all_of[1][visit] for visit in range(visits)], *between)
        parts = [(all_of[0][visit], *sides) for visit in range(visits)]
        return stage(every, mine, psf_taps, between, bands(every, psf_taps), [parts], lots)

    outer, inner = outer_plan(lots[0]), inner_plan(*lots)
    tables, inv_var = lax.optimization_barrier(
        ([bands(part, psf_taps) for part in (outer, inner)], inv_var)
    )
    arrived, later = lax.optimization_barrier((arrived, make(1, inv_var)))
    second = send(later)
    code = codes(arrived)
    coadd, strip, edge = place(code, arrived, lots[0])
    between, other_strip = rows_between(edge), swapped(strip)
    coadd, between, other_strip = lax.optimization_barrier((coadd, between, other_strip))
    sides = beyond([strip, other_strip], *between)
    other = swapped(coadd)
    second, sides, other = lax.optimization_barrier((second, sides, other))
    parts = [(coadd, *sides), (other, *sides)]
    coadd, strip, _ = place(code, second, lots[1])
    other = swapped(coadd)
    near = neighbours(strip[:HALO], strip[HALO:], "px")
    (parts, between), _ = lax.optimization_barrier(((parts, between), coadd))
    held = stage(outer, mine, psf_taps, between, tables[0], [parts], lots[:1])
    far = swapped(jnp.concatenate(near, axis=0))
    more = [(coadd, *near), (other, far, far)]
    return stage(inner, mine, psf_taps, between, tables[1], [parts, more], lots, held)


def codes(arrived):
    note = arrived[:, arrived.shape[1] - NOTE, :: SIDE // CAP]
    return note.astype(jnp.float32).astype(jnp.int32).reshape(-1)


def solution(mesh):
    in_specs = (
        P(EVERY, None, None),
        P(EVERY, None, None),
        P("visit", None),
        P("visit", None, None),
        P("visit", None, None),
        P(EVERY),
        P(EVERY, None),
        P(EVERY, None),
        P(),
    )
    out_specs = (P("py", "px"), P("py", "px"))
    return jax.shard_map(
        per_device, mesh=mesh, in_specs=in_specs, out_specs=out_specs, check_vma=False
    )
```

```python
import functools

import jax
import jax.numpy as jnp
from jax import lax
from jax.experimental import pallas as pl
from jax.experimental.pallas import tpu as pltpu
from jax.sharding import PartitionSpec as P

TY = 1024
TX = 1024
STEP = 128
CAP = 2
UNITS = TY // STEP
HALO = 8
EDGE = 16
SIDE = 128
WIDE = TX + SIDE
GROUP = 8
NOTE = 16
MIB = 1 << 20
EVERY = ("visit", "py", "px")
HBM = pl.BlockSpec(memory_space=pltpu.HBM)
SMEM = pl.BlockSpec(memory_space=pltpu.SMEM)
VMEM = pl.BlockSpec(memory_space=pltpu.VMEM)


def shares(visits):
    if visits == 2:
        edge, inner = 48, 16
        return [(edge, (0, STEP - edge)), (inner, (edge, edge + inner))]
    rows = STEP // visits
    return [(rows, tuple(visit * rows for visit in range(visits)))]


def warp_kernel(
    tiles, share, noted, visit_ref, tile_ref, offset_ref, good_ref, rows_hbm, cols_hbm, var_hbm,
    image_hbm, out_hbm, rows, cols, var, image, done, note, count, table_sems, sems, out_sems,
):
    blocks, side, _ = var.shape
    some, firsts = share
    groups = blocks // GROUP
    slot_rows = done.shape[2]
    tables = [
        pltpu.make_async_copy(rows_hbm, rows, table_sems.at[0]),
        pltpu.make_async_copy(cols_hbm, cols, table_sems.at[1]),
    ]

    def loads(group):
        span = pl.ds(group * GROUP, GROUP)
        return (
            pltpu.make_async_copy(var_hbm.at[span], var.at[span], sems.at[group, 0]),
            pltpu.make_async_copy(image_hbm.at[span], image.at[span], sems.at[group, 1]),
        )

    for load in tables:
        load.start()
    for group in range(groups):
        for load in loads(group):
            load.start()

    @pl.loop(0, tiles)
    def _(tile):
        count[tile] = 0

    if noted:
        note[...] = jnp.full(note.shape, -1, jnp.bfloat16)
        slot_of_lane = lax.broadcasted_iota(jnp.int32, (NOTE, SIDE), 1) // (SIDE // CAP)

    for load in tables:
        load.wait()

    strips = [first + strip * STEP for first in firsts for strip in range(side // STEP)]
    tall = some * len(strips)
    part = tall // len(firsts)

    @pl.loop(0, groups)
    def _(group):
        for load in loads(group):
            load.wait()
        visits = [visit_ref[group * GROUP + ahead] for ahead in range(GROUP)]
        planes, turned, warped = [], [], []
        for ahead in range(GROUP):
            block = group * GROUP + ahead
            good = good_ref[pl.ds(visits[ahead], 1), :].astype(jnp.float32)
            weight = var[block].astype(jnp.float32) * good
            data = weight * image[block].astype(jnp.float32)
            planes.append(
                jnp.concatenate([data.astype(jnp.bfloat16), weight.astype(jnp.bfloat16)], axis=1)
            )
        for ahead in range(GROUP):
            matrix = jnp.concatenate(
                [rows[visits[ahead], first : first + some, :] for first in strips], axis=0
            )
            turned.append(
                jnp.dot(matrix, planes[ahead], preferred_element_type=jnp.float32).astype(jnp.bfloat16)
            )
        for ahead in range(GROUP):
            both = jnp.concatenate([turned[ahead][:, :side], turned[ahead][:, side:]], axis=0)
            warped.append(
                lax.dot_general(
                    both,
                    cols[visits[ahead]],
                    (((1,), (1,)), ((), ())),
                    preferred_element_type=jnp.float32,
                ).astype(jnp.bfloat16)
            )
        for ahead in range(GROUP):
            block = group * GROUP + ahead
            for visit in range(len(firsts)):
                for half in range(side // SIDE):
                    for plane in range(2):
                        start = plane * tall + visit * part
                        into = (2 * half + plane) * part
                        done[block, visit, into : into + part, :] = warped[ahead][
                            start : start + part, half * SIDE : (half + 1) * SIDE
                        ]
        for ahead in range(GROUP):
            block = group * GROUP + ahead
            tile = tile_ref[block]
            rank = count[tile]
            count[tile] = rank + 1
            for visit in range(len(firsts)):
                target = visit * tiles + tile
                pltpu.make_async_copy(
                    done.at[block, visit],
                    out_hbm.at[target, pl.ds(pl.multiple_of(rank * slot_rows, NOTE), slot_rows)],
                    out_sems.at[block, visit],
                ).start()
                if noted:
                    code = offset_ref[0, block] * 8 + offset_ref[1, block]
                    note[target] = jnp.where(
                        slot_of_lane == rank, code.astype(jnp.float32), note[target].astype(jnp.float32)
                    ).astype(jnp.bfloat16)

    if noted:
        notes = pltpu.make_async_copy(
            note, out_hbm.at[:, pl.ds(CAP * slot_rows, NOTE)], table_sems.at[0]
        )
        notes.start()

    @pl.loop(0, blocks)
    def _(block):
        for visit in range(len(firsts)):
            pltpu.make_async_copy(
                done.at[block, visit], out_hbm.at[0, pl.ds(0, slot_rows)], out_sems.at[block, visit]
            ).wait()

    if noted:
        notes.wait()


def warp(tiles, share, noted, visit, tile, offset, good, rows, cols, var, image):
    blocks, side, _ = var.shape
    some, firsts = share
    slot_rows = 2 * (side // STEP) * some * (side // SIDE)
    visits = len(firsts)
    return pl.pallas_call(
        functools.partial(warp_kernel, tiles, share, noted),
        out_shape=jax.ShapeDtypeStruct(
            (visits * tiles, CAP * slot_rows + noted * NOTE, SIDE), jnp.bfloat16
        ),
        in_specs=[SMEM, SMEM, SMEM, VMEM, HBM, HBM, HBM, HBM],
        out_specs=HBM,
        scratch_shapes=[
            pltpu.VMEM(rows.shape, jnp.bfloat16),
            pltpu.VMEM(cols.shape, jnp.bfloat16),
            pltpu.VMEM(var.shape, jnp.bfloat16),
            pltpu.VMEM(var.shape, jnp.bfloat16),
            pltpu.VMEM((blocks, visits, slot_rows, SIDE), jnp.bfloat16),
            pltpu.VMEM((visits * tiles, NOTE, SIDE), jnp.bfloat16),
            pltpu.SMEM((tiles,), jnp.int32),
            pltpu.SemaphoreType.DMA((2,)),
            pltpu.SemaphoreType.DMA((blocks // GROUP, 2)),
            pltpu.SemaphoreType.DMA((blocks, visits)),
        ],
        compiler_params=pltpu.CompilerParams(vmem_limit_bytes=60 * MIB),
        cost_estimate=pl.CostEstimate(
            flops=8 * blocks * side**3, bytes_accessed=8 * blocks * side**2, transcendentals=0
        ),
        name="warp",
    )(visit, tile, offset, good, rows, cols, var, image)


def place_kernel(part, code_ref, blocks_ref, coadd_ref, strip_ref, edge_ref, data, weight):
    step = pl.program_id(0)
    some = blocks_ref.shape[0]
    height = data.shape[0]
    lot = height // UNITS

    @pl.when(step == 0)
    def _():
        data[...] = jnp.zeros_like(data)
        weight[...] = jnp.zeros_like(weight)

    for block in range(some):
        for slot in range(CAP):
            code = code_ref[(step * some + block) * CAP + slot]

            @pl.when(code >= 0)
            def _():
                row = pl.multiple_of((code // 8) * lot, lot)
                for half in range(2):
                    col = pl.multiple_of((code % 8 + half) * STEP, STEP)
                    cells = (pl.ds(row, part), pl.ds(col, STEP))
                    first = (slot * 2 + half) * 2 * part
                    data[cells] += blocks_ref[block, first : first + part].astype(jnp.float32)
                    weight[cells] += blocks_ref[block, first + part : first + 2 * part].astype(
                        jnp.float32
                    )

    @pl.when(step == pl.num_programs(0) - 1)
    def _():
        coadd = data[...] / jnp.maximum(weight[...], 1.0)
        coadd_ref[...] = coadd.astype(coadd_ref.dtype)
        strip_ref[:HALO] = coadd[:, :SIDE].T[:HALO]
        strip_ref[HALO:] = coadd[:, TX - SIDE :].T[SIDE - HALO :]
        edge_ref[:HALO] = coadd[:HALO]
        edge_ref[HALO:] = coadd[height - HALO :]


def place(code, blocks, lot):
    count, tall, side = blocks.shape
    some = 4
    height = lot * UNITS
    shapes = [((height, TX), jnp.bfloat16), ((2 * HALO, height), jnp.float32), ((2 * HALO, TX), jnp.float32)]
    return pl.pallas_call(
        functools.partial(place_kernel, 2 * lot),
        grid_spec=pltpu.PrefetchScalarGridSpec(
            num_scalar_prefetch=1,
            grid=(count // some,),
            in_specs=[pl.BlockSpec((some, tall, side), lambda step, code: (step, 0, 0))],
            out_specs=[pl.BlockSpec(shape, lambda step, code: (0, 0)) for shape, _ in shapes],
            scratch_shapes=[pltpu.VMEM((height, TX), jnp.float32)] * 2,
        ),
        out_shape=[jax.ShapeDtypeStruct(*shape) for shape in shapes],
        compiler_params=pltpu.CompilerParams(vmem_limit_bytes=32 * MIB),
        cost_estimate=pl.CostEstimate(
            flops=count * tall * side, bytes_accessed=count * tall * side * 2, transcendentals=0
        ),
        name="place",
    )(code, blocks)


def beside(axis):
    count = lax.axis_size(axis)
    up = [(i, i + 1) for i in range(count - 1)]
    return up, [(j, i) for i, j in up]


def neighbours(first, last, axis):
    up, down = beside(axis)
    return lax.ppermute(last, axis, up), lax.ppermute(first, axis, down)


def swapped(array):
    return lax.ppermute(array, "visit", [(0, 1), (1, 0)])


def beyond(strips, above, below):
    first = [strip[:HALO] for strip in strips] + [rows[:, :SIDE] for rows in (above, below)]
    last = [strip[HALO:] for strip in strips] + [rows[:, TX - SIDE :] for rows in (above, below)]
    return neighbours(jnp.concatenate(first, axis=1), jnp.concatenate(last, axis=1), "px")


def rows_between(edge):
    lower = lax.axis_index("visit") == 0
    mine = jnp.where(lower, edge[:HALO], edge[HALO:])
    count = lax.axis_size("py")
    up, down = beside("py")

    def pairs(cross):
        return [(i, j + cross * count) for i, j in down] + [
            (count + i, j + (1 - cross) * count) for i, j in up
        ]

    straight = lax.ppermute(mine, ("visit", "py"), pairs(0))
    crossed = lax.ppermute(mine, ("visit", "py"), pairs(1))
    return jnp.where(lower, crossed, straight), jnp.where(lower, straight, crossed)


def bands(plan, taps):
    tall, margin = plan[0]["tall"], plan[0]["margin"]
    row = jnp.arange(tall, dtype=jnp.int32)
    out = jnp.arange(tall - 2 * margin, dtype=jnp.int32) + margin
    three = (jnp.abs(row[:, None] - row[None, :]) <= 1).astype(jnp.bfloat16)
    nine = (jnp.abs(out[:, None] - row[None, :]) <= 4).astype(jnp.bfloat16)
    count = taps.shape[0]
    ahead = row[None, :] - out[:, None] + count // 2
    coarse, fine = split(sum(jnp.where(ahead == tap, taps[tap], 0.0) for tap in range(count)))
    lane = jnp.arange(4 * SIDE, dtype=jnp.int32)
    across = jnp.abs(lane[:, None] - lane[None, SIDE : 3 * SIDE]) <= 4
    return (
        three,
        nine,
        jnp.concatenate([coarse, coarse, fine], axis=1),
        across.astype(jnp.bfloat16),
    )


def split(value):
    coarse = value.astype(jnp.bfloat16)
    return coarse, (value - coarse.astype(jnp.float32)).astype(jnp.bfloat16)


def filtered(value, taps, tables, margin):
    three, nine, blur, across = [table[...] for table in tables]
    tall = value.shape[0]
    short = tall - 2 * margin

    def product(matrix, terms):
        return jnp.dot(matrix, jnp.concatenate(terms, axis=0), preferred_element_type=jnp.float32)

    moved = {
        by: (pltpu.roll(value, -by % WIDE, 1) if by else value).astype(jnp.float32)
        for by in range(-3, 4)
    }
    rowwise = sum(taps[tap] * moved[tap - 3] for tap in range(7))[:, :TX]
    resid = moved[0] - product(three, [(moved[-1] + moved[0] + moved[1]).astype(jnp.bfloat16)]) * (1.0 / 9.0)
    tower = product(nine, [(resid * resid).astype(jnp.bfloat16)]).astype(jnp.bfloat16)
    windows = [jnp.concatenate([tower[:, TX:], tower[:, : 3 * SIDE]], axis=1)]
    for start in range(2 * SIDE, TX, 2 * SIDE):
        windows.append(tower[:, start - SIDE : start + 3 * SIDE])
    boxes = jnp.dot(jnp.concatenate(windows, axis=0), across, preferred_element_type=jnp.float32)
    box = jnp.concatenate(
        [boxes[at * short : (at + 1) * short] for at in range(len(windows))], axis=1
    )
    local = box * (1.0 / 81.0) + 1e-05
    coarse, fine = split(rowwise)
    return product(blur, (coarse, fine, coarse)) * lax.rsqrt(local), local


def stage_kernel(plan, lots, *refs):
    mine_ref, taps_ref, above_ref, below_ref = refs[:4]
    tables = refs[4:8]
    fields, copies, outs = plan
    visits, margin = fields["visits"], fields["margin"]
    at = 8
    chunks = []
    for lot in lots:
        parts = []
        for _ in range(visits):
            parts.append(refs[at : at + 3])
            at += 3
        chunks.append(parts)
    at += fields["aliased"]
    detection_hbm, variance_hbm = refs[at : at + 2]
    field, detection, variance, sems = refs[at + 2 : at + 6]
    sides = refs[at + 6 :]
    spans, tall, _ = field.shape

    which = 0
    held = []
    for parts in chunks:
        group = []
        for number, (cells, left, right) in enumerate(parts):
            side = sides[which]
            which += 1
            height = cells.shape[0]
            first = number * height if left.shape[1] > height else 0
            here = slice(first, first + height)
            gap = jnp.zeros((SIDE - 2 * HALO, height), jnp.float32)
            side[...] = jnp.concatenate(
                [right[right.shape[0] - HALO :, here], gap, left[:HALO, here]], axis=0
            ).T.astype(jnp.bfloat16)
            group.append((cells, side))
        held.append(group)

    for span, first, rows in fields["blank"]:
        field[span, first : first + rows, :] = jnp.zeros((rows, WIDE), jnp.bfloat16)

    def assemble(order):
        for chunk, visit, first, rows, at_row, begin, end, shift in copies:
            cells, side = held[chunk][order[visit]]
            lot = lots[chunk]

            @pl.loop(begin, end)
            def _(unit):
                start = pl.multiple_of(unit * lot + first, EDGE)
                into = pl.ds(at_row, rows)
                field[unit + shift, into, :TX] = cells[pl.ds(start, rows), :]
                field[unit + shift, into, TX:] = side[pl.ds(start, rows), :]

    if visits == 2:
        for flip in range(2):

            @pl.when(mine_ref[0] == flip)
            def _():
                assemble((0, 1) if flip == 0 else (1, 0))

    else:
        assemble(tuple(range(visits)))

    if fields["between"]:
        _, left, right = chunks[0][0]
        corners = left.shape[1] - 2 * SIDE
        from_left = lax.broadcasted_iota(jnp.int32, (HALO, SIDE), 1) >= SIDE // 2
        none = jnp.zeros((EDGE - HALO, WIDE), jnp.float32)
        for number, (span, first, rows) in enumerate(
            zip((0, spans - 1), fields["between"], (above_ref, below_ref))
        ):
            here = slice(corners + number * SIDE, corners + (number + 1) * SIDE)
            wide = jnp.concatenate(
                [rows[...], jnp.where(from_left, left[:, here], right[:, here])], axis=1
            )
            strip = [none, wide] if number == 0 else [wide, none]
            field[span, first : first + EDGE, :] = jnp.concatenate(strip, axis=0).astype(jnp.bfloat16)

    taps = [taps_ref[tap] for tap in range(7)]

    def stores(unit, source, rows, target):
        return [
            pltpu.make_async_copy(
                scratch.at[unit, pl.ds(source, rows)], hbm.at[pl.ds(target, rows)], sems.at[unit, at]
            )
            for at, (scratch, hbm) in enumerate(
                ((detection, detection_hbm), (variance, variance_hbm))
            )
        ]

    some = next(count for count in (4, 3, 2, 1) if spans % count == 0 and count * tall <= 320)

    @pl.loop(0, spans, step=some)
    def _(first):
        for ahead in range(some):
            unit = first + ahead
            detection[unit], variance[unit] = filtered(field[unit], taps, tables, margin)
        for ahead in range(some):
            unit = first + ahead
            for begin, end, source, rows, shift in outs:

                @pl.when((unit >= begin) & (unit < end))
                def _():
                    target = pl.multiple_of(unit * STEP + shift, HALO)
                    for store in stores(unit, source, rows, target):
                        store.start()

    @pl.loop(0, spans)
    def _(unit):
        for begin, end, source, rows, shift in outs:

            @pl.when((unit >= begin) & (unit < end))
            def _():
                for store in stores(unit, source, rows, 0):
                    store.wait()


def stage(plan, mine, taps, between, tables, chunks, lots, held=()):
    fields, _, _ = plan
    spans, tall = fields["spans"], fields["tall"]
    shape = jax.ShapeDtypeStruct((TY, TX), jnp.float32)
    flat = [array for parts in chunks for part in parts for array in part]
    first = 8 + len(flat)
    out = pltpu.VMEM((spans, tall - 2 * fields["margin"], TX), jnp.float32)
    return pl.pallas_call(
        functools.partial(stage_kernel, plan, lots),
        out_shape=(shape, shape),
        in_specs=[SMEM, SMEM] + [VMEM] * (6 + len(flat)) + [HBM] * len(held),
        out_specs=(HBM, HBM),
        input_output_aliases={first + at: at for at in range(len(held))},
        scratch_shapes=[
            pltpu.VMEM((spans, tall, WIDE), jnp.bfloat16),
            out,
            out,
            pltpu.SemaphoreType.DMA((spans, 2)),
        ]
        + [pltpu.VMEM((part[0].shape[0], SIDE), jnp.bfloat16) for parts in chunks for part in parts],
        compiler_params=pltpu.CompilerParams(vmem_limit_bytes=32 * MIB),
        cost_estimate=pl.CostEstimate(
            flops=80 * spans * tall * WIDE, bytes_accessed=12 * spans * tall * WIDE, transcendentals=0
        ),
        name="stage",
    )(mine, taps, *between, *tables, *flat, *held)


def outer_plan(lot):
    fields = dict(
        visits=2, aliased=0, spans=UNITS + 1, tall=2 * lot, margin=HALO, between=(lot - EDGE, lot),
        blank=[(0, 0, lot - EDGE), (UNITS, lot + EDGE, lot - EDGE)],
    )
    copies = [(0, 1, 0, lot, 0, 0, UNITS, 1), (0, 0, 0, lot, lot, 0, UNITS, 0)]
    rows = lot - HALO
    outs = [
        (0, 1, rows, rows, 0),
        (1, UNITS, 0, 2 * rows, -rows),
        (UNITS, UNITS + 1, 0, rows, -rows),
    ]
    return fields, copies, outs


def inner_plan(lot, inner):
    tall = 2 * inner + 2 * EDGE
    fields = dict(
        visits=2, aliased=2, spans=UNITS, tall=tall, margin=HALO, between=None, blank=[]
    )
    copies = [
        (0, 0, lot - EDGE, EDGE, 0, 0, UNITS, 0),
        (1, 0, 0, inner, EDGE, 0, UNITS, 0),
        (1, 1, 0, inner, EDGE + inner, 0, UNITS, 0),
        (0, 1, 0, EDGE, EDGE + 2 * inner, 0, UNITS, 0),
    ]
    return fields, copies, [(0, UNITS, 0, tall - 2 * HALO, lot - HALO)]


def whole_plan(lot, visits):
    fields = dict(
        visits=visits, aliased=0, spans=UNITS, tall=STEP + 2 * EDGE, margin=EDGE,
        between=(0, EDGE + STEP), blank=[],
    )
    copies = [(0, visit, 0, lot, EDGE + visit * lot, 0, UNITS, 0) for visit in range(visits)]
    copies.append((0, visits - 1, lot - EDGE, EDGE, 0, 0, UNITS - 1, 1))
    copies.append((0, 0, 0, EDGE, EDGE + STEP, 1, UNITS, -1))
    return fields, copies, [(0, UNITS, 0, STEP, 0)]


def per_device(
    images, inv_var, good_columns, warp_rows, warp_cols, block_visit, dest_tile, offsets, psf_taps
):
    tiles = lax.axis_size("py") * lax.axis_size("px")
    visits = lax.axis_size("visit")
    plan = shares(visits)
    lots = [rows for rows, _ in plan]
    mine = lax.axis_index("visit").astype(jnp.int32).reshape(1)

    def make(chunk, var):
        return warp(
            tiles, plan[chunk], chunk == 0, block_visit, dest_tile[:, 0], offsets.T,
            good_columns, warp_rows, warp_cols, var, images,
        )

    def send(blocks):
        return lax.all_to_all(blocks, EVERY, split_axis=0, concat_axis=0, tiled=True)

    made, psf_taps = lax.optimization_barrier((make(0, inv_var), psf_taps))
    arrived = send(made)
    if len(plan) == 1:
        every = whole_plan(lots[0], visits)
        coadd, strip, edge = place(codes(arrived), arrived, lots[0])
        all_of = [lax.all_gather(part, "visit") for part in (coadd, strip, edge)]
        between = neighbours(all_of[2][0, :HALO], all_of[2][visits - 1, HALO:], "py")
        sides = beyond([all_of[1][visit] for visit in range(visits)], *between)
        parts = [(all_of[0][visit], *sides) for visit in range(visits)]
        return stage(every, mine, psf_taps, between, bands(every, psf_taps), [parts], lots)

    outer, inner = outer_plan(lots[0]), inner_plan(*lots)
    tables, inv_var = lax.optimization_barrier(
        ([bands(part, psf_taps) for part in (outer, inner)], inv_var)
    )
    arrived, later = lax.optimization_barrier((arrived, make(1, inv_var)))
    second = send(later)
    code = codes(arrived)
    coadd, strip, edge = place(code, arrived, lots[0])
    between, other_strip = rows_between(edge), swapped(strip)
    coadd, between, other_strip = lax.optimization_barrier((coadd, between, other_strip))
    sides = beyond([strip, other_strip], *between)
    other = swapped(coadd)
    second, sides = lax.optimization_barrier((second, sides))
    parts = [(coadd, *sides), (other, *sides)]
    coadd, strip, _ = place(code, second, lots[1])
    other = swapped(coadd)
    near = neighbours(strip[:HALO], strip[HALO:], "px")
    (parts, between), _ = lax.optimization_barrier(((parts, between), coadd))
    held = stage(outer, mine, psf_taps, between, tables[0], [parts], lots[:1])
    far = swapped(jnp.concatenate(near, axis=0))
    more = [(coadd, *near), (other, far, far)]
    return stage(inner, mine, psf_taps, between, tables[1], [parts, more], lots, held)


def codes(arrived):
    note = arrived[:, arrived.shape[1] - NOTE, :: SIDE // CAP]
    return note.astype(jnp.float32).astype(jnp.int32).reshape(-1)


def solution(mesh):
    in_specs = (
        P(EVERY, None, None),
        P(EVERY, None, None),
        P("visit", None),
        P("visit", None, None),
        P("visit", None, None),
        P(EVERY),
        P(EVERY, None),
        P(EVERY, None),
        P(),
    )
    out_specs = (P("py", "px"), P("py", "px"))
    return jax.shard_map(
        per_device, mesh=mesh, in_specs=in_specs, out_specs=out_specs, check_vma=False
    )
```

```python
import functools

import jax
import jax.numpy as jnp
from jax import lax
from jax.experimental import pallas as pl
from jax.experimental.pallas import tpu as pltpu
from jax.sharding import PartitionSpec as P

TY = 1024
TX = 1024
STEP = 128
CAP = 2
UNITS = TY // STEP
HALO = 8
EDGE = 16
SIDE = 128
WIDE = TX + SIDE
GROUP = 8
NOTE = 16
MIB = 1 << 20
EVERY = ("visit", "py", "px")
HBM = pl.BlockSpec(memory_space=pltpu.HBM)
SMEM = pl.BlockSpec(memory_space=pltpu.SMEM)
VMEM = pl.BlockSpec(memory_space=pltpu.VMEM)


def shares(visits):
    if visits == 2:
        edge, inner = 48, 16
        return [(edge, (0, STEP - edge)), (inner, (edge, edge + inner))]
    rows = STEP // visits
    return [(rows, tuple(visit * rows for visit in range(visits)))]


def warp_kernel(
    tiles, share, noted, visit_ref, tile_ref, offset_ref, good_ref, rows_hbm, cols_hbm, var_hbm,
    image_hbm, out_hbm, rows, cols, var, image, done, note, count, table_sems, sems, out_sems,
):
    blocks, side, _ = var.shape
    some, firsts = share
    groups = blocks // GROUP
    slot_rows = done.shape[2]
    tables = [
        pltpu.make_async_copy(rows_hbm, rows, table_sems.at[0]),
        pltpu.make_async_copy(cols_hbm, cols, table_sems.at[1]),
    ]

    def loads(group):
        span = pl.ds(group * GROUP, GROUP)
        return (
            pltpu.make_async_copy(var_hbm.at[span], var.at[span], sems.at[group, 0]),
            pltpu.make_async_copy(image_hbm.at[span], image.at[span], sems.at[group, 1]),
        )

    for load in tables:
        load.start()
    for group in range(groups):
        for load in loads(group):
            load.start()

    @pl.loop(0, tiles)
    def _(tile):
        count[tile] = 0

    if noted:
        note[...] = jnp.full(note.shape, -1, jnp.bfloat16)
        slot_of_lane = lax.broadcasted_iota(jnp.int32, (NOTE, SIDE), 1) // (SIDE // CAP)

    for load in tables:
        load.wait()

    strips = [first + strip * STEP for first in firsts for strip in range(side // STEP)]
    tall = some * len(strips)
    part = tall // len(firsts)

    @pl.loop(0, groups)
    def _(group):
        for load in loads(group):
            load.wait()
        visits = [visit_ref[group * GROUP + ahead] for ahead in range(GROUP)]
        planes, turned, warped = [], [], []
        for ahead in range(GROUP):
            block = group * GROUP + ahead
            good = good_ref[pl.ds(visits[ahead], 1), :].astype(jnp.float32)
            weight = var[block].astype(jnp.float32) * good
            data = weight * image[block].astype(jnp.float32)
            planes.append(
                jnp.concatenate([data.astype(jnp.bfloat16), weight.astype(jnp.bfloat16)], axis=1)
            )
        for ahead in range(GROUP):
            matrix = jnp.concatenate(
                [rows[visits[ahead], first : first + some, :] for first in strips], axis=0
            )
            turned.append(
                jnp.dot(matrix, planes[ahead], preferred_element_type=jnp.float32).astype(jnp.bfloat16)
            )
        for ahead in range(GROUP):
            both = jnp.concatenate([turned[ahead][:, :side], turned[ahead][:, side:]], axis=0)
            warped.append(
                lax.dot_general(
                    both,
                    cols[visits[ahead]],
                    (((1,), (1,)), ((), ())),
                    preferred_element_type=jnp.float32,
                ).astype(jnp.bfloat16)
            )
        for ahead in range(GROUP):
            block = group * GROUP + ahead
            for visit in range(len(firsts)):
                for half in range(side // SIDE):
                    for plane in range(2):
                        start = plane * tall + visit * part
                        into = (2 * half + plane) * part
                        done[block, visit, into : into + part, :] = warped[ahead][
                            start : start + part, half * SIDE : (half + 1) * SIDE
                        ]
        for ahead in range(GROUP):
            block = group * GROUP + ahead
            tile = tile_ref[block]
            rank = count[tile]
            count[tile] = rank + 1
            for visit in range(len(firsts)):
                target = visit * tiles + tile
                pltpu.make_async_copy(
                    done.at[block, visit],
                    out_hbm.at[target, pl.ds(pl.multiple_of(rank * slot_rows, NOTE), slot_rows)],
                    out_sems.at[block, visit],
                ).start()
                if noted:
                    code = offset_ref[0, block] * 8 + offset_ref[1, block]
                    note[target] = jnp.where(
                        slot_of_lane == rank, code.astype(jnp.float32), note[target].astype(jnp.float32)
                    ).astype(jnp.bfloat16)

    if noted:
        notes = pltpu.make_async_copy(
            note, out_hbm.at[:, pl.ds(CAP * slot_rows, NOTE)], table_sems.at[0]
        )
        notes.start()

    @pl.loop(0, blocks)
    def _(block):
        for visit in range(len(firsts)):
            pltpu.make_async_copy(
                done.at[block, visit], out_hbm.at[0, pl.ds(0, slot_rows)], out_sems.at[block, visit]
            ).wait()

    if noted:
        notes.wait()


def warp(tiles, share, noted, visit, tile, offset, good, rows, cols, var, image):
    blocks, side, _ = var.shape
    some, firsts = share
    slot_rows = 2 * (side // STEP) * some * (side // SIDE)
    visits = len(firsts)
    return pl.pallas_call(
        functools.partial(warp_kernel, tiles, share, noted),
        out_shape=jax.ShapeDtypeStruct(
            (visits * tiles, CAP * slot_rows + noted * NOTE, SIDE), jnp.bfloat16
        ),
        in_specs=[SMEM, SMEM, SMEM, VMEM, HBM, HBM, HBM, HBM],
        out_specs=HBM,
        scratch_shapes=[
            pltpu.VMEM(rows.shape, jnp.bfloat16),
            pltpu.VMEM(cols.shape, jnp.bfloat16),
            pltpu.VMEM(var.shape, jnp.bfloat16),
            pltpu.VMEM(var.shape, jnp.bfloat16),
            pltpu.VMEM((blocks, visits, slot_rows, SIDE), jnp.bfloat16),
            pltpu.VMEM((visits * tiles, NOTE, SIDE), jnp.bfloat16),
            pltpu.SMEM((tiles,), jnp.int32),
            pltpu.SemaphoreType.DMA((2,)),
            pltpu.SemaphoreType.DMA((blocks // GROUP, 2)),
            pltpu.SemaphoreType.DMA((blocks, visits)),
        ],
        compiler_params=pltpu.CompilerParams(vmem_limit_bytes=60 * MIB),
        cost_estimate=pl.CostEstimate(
            flops=8 * blocks * side**3, bytes_accessed=8 * blocks * side**2, transcendentals=0
        ),
        name="warp",
    )(visit, tile, offset, good, rows, cols, var, image)


def place_kernel(part, code_ref, blocks_ref, coadd_ref, strip_ref, edge_ref, data, weight):
    step = pl.program_id(0)
    some = blocks_ref.shape[0]
    height = data.shape[0]
    lot = height // UNITS

    @pl.when(step == 0)
    def _():
        data[...] = jnp.zeros_like(data)
        weight[...] = jnp.zeros_like(weight)

    for block in range(some):
        for slot in range(CAP):
            code = code_ref[(step * some + block) * CAP + slot]

            @pl.when(code >= 0)
            def _():
                row = pl.multiple_of((code // 8) * lot, lot)
                for half in range(2):
                    col = pl.multiple_of((code % 8 + half) * STEP, STEP)
                    cells = (pl.ds(row, part), pl.ds(col, STEP))
                    first = (slot * 2 + half) * 2 * part
                    data[cells] += blocks_ref[block, first : first + part].astype(jnp.float32)
                    weight[cells] += blocks_ref[block, first + part : first + 2 * part].astype(
                        jnp.float32
                    )

    @pl.when(step == pl.num_programs(0) - 1)
    def _():
        coadd = data[...] / jnp.maximum(weight[...], 1.0)
        coadd_ref[...] = coadd.astype(coadd_ref.dtype)
        strip_ref[:HALO] = coadd[:, :SIDE].T[:HALO]
        strip_ref[HALO:] = coadd[:, TX - SIDE :].T[SIDE - HALO :]
        edge_ref[:HALO] = coadd[:HALO]
        edge_ref[HALO:] = coadd[height - HALO :]


def place(code, blocks, lot):
    count, tall, side = blocks.shape
    some = 4
    height = lot * UNITS
    shapes = [((height, TX), jnp.bfloat16), ((2 * HALO, height), jnp.float32), ((2 * HALO, TX), jnp.float32)]
    return pl.pallas_call(
        functools.partial(place_kernel, 2 * lot),
        grid_spec=pltpu.PrefetchScalarGridSpec(
            num_scalar_prefetch=1,
            grid=(count // some,),
            in_specs=[pl.BlockSpec((some, tall, side), lambda step, code: (step, 0, 0))],
            out_specs=[pl.BlockSpec(shape, lambda step, code: (0, 0)) for shape, _ in shapes],
            scratch_shapes=[pltpu.VMEM((height, TX), jnp.float32)] * 2,
        ),
        out_shape=[jax.ShapeDtypeStruct(*shape) for shape in shapes],
        compiler_params=pltpu.CompilerParams(vmem_limit_bytes=32 * MIB),
        cost_estimate=pl.CostEstimate(
            flops=count * tall * side, bytes_accessed=count * tall * side * 2, transcendentals=0
        ),
        name="place",
    )(code, blocks)


def beside(axis):
    count = lax.axis_size(axis)
    up = [(i, i + 1) for i in range(count - 1)]
    return up, [(j, i) for i, j in up]


def neighbours(first, last, axis):
    up, down = beside(axis)
    return lax.ppermute(last, axis, up), lax.ppermute(first, axis, down)


def swapped(array):
    return lax.ppermute(array, "visit", [(0, 1), (1, 0)])


def beyond(strips, above, below):
    first = [strip[:HALO] for strip in strips] + [rows[:, :SIDE] for rows in (above, below)]
    last = [strip[HALO:] for strip in strips] + [rows[:, TX - SIDE :] for rows in (above, below)]
    return neighbours(jnp.concatenate(first, axis=1), jnp.concatenate(last, axis=1), "px")


def rows_between(edge):
    lower = lax.axis_index("visit") == 0
    mine = jnp.where(lower, edge[:HALO], edge[HALO:])
    count = lax.axis_size("py")
    up, down = beside("py")

    def pairs(cross):
        return [(i, j + cross * count) for i, j in down] + [
            (count + i, j + (1 - cross) * count) for i, j in up
        ]

    straight = lax.ppermute(mine, ("visit", "py"), pairs(0))
    crossed = lax.ppermute(mine, ("visit", "py"), pairs(1))
    return jnp.where(lower, crossed, straight), jnp.where(lower, straight, crossed)


def bands(plan, taps):
    tall, margin = plan[0]["tall"], plan[0]["margin"]
    row = jnp.arange(tall, dtype=jnp.int32)
    out = jnp.arange(tall - 2 * margin, dtype=jnp.int32) + margin
    three = (jnp.abs(row[:, None] - row[None, :]) <= 1).astype(jnp.bfloat16)
    nine = (jnp.abs(out[:, None] - row[None, :]) <= 4).astype(jnp.bfloat16)
    count = taps.shape[0]
    ahead = row[None, :] - out[:, None] + count // 2
    coarse, fine = split(sum(jnp.where(ahead == tap, taps[tap], 0.0) for tap in range(count)))
    lane = jnp.arange(4 * SIDE, dtype=jnp.int32)
    across = jnp.abs(lane[:, None] - lane[None, SIDE : 3 * SIDE]) <= 4
    return (
        three,
        nine,
        jnp.concatenate([coarse, coarse, fine], axis=1),
        across.astype(jnp.bfloat16),
    )


def split(value):
    coarse = value.astype(jnp.bfloat16)
    return coarse, (value - coarse.astype(jnp.float32)).astype(jnp.bfloat16)


def filtered(value, taps, tables, margin):
    three, nine, blur, across = [table[...] for table in tables]
    tall = value.shape[0]
    short = tall - 2 * margin

    def product(matrix, terms):
        return jnp.dot(matrix, jnp.concatenate(terms, axis=0), preferred_element_type=jnp.float32)

    moved = {
        by: (pltpu.roll(value, -by % WIDE, 1) if by else value).astype(jnp.float32)
        for by in range(-3, 4)
    }
    rowwise = sum(taps[tap] * moved[tap - 3] for tap in range(7))[:, :TX]
    resid = moved[0] - product(three, [(moved[-1] + moved[0] + moved[1]).astype(jnp.bfloat16)]) * (1.0 / 9.0)
    tower = product(nine, [(resid * resid).astype(jnp.bfloat16)]).astype(jnp.bfloat16)
    windows = [jnp.concatenate([tower[:, TX:], tower[:, : 3 * SIDE]], axis=1)]
    for start in range(2 * SIDE, TX, 2 * SIDE):
        windows.append(tower[:, start - SIDE : start + 3 * SIDE])
    boxes = jnp.dot(jnp.concatenate(windows, axis=0), across, preferred_element_type=jnp.float32)
    box = jnp.concatenate(
        [boxes[at * short : (at + 1) * short] for at in range(len(windows))], axis=1
    )
    local = box * (1.0 / 81.0) + 1e-05
    coarse, fine = split(rowwise)
    return product(blur, (coarse, fine, coarse)) * lax.rsqrt(local), local


def stage_kernel(plan, lots, *refs):
    mine_ref, taps_ref, above_ref, below_ref = refs[:4]
    tables = refs[4:8]
    fields, copies, outs = plan
    visits, margin = fields["visits"], fields["margin"]
    at = 8
    chunks = []
    for lot in lots:
        parts = []
        for _ in range(visits):
            parts.append(refs[at : at + 3])
            at += 3
        chunks.append(parts)
    at += fields["aliased"]
    detection_hbm, variance_hbm = refs[at : at + 2]
    field, detection, variance, sems = refs[at + 2 : at + 6]
    sides = refs[at + 6 :]
    spans, tall, _ = field.shape

    which = 0
    held = []
    for parts in chunks:
        group = []
        for number, (cells, left, right) in enumerate(parts):
            side = sides[which]
            which += 1
            height = cells.shape[0]
            first = number * height if left.shape[1] > height else 0
            here = slice(first, first + height)
            gap = jnp.zeros((SIDE - 2 * HALO, height), jnp.float32)
            side[...] = jnp.concatenate(
                [right[right.shape[0] - HALO :, here], gap, left[:HALO, here]], axis=0
            ).T.astype(jnp.bfloat16)
            group.append((cells, side))
        held.append(group)

    for span, first, rows in fields["blank"]:
        field[span, first : first + rows, :] = jnp.zeros((rows, WIDE), jnp.bfloat16)

    def assemble(order):
        for chunk, visit, first, rows, at_row, begin, end, shift in copies:
            cells, side = held[chunk][order[visit]]
            lot = lots[chunk]

            @pl.loop(begin, end)
            def _(unit):
                start = pl.multiple_of(unit * lot + first, EDGE)
                into = pl.ds(at_row, rows)
                field[unit + shift, into, :TX] = cells[pl.ds(start, rows), :]
                field[unit + shift, into, TX:] = side[pl.ds(start, rows), :]

    if visits == 2:
        for flip in range(2):

            @pl.when(mine_ref[0] == flip)
            def _():
                assemble((0, 1) if flip == 0 else (1, 0))

    else:
        assemble(tuple(range(visits)))

    if fields["between"]:
        _, left, right = chunks[0][0]
        corners = left.shape[1] - 2 * SIDE
        from_left = lax.broadcasted_iota(jnp.int32, (HALO, SIDE), 1) >= SIDE // 2
        none = jnp.zeros((EDGE - HALO, WIDE), jnp.float32)
        for number, (span, first, rows) in enumerate(
            zip((0, spans - 1), fields["between"], (above_ref, below_ref))
        ):
            here = slice(corners + number * SIDE, corners + (number + 1) * SIDE)
            wide = jnp.concatenate(
                [rows[...], jnp.where(from_left, left[:, here], right[:, here])], axis=1
            )
            strip = [none, wide] if number == 0 else [wide, none]
            field[span, first : first + EDGE, :] = jnp.concatenate(strip, axis=0).astype(jnp.bfloat16)

    taps = [taps_ref[tap] for tap in range(7)]

    def stores(unit, source, rows, target):
        return [
            pltpu.make_async_copy(
                scratch.at[unit, pl.ds(source, rows)], hbm.at[pl.ds(target, rows)], sems.at[unit, at]
            )
            for at, (scratch, hbm) in enumerate(
                ((detection, detection_hbm), (variance, variance_hbm))
            )
        ]

    some = next(count for count in (4, 3, 2, 1) if spans % count == 0 and count * tall <= 320)

    @pl.loop(0, spans, step=some)
    def _(first):
        for ahead in range(some):
            unit = first + ahead
            detection[unit], variance[unit] = filtered(field[unit], taps, tables, margin)
        for ahead in range(some):
            unit = first + ahead
            for begin, end, source, rows, shift in outs:

                @pl.when((unit >= begin) & (unit < end))
                def _():
                    target = pl.multiple_of(unit * STEP + shift, HALO)
                    for store in stores(unit, source, rows, target):
                        store.start()

    @pl.loop(0, spans)
    def _(unit):
        for begin, end, source, rows, shift in outs:

            @pl.when((unit >= begin) & (unit < end))
            def _():
                for store in stores(unit, source, rows, 0):
                    store.wait()


def stage(plan, mine, taps, between, tables, chunks, lots, held=()):
    fields, _, _ = plan
    spans, tall = fields["spans"], fields["tall"]
    shape = jax.ShapeDtypeStruct((TY, TX), jnp.float32)
    flat = [array for parts in chunks for part in parts for array in part]
    first = 8 + len(flat)
    out = pltpu.VMEM((spans, tall - 2 * fields["margin"], TX), jnp.float32)
    return pl.pallas_call(
        functools.partial(stage_kernel, plan, lots),
        out_shape=(shape, shape),
        in_specs=[SMEM, SMEM] + [VMEM] * (6 + len(flat)) + [HBM] * len(held),
        out_specs=(HBM, HBM),
        input_output_aliases={first + at: at for at in range(len(held))},
        scratch_shapes=[
            pltpu.VMEM((spans, tall, WIDE), jnp.bfloat16),
            out,
            out,
            pltpu.SemaphoreType.DMA((spans, 2)),
        ]
        + [pltpu.VMEM((part[0].shape[0], SIDE), jnp.bfloat16) for parts in chunks for part in parts],
        compiler_params=pltpu.CompilerParams(vmem_limit_bytes=32 * MIB),
        cost_estimate=pl.CostEstimate(
            flops=80 * spans * tall * WIDE, bytes_accessed=12 * spans * tall * WIDE, transcendentals=0
        ),
        name="stage",
    )(mine, taps, *between, *tables, *flat, *held)


def outer_plan(lot):
    fields = dict(
        visits=2, aliased=0, spans=UNITS + 1, tall=2 * lot, margin=HALO, between=(lot - EDGE, lot),
        blank=[(0, 0, lot - EDGE), (UNITS, lot + EDGE, lot - EDGE)],
    )
    copies = [(0, 1, 0, lot, 0, 0, UNITS, 1), (0, 0, 0, lot, lot, 0, UNITS, 0)]
    rows = lot - HALO
    outs = [
        (0, 1, rows, rows, 0),
        (1, UNITS, 0, 2 * rows, -rows),
        (UNITS, UNITS + 1, 0, rows, -rows),
    ]
    return fields, copies, outs


def inner_plan(lot, inner):
    tall = 2 * inner + 2 * EDGE
    fields = dict(
        visits=2, aliased=2, spans=UNITS, tall=tall, margin=HALO, between=None, blank=[]
    )
    copies = [
        (0, 0, lot - EDGE, EDGE, 0, 0, UNITS, 0),
        (1, 0, 0, inner, EDGE, 0, UNITS, 0),
        (1, 1, 0, inner, EDGE + inner, 0, UNITS, 0),
        (0, 1, 0, EDGE, EDGE + 2 * inner, 0, UNITS, 0),
    ]
    return fields, copies, [(0, UNITS, 0, tall - 2 * HALO, lot - HALO)]


def whole_plan(lot, visits):
    fields = dict(
        visits=visits, aliased=0, spans=UNITS, tall=STEP + 2 * EDGE, margin=EDGE,
        between=(0, EDGE + STEP), blank=[],
    )
    copies = [(0, visit, 0, lot, EDGE + visit * lot, 0, UNITS, 0) for visit in range(visits)]
    copies.append((0, visits - 1, lot - EDGE, EDGE, 0, 0, UNITS - 1, 1))
    copies.append((0, 0, 0, EDGE, EDGE + STEP, 1, UNITS, -1))
    return fields, copies, [(0, UNITS, 0, STEP, 0)]


def per_device(
    images, inv_var, good_columns, warp_rows, warp_cols, block_visit, dest_tile, offsets, psf_taps
):
    tiles = lax.axis_size("py") * lax.axis_size("px")
    visits = lax.axis_size("visit")
    plan = shares(visits)
    lots = [rows for rows, _ in plan]
    mine = lax.axis_index("visit").astype(jnp.int32).reshape(1)

    def make(chunk, var):
        return warp(
            tiles, plan[chunk], chunk == 0, block_visit, dest_tile[:, 0], offsets.T,
            good_columns, warp_rows, warp_cols, var, images,
        )

    def send(blocks):
        return lax.all_to_all(blocks, EVERY, split_axis=0, concat_axis=0, tiled=True)

    made, psf_taps = lax.optimization_barrier((make(0, inv_var), psf_taps))
    arrived = send(made)
    if len(plan) == 1:
        every = whole_plan(lots[0], visits)
        coadd, strip, edge = place(codes(arrived), arrived, lots[0])
        all_of = [lax.all_gather(part, "visit") for part in (coadd, strip, edge)]
        between = neighbours(all_of[2][0, :HALO], all_of[2][visits - 1, HALO:], "py")
        sides = beyond([all_of[1][visit] for visit in range(visits)], *between)
        parts = [(all_of[0][visit], *sides) for visit in range(visits)]
        return stage(every, mine, psf_taps, between, bands(every, psf_taps), [parts], lots)

    outer, inner = outer_plan(lots[0]), inner_plan(*lots)
    tables, inv_var = lax.optimization_barrier(
        ([bands(part, psf_taps) for part in (outer, inner)], inv_var)
    )
    arrived, later = lax.optimization_barrier((arrived, make(1, inv_var)))
    second = send(later)
    code = codes(arrived)
    coadd, strip, edge = place(code, arrived, lots[0])
    between, other_strip = rows_between(edge), swapped(strip)
    coadd, between, other_strip = lax.optimization_barrier((coadd, between, other_strip))
    sides = beyond([strip, other_strip], *between)
    other = swapped(coadd)
    second, sides = lax.optimization_barrier((second, sides))
    parts = [(coadd, *sides), (other, *sides)]
    coadd, strip, _ = place(code, second, lots[1])
    near = neighbours(strip[:HALO], strip[HALO:], "px")
    coadd, near = lax.optimization_barrier((coadd, near))
    far = swapped(jnp.concatenate(near, axis=0))
    other = swapped(coadd)
    (parts, between), _ = lax.optimization_barrier(((parts, between), coadd))
    held = stage(outer, mine, psf_taps, between, tables[0], [parts], lots[:1])
    more = [(coadd, *near), (other, far, far)]
    return stage(inner, mine, psf_taps, between, tables[1], [parts, more], lots, held)


def codes(arrived):
    note = arrived[:, arrived.shape[1] - NOTE, :: SIDE // CAP]
    return note.astype(jnp.float32).astype(jnp.int32).reshape(-1)


def solution(mesh):
    in_specs = (
        P(EVERY, None, None),
        P(EVERY, None, None),
        P("visit", None),
        P("visit", None, None),
        P("visit", None, None),
        P(EVERY),
        P(EVERY, None),
        P(EVERY, None),
        P(),
    )
    out_specs = (P("py", "px"), P("py", "px"))
    return jax.shard_map(
        per_device, mesh=mesh, in_specs=in_specs, out_specs=out_specs, check_vma=False
    )
```

```python
import functools

import jax
import jax.numpy as jnp
from jax import lax
from jax.experimental import pallas as pl
from jax.experimental.pallas import tpu as pltpu
from jax.sharding import PartitionSpec as P

TY = 1024
TX = 1024
STEP = 128
CAP = 2
UNITS = TY // STEP
HALO = 8
EDGE = 16
SIDE = 128
WIDE = TX + SIDE
GROUP = 8
NOTE = 16
MIB = 1 << 20
EVERY = ("visit", "py", "px")
HBM = pl.BlockSpec(memory_space=pltpu.HBM)
SMEM = pl.BlockSpec(memory_space=pltpu.SMEM)
VMEM = pl.BlockSpec(memory_space=pltpu.VMEM)


def shares(visits):
    if visits == 2:
        edge, inner = 48, 16
        return [(edge, (0, STEP - edge)), (inner, (edge, edge + inner))]
    rows = STEP // visits
    return [(rows, tuple(visit * rows for visit in range(visits)))]


def warp_kernel(
    tiles, share, noted, visit_ref, tile_ref, offset_ref, good_ref, rows_hbm, cols_hbm, var_hbm,
    image_hbm, out_hbm, rows, cols, var, image, done, note, count, table_sems, sems, out_sems,
):
    blocks, side, _ = var.shape
    some, firsts = share
    groups = blocks // GROUP
    slot_rows = done.shape[2]
    tables = [
        pltpu.make_async_copy(rows_hbm, rows, table_sems.at[0]),
        pltpu.make_async_copy(cols_hbm, cols, table_sems.at[1]),
    ]

    def loads(group):
        span = pl.ds(group * GROUP, GROUP)
        return (
            pltpu.make_async_copy(var_hbm.at[span], var.at[span], sems.at[group, 0]),
            pltpu.make_async_copy(image_hbm.at[span], image.at[span], sems.at[group, 1]),
        )

    for load in tables:
        load.start()
    for group in range(groups):
        for load in loads(group):
            load.start()

    @pl.loop(0, tiles)
    def _(tile):
        count[tile] = 0

    if noted:
        note[...] = jnp.full(note.shape, -1, jnp.bfloat16)
        slot_of_lane = lax.broadcasted_iota(jnp.int32, (NOTE, SIDE), 1) // (SIDE // CAP)

    for load in tables:
        load.wait()

    strips = [first + strip * STEP for first in firsts for strip in range(side // STEP)]
    tall = some * len(strips)
    part = tall // len(firsts)

    @pl.loop(0, groups)
    def _(group):
        for load in loads(group):
            load.wait()
        visits = [visit_ref[group * GROUP + ahead] for ahead in range(GROUP)]
        planes, turned, warped = [], [], []
        for ahead in range(GROUP):
            block = group * GROUP + ahead
            good = good_ref[pl.ds(visits[ahead], 1), :].astype(jnp.float32)
            weight = var[block].astype(jnp.float32) * good
            data = weight * image[block].astype(jnp.float32)
            planes.append(
                jnp.concatenate([data.astype(jnp.bfloat16), weight.astype(jnp.bfloat16)], axis=1)
            )
        for ahead in range(GROUP):
            matrix = jnp.concatenate(
                [rows[visits[ahead], first : first + some, :] for first in strips], axis=0
            )
            turned.append(
                jnp.dot(matrix, planes[ahead], preferred_element_type=jnp.float32).astype(jnp.bfloat16)
            )
        for ahead in range(GROUP):
            both = jnp.concatenate([turned[ahead][:, :side], turned[ahead][:, side:]], axis=0)
            warped.append(
                lax.dot_general(
                    both,
                    cols[visits[ahead]],
                    (((1,), (1,)), ((), ())),
                    preferred_element_type=jnp.float32,
                ).astype(jnp.bfloat16)
            )
        for ahead in range(GROUP):
            block = group * GROUP + ahead
            for visit in range(len(firsts)):
                for half in range(side // SIDE):
                    for plane in range(2):
                        start = plane * tall + visit * part
                        into = (2 * half + plane) * part
                        done[block, visit, into : into + part, :] = warped[ahead][
                            start : start + part, half * SIDE : (half + 1) * SIDE
                        ]
        for ahead in range(GROUP):
            block = group * GROUP + ahead
            tile = tile_ref[block]
            rank = count[tile]
            count[tile] = rank + 1
            for visit in range(len(firsts)):
                target = visit * tiles + tile
                pltpu.make_async_copy(
                    done.at[block, visit],
                    out_hbm.at[target, pl.ds(pl.multiple_of(rank * slot_rows, NOTE), slot_rows)],
                    out_sems.at[block, visit],
                ).start()
                if noted:
                    code = offset_ref[0, block] * 8 + offset_ref[1, block]
                    note[target] = jnp.where(
                        slot_of_lane == rank, code.astype(jnp.float32), note[target].astype(jnp.float32)
                    ).astype(jnp.bfloat16)

    if noted:
        notes = pltpu.make_async_copy(
            note, out_hbm.at[:, pl.ds(CAP * slot_rows, NOTE)], table_sems.at[0]
        )
        notes.start()

    @pl.loop(0, blocks)
    def _(block):
        for visit in range(len(firsts)):
            pltpu.make_async_copy(
                done.at[block, visit], out_hbm.at[0, pl.ds(0, slot_rows)], out_sems.at[block, visit]
            ).wait()

    if noted:
        notes.wait()


def warp(tiles, share, noted, visit, tile, offset, good, rows, cols, var, image):
    blocks, side, _ = var.shape
    some, firsts = share
    slot_rows = 2 * (side // STEP) * some * (side // SIDE)
    visits = len(firsts)
    return pl.pallas_call(
        functools.partial(warp_kernel, tiles, share, noted),
        out_shape=jax.ShapeDtypeStruct(
            (visits * tiles, CAP * slot_rows + noted * NOTE, SIDE), jnp.bfloat16
        ),
        in_specs=[SMEM, SMEM, SMEM, VMEM, HBM, HBM, HBM, HBM],
        out_specs=HBM,
        scratch_shapes=[
            pltpu.VMEM(rows.shape, jnp.bfloat16),
            pltpu.VMEM(cols.shape, jnp.bfloat16),
            pltpu.VMEM(var.shape, jnp.bfloat16),
            pltpu.VMEM(var.shape, jnp.bfloat16),
            pltpu.VMEM((blocks, visits, slot_rows, SIDE), jnp.bfloat16),
            pltpu.VMEM((visits * tiles, NOTE, SIDE), jnp.bfloat16),
            pltpu.SMEM((tiles,), jnp.int32),
            pltpu.SemaphoreType.DMA((2,)),
            pltpu.SemaphoreType.DMA((blocks // GROUP, 2)),
            pltpu.SemaphoreType.DMA((blocks, visits)),
        ],
        compiler_params=pltpu.CompilerParams(vmem_limit_bytes=60 * MIB),
        cost_estimate=pl.CostEstimate(
            flops=8 * blocks * side**3, bytes_accessed=8 * blocks * side**2, transcendentals=0
        ),
        name="warp",
    )(visit, tile, offset, good, rows, cols, var, image)


def place_kernel(part, code_ref, blocks_ref, coadd_ref, strip_ref, edge_ref, data, weight):
    step = pl.program_id(0)
    some = blocks_ref.shape[0]
    height = data.shape[0]
    lot = height // UNITS

    @pl.when(step == 0)
    def _():
        data[...] = jnp.zeros_like(data)
        weight[...] = jnp.zeros_like(weight)

    for block in range(some):
        for slot in range(CAP):
            code = code_ref[(step * some + block) * CAP + slot]

            @pl.when(code >= 0)
            def _():
                row = pl.multiple_of((code // 8) * lot, lot)
                for half in range(2):
                    col = pl.multiple_of((code % 8 + half) * STEP, STEP)
                    cells = (pl.ds(row, part), pl.ds(col, STEP))
                    first = (slot * 2 + half) * 2 * part
                    data[cells] += blocks_ref[block, first : first + part].astype(jnp.float32)
                    weight[cells] += blocks_ref[block, first + part : first + 2 * part].astype(
                        jnp.float32
                    )

    @pl.when(step == pl.num_programs(0) - 1)
    def _():
        coadd = data[...] / jnp.maximum(weight[...], 1.0)
        coadd_ref[...] = coadd.astype(coadd_ref.dtype)
        strip_ref[:HALO] = coadd[:, :SIDE].T[:HALO]
        strip_ref[HALO:] = coadd[:, TX - SIDE :].T[SIDE - HALO :]
        edge_ref[:HALO] = coadd[:HALO]
        edge_ref[HALO:] = coadd[height - HALO :]


def place(code, blocks, lot):
    count, tall, side = blocks.shape
    some = 4
    height = lot * UNITS
    shapes = [((height, TX), jnp.bfloat16), ((2 * HALO, height), jnp.float32), ((2 * HALO, TX), jnp.float32)]
    return pl.pallas_call(
        functools.partial(place_kernel, 2 * lot),
        grid_spec=pltpu.PrefetchScalarGridSpec(
            num_scalar_prefetch=1,
            grid=(count // some,),
            in_specs=[pl.BlockSpec((some, tall, side), lambda step, code: (step, 0, 0))],
            out_specs=[pl.BlockSpec(shape, lambda step, code: (0, 0)) for shape, _ in shapes],
            scratch_shapes=[pltpu.VMEM((height, TX), jnp.float32)] * 2,
        ),
        out_shape=[jax.ShapeDtypeStruct(*shape) for shape in shapes],
        compiler_params=pltpu.CompilerParams(vmem_limit_bytes=32 * MIB),
        cost_estimate=pl.CostEstimate(
            flops=count * tall * side, bytes_accessed=count * tall * side * 2, transcendentals=0
        ),
        name="place",
    )(code, blocks)


def beside(axis):
    count = lax.axis_size(axis)
    up = [(i, i + 1) for i in range(count - 1)]
    return up, [(j, i) for i, j in up]


def neighbours(first, last, axis):
    up, down = beside(axis)
    return lax.ppermute(last, axis, up), lax.ppermute(first, axis, down)


def swapped(array):
    return lax.ppermute(array, "visit", [(0, 1), (1, 0)])


def beyond(strips, above, below):
    first = [strip[:HALO] for strip in strips] + [rows[:, :SIDE] for rows in (above, below)]
    last = [strip[HALO:] for strip in strips] + [rows[:, TX - SIDE :] for rows in (above, below)]
    return neighbours(jnp.concatenate(first, axis=1), jnp.concatenate(last, axis=1), "px")


def rows_between(edge):
    lower = lax.axis_index("visit") == 0
    mine = jnp.where(lower, edge[:HALO], edge[HALO:])
    count = lax.axis_size("py")
    up, down = beside("py")

    def pairs(cross):
        return [(i, j + cross * count) for i, j in down] + [
            (count + i, j + (1 - cross) * count) for i, j in up
        ]

    straight = lax.ppermute(mine, ("visit", "py"), pairs(0))
    crossed = lax.ppermute(mine, ("visit", "py"), pairs(1))
    return jnp.where(lower, crossed, straight), jnp.where(lower, straight, crossed)


def bands(plan, taps):
    tall, margin = plan[0]["tall"], plan[0]["margin"]
    row = jnp.arange(tall, dtype=jnp.int32)
    out = jnp.arange(tall - 2 * margin, dtype=jnp.int32) + margin
    three = (jnp.abs(row[:, None] - row[None, :]) <= 1).astype(jnp.bfloat16)
    nine = (jnp.abs(out[:, None] - row[None, :]) <= 4).astype(jnp.bfloat16)
    count = taps.shape[0]
    ahead = row[None, :] - out[:, None] + count // 2
    coarse, fine = split(sum(jnp.where(ahead == tap, taps[tap], 0.0) for tap in range(count)))
    lane = jnp.arange(4 * SIDE, dtype=jnp.int32)
    across = jnp.abs(lane[:, None] - lane[None, SIDE : 3 * SIDE]) <= 4
    return (
        three,
        nine,
        jnp.concatenate([coarse, coarse, fine], axis=1),
        across.astype(jnp.bfloat16),
    )


def split(value):
    coarse = value.astype(jnp.bfloat16)
    return coarse, (value - coarse.astype(jnp.float32)).astype(jnp.bfloat16)


def filtered(value, taps, tables, margin):
    three, nine, blur, across = [table[...] for table in tables]
    tall = value.shape[0]
    short = tall - 2 * margin

    def product(matrix, terms):
        return jnp.dot(matrix, jnp.concatenate(terms, axis=0), preferred_element_type=jnp.float32)

    moved = {
        by: (pltpu.roll(value, -by % WIDE, 1) if by else value).astype(jnp.float32)
        for by in range(-3, 4)
    }
    rowwise = sum(taps[tap] * moved[tap - 3] for tap in range(7))[:, :TX]
    resid = moved[0] - product(three, [(moved[-1] + moved[0] + moved[1]).astype(jnp.bfloat16)]) * (1.0 / 9.0)
    tower = product(nine, [(resid * resid).astype(jnp.bfloat16)]).astype(jnp.bfloat16)
    windows = [jnp.concatenate([tower[:, TX:], tower[:, : 3 * SIDE]], axis=1)]
    for start in range(2 * SIDE, TX, 2 * SIDE):
        windows.append(tower[:, start - SIDE : start + 3 * SIDE])
    boxes = jnp.dot(jnp.concatenate(windows, axis=0), across, preferred_element_type=jnp.float32)
    box = jnp.concatenate(
        [boxes[at * short : (at + 1) * short] for at in range(len(windows))], axis=1
    )
    local = box * (1.0 / 81.0) + 1e-05
    coarse, fine = split(rowwise)
    return product(blur, (coarse, fine, coarse)) * lax.rsqrt(local), local


def stage_kernel(plan, lots, *refs):
    mine_ref, taps_ref, above_ref, below_ref = refs[:4]
    tables = refs[4:8]
    fields, copies, outs = plan
    visits, margin = fields["visits"], fields["margin"]
    at = 8
    chunks = []
    for lot in lots:
        parts = []
        for _ in range(visits):
            parts.append(refs[at : at + 3])
            at += 3
        chunks.append(parts)
    at += fields["aliased"]
    detection_hbm, variance_hbm = refs[at : at + 2]
    field, detection, variance, sems = refs[at + 2 : at + 6]
    sides = refs[at + 6 :]
    spans, tall, _ = field.shape

    which = 0
    held = []
    for parts in chunks:
        group = []
        for number, (cells, left, right) in enumerate(parts):
            side = sides[which]
            which += 1
            height = cells.shape[0]
            first = number * height if left.shape[1] > height else 0
            here = slice(first, first + height)
            gap = jnp.zeros((SIDE - 2 * HALO, height), jnp.float32)
            side[...] = jnp.concatenate(
                [right[right.shape[0] - HALO :, here], gap, left[:HALO, here]], axis=0
            ).T.astype(jnp.bfloat16)
            group.append((cells, side))
        held.append(group)

    for span, first, rows in fields["blank"]:
        field[span, first : first + rows, :] = jnp.zeros((rows, WIDE), jnp.bfloat16)

    def assemble(order):
        for chunk, visit, first, rows, at_row, begin, end, shift in copies:
            cells, side = held[chunk][order[visit]]
            lot = lots[chunk]

            @pl.loop(begin, end)
            def _(unit):
                start = pl.multiple_of(unit * lot + first, EDGE)
                into = pl.ds(at_row, rows)
                field[unit + shift, into, :TX] = cells[pl.ds(start, rows), :]
                field[unit + shift, into, TX:] = side[pl.ds(start, rows), :]

    if visits == 2:
        for flip in range(2):

            @pl.when(mine_ref[0] == flip)
            def _():
                assemble((0, 1) if flip == 0 else (1, 0))

    else:
        assemble(tuple(range(visits)))

    if fields["between"]:
        _, left, right = chunks[0][0]
        corners = left.shape[1] - 2 * SIDE
        from_left = lax.broadcasted_iota(jnp.int32, (HALO, SIDE), 1) >= SIDE // 2
        none = jnp.zeros((EDGE - HALO, WIDE), jnp.float32)
        for number, (span, first, rows) in enumerate(
            zip((0, spans - 1), fields["between"], (above_ref, below_ref))
        ):
            here = slice(corners + number * SIDE, corners + (number + 1) * SIDE)
            wide = jnp.concatenate(
                [rows[...], jnp.where(from_left, left[:, here], right[:, here])], axis=1
            )
            strip = [none, wide] if number == 0 else [wide, none]
            field[span, first : first + EDGE, :] = jnp.concatenate(strip, axis=0).astype(jnp.bfloat16)

    taps = [taps_ref[tap] for tap in range(7)]

    def stores(unit, source, rows, target):
        return [
            pltpu.make_async_copy(
                scratch.at[unit, pl.ds(source, rows)], hbm.at[pl.ds(target, rows)], sems.at[unit, at]
            )
            for at, (scratch, hbm) in enumerate(
                ((detection, detection_hbm), (variance, variance_hbm))
            )
        ]

    some = next(count for count in (4, 3, 2, 1) if spans % count == 0 and count * tall <= 320)

    @pl.loop(0, spans, step=some)
    def _(first):
        for ahead in range(some):
            unit = first + ahead
            detection[unit], variance[unit] = filtered(field[unit], taps, tables, margin)
        for ahead in range(some):
            unit = first + ahead
            for begin, end, source, rows, shift in outs:

                @pl.when((unit >= begin) & (unit < end))
                def _():
                    target = pl.multiple_of(unit * STEP + shift, HALO)
                    for store in stores(unit, source, rows, target):
                        store.start()

    @pl.loop(0, spans)
    def _(unit):
        for begin, end, source, rows, shift in outs:

            @pl.when((unit >= begin) & (unit < end))
            def _():
                for store in stores(unit, source, rows, 0):
                    store.wait()


def stage(plan, mine, taps, between, tables, chunks, lots, held=()):
    fields, _, _ = plan
    spans, tall = fields["spans"], fields["tall"]
    shape = jax.ShapeDtypeStruct((TY, TX), jnp.float32)
    flat = [array for parts in chunks for part in parts for array in part]
    first = 8 + len(flat)
    out = pltpu.VMEM((spans, tall - 2 * fields["margin"], TX), jnp.float32)
    return pl.pallas_call(
        functools.partial(stage_kernel, plan, lots),
        out_shape=(shape, shape),
        in_specs=[SMEM, SMEM] + [VMEM] * (6 + len(flat)) + [HBM] * len(held),
        out_specs=(HBM, HBM),
        input_output_aliases={first + at: at for at in range(len(held))},
        scratch_shapes=[
            pltpu.VMEM((spans, tall, WIDE), jnp.bfloat16),
            out,
            out,
            pltpu.SemaphoreType.DMA((spans, 2)),
        ]
        + [pltpu.VMEM((part[0].shape[0], SIDE), jnp.bfloat16) for parts in chunks for part in parts],
        compiler_params=pltpu.CompilerParams(vmem_limit_bytes=32 * MIB),
        cost_estimate=pl.CostEstimate(
            flops=80 * spans * tall * WIDE, bytes_accessed=12 * spans * tall * WIDE, transcendentals=0
        ),
        name="stage",
    )(mine, taps, *between, *tables, *flat, *held)


def outer_plan(lot):
    fields = dict(
        visits=2, aliased=0, spans=UNITS + 1, tall=2 * lot, margin=HALO, between=(lot - EDGE, lot),
        blank=[(0, 0, lot - EDGE), (UNITS, lot + EDGE, lot - EDGE)],
    )
    copies = [(0, 1, 0, lot, 0, 0, UNITS, 1), (0, 0, 0, lot, lot, 0, UNITS, 0)]
    rows = lot - HALO
    outs = [
        (0, 1, rows, rows, 0),
        (1, UNITS, 0, 2 * rows, -rows),
        (UNITS, UNITS + 1, 0, rows, -rows),
    ]
    return fields, copies, outs


def inner_plan(lot, inner):
    tall = 2 * inner + 2 * EDGE
    fields = dict(
        visits=2, aliased=2, spans=UNITS, tall=tall, margin=HALO, between=None, blank=[]
    )
    copies = [
        (0, 0, lot - EDGE, EDGE, 0, 0, UNITS, 0),
        (1, 0, 0, inner, EDGE, 0, UNITS, 0),
        (1, 1, 0, inner, EDGE + inner, 0, UNITS, 0),
        (0, 1, 0, EDGE, EDGE + 2 * inner, 0, UNITS, 0),
    ]
    return fields, copies, [(0, UNITS, 0, tall - 2 * HALO, lot - HALO)]


def whole_plan(lot, visits):
    fields = dict(
        visits=visits, aliased=0, spans=UNITS, tall=STEP + 2 * EDGE, margin=EDGE,
        between=(0, EDGE + STEP), blank=[],
    )
    copies = [(0, visit, 0, lot, EDGE + visit * lot, 0, UNITS, 0) for visit in range(visits)]
    copies.append((0, visits - 1, lot - EDGE, EDGE, 0, 0, UNITS - 1, 1))
    copies.append((0, 0, 0, EDGE, EDGE + STEP, 1, UNITS, -1))
    return fields, copies, [(0, UNITS, 0, STEP, 0)]


def per_device(
    images, inv_var, good_columns, warp_rows, warp_cols, block_visit, dest_tile, offsets, psf_taps
):
    tiles = lax.axis_size("py") * lax.axis_size("px")
    visits = lax.axis_size("visit")
    plan = shares(visits)
    lots = [rows for rows, _ in plan]
    mine = lax.axis_index("visit").astype(jnp.int32).reshape(1)

    def make(chunk, var):
        return warp(
            tiles, plan[chunk], chunk == 0, block_visit, dest_tile[:, 0], offsets.T,
            good_columns, warp_rows, warp_cols, var, images,
        )

    def send(blocks):
        return lax.all_to_all(blocks, EVERY, split_axis=0, concat_axis=0, tiled=True)

    made, psf_taps = lax.optimization_barrier((make(0, inv_var), psf_taps))
    arrived = send(made)
    if len(plan) == 1:
        every = whole_plan(lots[0], visits)
        coadd, strip, edge = place(codes(arrived), arrived, lots[0])
        all_of = [lax.all_gather(part, "visit") for part in (coadd, strip, edge)]
        between = neighbours(all_of[2][0, :HALO], all_of[2][visits - 1, HALO:], "py")
        sides = beyond([all_of[1][visit] for visit in range(visits)], *between)
        parts = [(all_of[0][visit], *sides) for visit in range(visits)]
        return stage(every, mine, psf_taps, between, bands(every, psf_taps), [parts], lots)

    outer, inner = outer_plan(lots[0]), inner_plan(*lots)
    tables, inv_var = lax.optimization_barrier(
        ([bands(part, psf_taps) for part in (outer, inner)], inv_var)
    )
    arrived, later = lax.optimization_barrier((arrived, make(1, inv_var)))
    second = send(later)
    code = codes(arrived)
    coadd, strip, edge = place(code, arrived, lots[0])
    between, other_strip = rows_between(edge), swapped(strip)
    coadd, between, other_strip = lax.optimization_barrier((coadd, between, other_strip))
    sides = beyond([strip, other_strip], *between)
    other = swapped(coadd)
    second, sides = lax.optimization_barrier((second, sides))
    parts = [(coadd, *sides), (other, *sides)]
    coadd, strip, _ = place(code, second, lots[1])
    other = swapped(coadd)
    (parts, between), _ = lax.optimization_barrier(((parts, between), coadd))
    held = stage(outer, mine, psf_taps, between, tables[0], [parts], lots[:1])
    strip, held = lax.optimization_barrier((strip, held))
    near = neighbours(strip[:HALO], strip[HALO:], "px")
    far = swapped(jnp.concatenate(near, axis=0))
    more = [(coadd, *near), (other, far, far)]
    return stage(inner, mine, psf_taps, between, tables[1], [parts, more], lots, held)


def codes(arrived):
    note = arrived[:, arrived.shape[1] - NOTE, :: SIDE // CAP]
    return note.astype(jnp.float32).astype(jnp.int32).reshape(-1)


def solution(mesh):
    in_specs = (
        P(EVERY, None, None),
        P(EVERY, None, None),
        P("visit", None),
        P("visit", None, None),
        P("visit", None, None),
        P(EVERY),
        P(EVERY, None),
        P(EVERY, None),
        P(),
    )
    out_specs = (P("py", "px"), P("py", "px"))
    return jax.shard_map(
        per_device, mesh=mesh, in_specs=in_specs, out_specs=out_specs, check_vma=False
    )
```

```python
import functools

import jax
import jax.numpy as jnp
from jax import lax
from jax.experimental import pallas as pl
from jax.experimental.pallas import tpu as pltpu
from jax.sharding import PartitionSpec as P

TY = 1024
TX = 1024
STEP = 128
CAP = 2
UNITS = TY // STEP
HALO = 8
EDGE = 16
SIDE = 128
WIDE = TX + SIDE
GROUP = 8
NOTE = 16
MIB = 1 << 20
EVERY = ("visit", "py", "px")
HBM = pl.BlockSpec(memory_space=pltpu.HBM)
SMEM = pl.BlockSpec(memory_space=pltpu.SMEM)
VMEM = pl.BlockSpec(memory_space=pltpu.VMEM)


def shares(visits):
    if visits == 2:
        edge, inner = 48, 16
        return [(edge, (0, STEP - edge)), (inner, (edge, edge + inner))]
    rows = STEP // visits
    return [(rows, tuple(visit * rows for visit in range(visits)))]


def warp_kernel(
    tiles, share, noted, visit_ref, tile_ref, offset_ref, good_ref, rows_hbm, cols_hbm, var_hbm,
    image_hbm, out_hbm, rows, cols, var, image, done, note, count, table_sems, sems, out_sems,
):
    blocks, side, _ = var.shape
    some, firsts = share
    groups = blocks // GROUP
    slot_rows = done.shape[2]
    tables = [
        pltpu.make_async_copy(rows_hbm, rows, table_sems.at[0]),
        pltpu.make_async_copy(cols_hbm, cols, table_sems.at[1]),
    ]

    def loads(group):
        span = pl.ds(group * GROUP, GROUP)
        return (
            pltpu.make_async_copy(var_hbm.at[span], var.at[span], sems.at[group, 0]),
            pltpu.make_async_copy(image_hbm.at[span], image.at[span], sems.at[group, 1]),
        )

    for load in tables:
        load.start()
    for group in range(groups):
        for load in loads(group):
            load.start()

    @pl.loop(0, tiles)
    def _(tile):
        count[tile] = 0

    if noted:
        note[...] = jnp.full(note.shape, -1, jnp.bfloat16)
        slot_of_lane = lax.broadcasted_iota(jnp.int32, (NOTE, SIDE), 1) // (SIDE // CAP)

    for load in tables:
        load.wait()

    strips = [first + strip * STEP for first in firsts for strip in range(side // STEP)]
    tall = some * len(strips)
    part = tall // len(firsts)

    @pl.loop(0, groups)
    def _(group):
        for load in loads(group):
            load.wait()
        visits = [visit_ref[group * GROUP + ahead] for ahead in range(GROUP)]
        planes, turned, warped = [], [], []
        for ahead in range(GROUP):
            block = group * GROUP + ahead
            good = good_ref[pl.ds(visits[ahead], 1), :].astype(jnp.float32)
            weight = var[block].astype(jnp.float32) * good
            data = weight * image[block].astype(jnp.float32)
            planes.append(
                jnp.concatenate([data.astype(jnp.bfloat16), weight.astype(jnp.bfloat16)], axis=1)
            )
        for ahead in range(GROUP):
            matrix = jnp.concatenate(
                [rows[visits[ahead], first : first + some, :] for first in strips], axis=0
            )
            turned.append(
                jnp.dot(matrix, planes[ahead], preferred_element_type=jnp.float32).astype(jnp.bfloat16)
            )
        for ahead in range(GROUP):
            both = jnp.concatenate([turned[ahead][:, :side], turned[ahead][:, side:]], axis=0)
            warped.append(
                lax.dot_general(
                    both,
                    cols[visits[ahead]],
                    (((1,), (1,)), ((), ())),
                    preferred_element_type=jnp.float32,
                ).astype(jnp.bfloat16)
            )
        for ahead in range(GROUP):
            block = group * GROUP + ahead
            for visit in range(len(firsts)):
                for half in range(side // SIDE):
                    for plane in range(2):
                        start = plane * tall + visit * part
                        into = (2 * half + plane) * part
                        done[block, visit, into : into + part, :] = warped[ahead][
                            start : start + part, half * SIDE : (half + 1) * SIDE
                        ]
        for ahead in range(GROUP):
            block = group * GROUP + ahead
            tile = tile_ref[block]
            rank = count[tile]
            count[tile] = rank + 1
            for visit in range(len(firsts)):
                target = visit * tiles + tile
                pltpu.make_async_copy(
                    done.at[block, visit],
                    out_hbm.at[target, pl.ds(pl.multiple_of(rank * slot_rows, NOTE), slot_rows)],
                    out_sems.at[block, visit],
                ).start()
                if noted:
                    code = offset_ref[0, block] * 8 + offset_ref[1, block]
                    note[target] = jnp.where(
                        slot_of_lane == rank, code.astype(jnp.float32), note[target].astype(jnp.float32)
                    ).astype(jnp.bfloat16)

    if noted:
        notes = pltpu.make_async_copy(
            note, out_hbm.at[:, pl.ds(CAP * slot_rows, NOTE)], table_sems.at[0]
        )
        notes.start()

    @pl.loop(0, blocks)
    def _(block):
        for visit in range(len(firsts)):
            pltpu.make_async_copy(
                done.at[block, visit], out_hbm.at[0, pl.ds(0, slot_rows)], out_sems.at[block, visit]
            ).wait()

    if noted:
        notes.wait()


def warp(tiles, share, noted, visit, tile, offset, good, rows, cols, var, image):
    blocks, side, _ = var.shape
    some, firsts = share
    slot_rows = 2 * (side // STEP) * some * (side // SIDE)
    visits = len(firsts)
    return pl.pallas_call(
        functools.partial(warp_kernel, tiles, share, noted),
        out_shape=jax.ShapeDtypeStruct(
            (visits * tiles, CAP * slot_rows + noted * NOTE, SIDE), jnp.bfloat16
        ),
        in_specs=[SMEM, SMEM, SMEM, VMEM, HBM, HBM, HBM, HBM],
        out_specs=HBM,
        scratch_shapes=[
            pltpu.VMEM(rows.shape, jnp.bfloat16),
            pltpu.VMEM(cols.shape, jnp.bfloat16),
            pltpu.VMEM(var.shape, jnp.bfloat16),
            pltpu.VMEM(var.shape, jnp.bfloat16),
            pltpu.VMEM((blocks, visits, slot_rows, SIDE), jnp.bfloat16),
            pltpu.VMEM((visits * tiles, NOTE, SIDE), jnp.bfloat16),
            pltpu.SMEM((tiles,), jnp.int32),
            pltpu.SemaphoreType.DMA((2,)),
            pltpu.SemaphoreType.DMA((blocks // GROUP, 2)),
            pltpu.SemaphoreType.DMA((blocks, visits)),
        ],
        compiler_params=pltpu.CompilerParams(vmem_limit_bytes=60 * MIB),
        cost_estimate=pl.CostEstimate(
            flops=8 * blocks * side**3, bytes_accessed=8 * blocks * side**2, transcendentals=0
        ),
        name="warp",
    )(visit, tile, offset, good, rows, cols, var, image)


def place_kernel(part, code_ref, blocks_ref, coadd_ref, strip_ref, edge_ref, data, weight):
    step = pl.program_id(0)
    some = blocks_ref.shape[0]
    height = data.shape[0]
    lot = height // UNITS

    @pl.when(step == 0)
    def _():
        data[...] = jnp.zeros_like(data)
        weight[...] = jnp.zeros_like(weight)

    for block in range(some):
        for slot in range(CAP):
            code = code_ref[(step * some + block) * CAP + slot]

            @pl.when(code >= 0)
            def _():
                row = pl.multiple_of((code // 8) * lot, lot)
                for half in range(2):
                    col = pl.multiple_of((code % 8 + half) * STEP, STEP)
                    cells = (pl.ds(row, part), pl.ds(col, STEP))
                    first = (slot * 2 + half) * 2 * part
                    data[cells] += blocks_ref[block, first : first + part].astype(jnp.float32)
                    weight[cells] += blocks_ref[block, first + part : first + 2 * part].astype(
                        jnp.float32
                    )

    @pl.when(step == pl.num_programs(0) - 1)
    def _():
        coadd = data[...] / jnp.maximum(weight[...], 1.0)
        coadd_ref[...] = coadd.astype(coadd_ref.dtype)
        strip_ref[:HALO] = coadd[:, :SIDE].T[:HALO]
        strip_ref[HALO:] = coadd[:, TX - SIDE :].T[SIDE - HALO :]
        edge_ref[:HALO] = coadd[:HALO]
        edge_ref[HALO:] = coadd[height - HALO :]


def place(code, blocks, lot):
    count, tall, side = blocks.shape
    some = next(some for some in (16, 8, 4, 2, 1) if count % some == 0 and some * tall <= 4096)
    height = lot * UNITS
    shapes = [((height, TX), jnp.bfloat16), ((2 * HALO, height), jnp.float32), ((2 * HALO, TX), jnp.float32)]
    return pl.pallas_call(
        functools.partial(place_kernel, 2 * lot),
        grid_spec=pltpu.PrefetchScalarGridSpec(
            num_scalar_prefetch=1,
            grid=(count // some,),
            in_specs=[pl.BlockSpec((some, tall, side), lambda step, code: (step, 0, 0))],
            out_specs=[pl.BlockSpec(shape, lambda step, code: (0, 0)) for shape, _ in shapes],
            scratch_shapes=[pltpu.VMEM((height, TX), jnp.float32)] * 2,
        ),
        out_shape=[jax.ShapeDtypeStruct(*shape) for shape in shapes],
        compiler_params=pltpu.CompilerParams(vmem_limit_bytes=32 * MIB),
        cost_estimate=pl.CostEstimate(
            flops=count * tall * side, bytes_accessed=count * tall * side * 2, transcendentals=0
        ),
        name="place",
    )(code, blocks)


def beside(axis):
    count = lax.axis_size(axis)
    up = [(i, i + 1) for i in range(count - 1)]
    return up, [(j, i) for i, j in up]


def neighbours(first, last, axis):
    up, down = beside(axis)
    return lax.ppermute(last, axis, up), lax.ppermute(first, axis, down)


def swapped(array):
    return lax.ppermute(array, "visit", [(0, 1), (1, 0)])


def beyond(strips, above, below):
    first = [strip[:HALO] for strip in strips] + [rows[:, :SIDE] for rows in (above, below)]
    last = [strip[HALO:] for strip in strips] + [rows[:, TX - SIDE :] for rows in (above, below)]
    return neighbours(jnp.concatenate(first, axis=1), jnp.concatenate(last, axis=1), "px")


def rows_between(edge):
    lower = lax.axis_index("visit") == 0
    mine = jnp.where(lower, edge[:HALO], edge[HALO:])
    count = lax.axis_size("py")
    up, down = beside("py")

    def pairs(cross):
        return [(i, j + cross * count) for i, j in down] + [
            (count + i, j + (1 - cross) * count) for i, j in up
        ]

    straight = lax.ppermute(mine, ("visit", "py"), pairs(0))
    crossed = lax.ppermute(mine, ("visit", "py"), pairs(1))
    return jnp.where(lower, crossed, straight), jnp.where(lower, straight, crossed)


def bands(plan, taps):
    tall, margin = plan[0]["tall"], plan[0]["margin"]
    row = jnp.arange(tall, dtype=jnp.int32)
    out = jnp.arange(tall - 2 * margin, dtype=jnp.int32) + margin
    three = (jnp.abs(row[:, None] - row[None, :]) <= 1).astype(jnp.bfloat16)
    nine = (jnp.abs(out[:, None] - row[None, :]) <= 4).astype(jnp.bfloat16)
    count = taps.shape[0]
    ahead = row[None, :] - out[:, None] + count // 2
    coarse, fine = split(sum(jnp.where(ahead == tap, taps[tap], 0.0) for tap in range(count)))
    lane = jnp.arange(4 * SIDE, dtype=jnp.int32)
    across = jnp.abs(lane[:, None] - lane[None, SIDE : 3 * SIDE]) <= 4
    return (
        three,
        nine,
        jnp.concatenate([coarse, coarse, fine], axis=1),
        across.astype(jnp.bfloat16),
    )


def split(value):
    coarse = value.astype(jnp.bfloat16)
    return coarse, (value - coarse.astype(jnp.float32)).astype(jnp.bfloat16)


def filtered(value, taps, tables, margin):
    three, nine, blur, across = [table[...] for table in tables]
    tall = value.shape[0]
    short = tall - 2 * margin

    def product(matrix, terms):
        return jnp.dot(matrix, jnp.concatenate(terms, axis=0), preferred_element_type=jnp.float32)

    moved = {
        by: (pltpu.roll(value, -by % WIDE, 1) if by else value).astype(jnp.float32)
        for by in range(-3, 4)
    }
    rowwise = sum(taps[tap] * moved[tap - 3] for tap in range(7))[:, :TX]
    resid = moved[0] - product(three, [(moved[-1] + moved[0] + moved[1]).astype(jnp.bfloat16)]) * (1.0 / 9.0)
    tower = product(nine, [(resid * resid).astype(jnp.bfloat16)]).astype(jnp.bfloat16)
    windows = [jnp.concatenate([tower[:, TX:], tower[:, : 3 * SIDE]], axis=1)]
    for start in range(2 * SIDE, TX, 2 * SIDE):
        windows.append(tower[:, start - SIDE : start + 3 * SIDE])
    boxes = jnp.dot(jnp.concatenate(windows, axis=0), across, preferred_element_type=jnp.float32)
    box = jnp.concatenate(
        [boxes[at * short : (at + 1) * short] for at in range(len(windows))], axis=1
    )
    local = box * (1.0 / 81.0) + 1e-05
    coarse, fine = split(rowwise)
    return product(blur, (coarse, fine, coarse)) * lax.rsqrt(local), local


def stage_kernel(plan, lots, *refs):
    mine_ref, taps_ref, above_ref, below_ref = refs[:4]
    tables = refs[4:8]
    fields, copies, outs = plan
    visits, margin = fields["visits"], fields["margin"]
    at = 8
    chunks = []
    for lot in lots:
        parts = []
        for _ in range(visits):
            parts.append(refs[at : at + 3])
            at += 3
        chunks.append(parts)
    at += fields["aliased"]
    detection_hbm, variance_hbm = refs[at : at + 2]
    field, detection, variance, sems = refs[at + 2 : at + 6]
    sides = refs[at + 6 :]
    spans, tall, _ = field.shape

    which = 0
    held = []
    for parts in chunks:
        group = []
        for number, (cells, left, right) in enumerate(parts):
            side = sides[which]
            which += 1
            height = cells.shape[0]
            first = number * height if left.shape[1] > height else 0
            here = slice(first, first + height)
            gap = jnp.zeros((SIDE - 2 * HALO, height), jnp.float32)
            side[...] = jnp.concatenate(
                [right[right.shape[0] - HALO :, here], gap, left[:HALO, here]], axis=0
            ).T.astype(jnp.bfloat16)
            group.append((cells, side))
        held.append(group)

    for span, first, rows in fields["blank"]:
        field[span, first : first + rows, :] = jnp.zeros((rows, WIDE), jnp.bfloat16)

    def assemble(order):
        for chunk, visit, first, rows, at_row, begin, end, shift in copies:
            cells, side = held[chunk][order[visit]]
            lot = lots[chunk]

            @pl.loop(begin, end)
            def _(unit):
                start = pl.multiple_of(unit * lot + first, EDGE)
                into = pl.ds(at_row, rows)
                field[unit + shift, into, :TX] = cells[pl.ds(start, rows), :]
                field[unit + shift, into, TX:] = side[pl.ds(start, rows), :]

    if visits == 2:
        for flip in range(2):

            @pl.when(mine_ref[0] == flip)
            def _():
                assemble((0, 1) if flip == 0 else (1, 0))

    else:
        assemble(tuple(range(visits)))

    if fields["between"]:
        _, left, right = chunks[0][0]
        corners = left.shape[1] - 2 * SIDE
        from_left = lax.broadcasted_iota(jnp.int32, (HALO, SIDE), 1) >= SIDE // 2
        none = jnp.zeros((EDGE - HALO, WIDE), jnp.float32)
        for number, (span, first, rows) in enumerate(
            zip((0, spans - 1), fields["between"], (above_ref, below_ref))
        ):
            here = slice(corners + number * SIDE, corners + (number + 1) * SIDE)
            wide = jnp.concatenate(
                [rows[...], jnp.where(from_left, left[:, here], right[:, here])], axis=1
            )
            strip = [none, wide] if number == 0 else [wide, none]
            field[span, first : first + EDGE, :] = jnp.concatenate(strip, axis=0).astype(jnp.bfloat16)

    taps = [taps_ref[tap] for tap in range(7)]

    def stores(unit, source, rows, target):
        return [
            pltpu.make_async_copy(
                scratch.at[unit, pl.ds(source, rows)], hbm.at[pl.ds(target, rows)], sems.at[unit, at]
            )
            for at, (scratch, hbm) in enumerate(
                ((detection, detection_hbm), (variance, variance_hbm))
            )
        ]

    some = next(count for count in (4, 3, 2, 1) if spans % count == 0 and count * tall <= 320)

    @pl.loop(0, spans, step=some)
    def _(first):
        for ahead in range(some):
            unit = first + ahead
            detection[unit], variance[unit] = filtered(field[unit], taps, tables, margin)
        for ahead in range(some):
            unit = first + ahead
            for begin, end, source, rows, shift in outs:

                @pl.when((unit >= begin) & (unit < end))
                def _():
                    target = pl.multiple_of(unit * STEP + shift, HALO)
                    for store in stores(unit, source, rows, target):
                        store.start()

    @pl.loop(0, spans)
    def _(unit):
        for begin, end, source, rows, shift in outs:

            @pl.when((unit >= begin) & (unit < end))
            def _():
                for store in stores(unit, source, rows, 0):
                    store.wait()


def stage(plan, mine, taps, between, tables, chunks, lots, held=()):
    fields, _, _ = plan
    spans, tall = fields["spans"], fields["tall"]
    shape = jax.ShapeDtypeStruct((TY, TX), jnp.float32)
    flat = [array for parts in chunks for part in parts for array in part]
    first = 8 + len(flat)
    out = pltpu.VMEM((spans, tall - 2 * fields["margin"], TX), jnp.float32)
    return pl.pallas_call(
        functools.partial(stage_kernel, plan, lots),
        out_shape=(shape, shape),
        in_specs=[SMEM, SMEM] + [VMEM] * (6 + len(flat)) + [HBM] * len(held),
        out_specs=(HBM, HBM),
        input_output_aliases={first + at: at for at in range(len(held))},
        scratch_shapes=[
            pltpu.VMEM((spans, tall, WIDE), jnp.bfloat16),
            out,
            out,
            pltpu.SemaphoreType.DMA((spans, 2)),
        ]
        + [pltpu.VMEM((part[0].shape[0], SIDE), jnp.bfloat16) for parts in chunks for part in parts],
        compiler_params=pltpu.CompilerParams(vmem_limit_bytes=32 * MIB),
        cost_estimate=pl.CostEstimate(
            flops=80 * spans * tall * WIDE, bytes_accessed=12 * spans * tall * WIDE, transcendentals=0
        ),
        name="stage",
    )(mine, taps, *between, *tables, *flat, *held)


def outer_plan(lot):
    fields = dict(
        visits=2, aliased=0, spans=UNITS + 1, tall=2 * lot, margin=HALO, between=(lot - EDGE, lot),
        blank=[(0, 0, lot - EDGE), (UNITS, lot + EDGE, lot - EDGE)],
    )
    copies = [(0, 1, 0, lot, 0, 0, UNITS, 1), (0, 0, 0, lot, lot, 0, UNITS, 0)]
    rows = lot - HALO
    outs = [
        (0, 1, rows, rows, 0),
        (1, UNITS, 0, 2 * rows, -rows),
        (UNITS, UNITS + 1, 0, rows, -rows),
    ]
    return fields, copies, outs


def inner_plan(lot, inner):
    tall = 2 * inner + 2 * EDGE
    fields = dict(
        visits=2, aliased=2, spans=UNITS, tall=tall, margin=HALO, between=None, blank=[]
    )
    copies = [
        (0, 0, lot - EDGE, EDGE, 0, 0, UNITS, 0),
        (1, 0, 0, inner, EDGE, 0, UNITS, 0),
        (1, 1, 0, inner, EDGE + inner, 0, UNITS, 0),
        (0, 1, 0, EDGE, EDGE + 2 * inner, 0, UNITS, 0),
    ]
    return fields, copies, [(0, UNITS, 0, tall - 2 * HALO, lot - HALO)]


def whole_plan(lot, visits):
    fields = dict(
        visits=visits, aliased=0, spans=UNITS, tall=STEP + 2 * EDGE, margin=EDGE,
        between=(0, EDGE + STEP), blank=[],
    )
    copies = [(0, visit, 0, lot, EDGE + visit * lot, 0, UNITS, 0) for visit in range(visits)]
    copies.append((0, visits - 1, lot - EDGE, EDGE, 0, 0, UNITS - 1, 1))
    copies.append((0, 0, 0, EDGE, EDGE + STEP, 1, UNITS, -1))
    return fields, copies, [(0, UNITS, 0, STEP, 0)]


def per_device(
    images, inv_var, good_columns, warp_rows, warp_cols, block_visit, dest_tile, offsets, psf_taps
):
    tiles = lax.axis_size("py") * lax.axis_size("px")
    visits = lax.axis_size("visit")
    plan = shares(visits)
    lots = [rows for rows, _ in plan]
    mine = lax.axis_index("visit").astype(jnp.int32).reshape(1)

    def make(chunk, var):
        return warp(
            tiles, plan[chunk], chunk == 0, block_visit, dest_tile[:, 0], offsets.T,
            good_columns, warp_rows, warp_cols, var, images,
        )

    def send(blocks):
        return lax.all_to_all(blocks, EVERY, split_axis=0, concat_axis=0, tiled=True)

    made, psf_taps = lax.optimization_barrier((make(0, inv_var), psf_taps))
    arrived = send(made)
    if len(plan) == 1:
        every = whole_plan(lots[0], visits)
        coadd, strip, edge = place(codes(arrived), arrived, lots[0])
        all_of = [lax.all_gather(part, "visit") for part in (coadd, strip, edge)]
        between = neighbours(all_of[2][0, :HALO], all_of[2][visits - 1, HALO:], "py")
        sides = beyond([all_of[1][visit] for visit in range(visits)], *between)
        parts = [(all_of[0][visit], *sides) for visit in range(visits)]
        return stage(every, mine, psf_taps, between, bands(every, psf_taps), [parts], lots)

    outer, inner = outer_plan(lots[0]), inner_plan(*lots)
    tables, inv_var = lax.optimization_barrier(
        ([bands(part, psf_taps) for part in (outer, inner)], inv_var)
    )
    arrived, later = lax.optimization_barrier((arrived, make(1, inv_var)))
    second = send(later)
    code = codes(arrived)
    coadd, strip, edge = place(code, arrived, lots[0])
    between, other_strip = rows_between(edge), swapped(strip)
    coadd, between, other_strip = lax.optimization_barrier((coadd, between, other_strip))
    sides = beyond([strip, other_strip], *between)
    other = swapped(coadd)
    second, sides = lax.optimization_barrier((second, sides))
    parts = [(coadd, *sides), (other, *sides)]
    coadd, strip, _ = place(code, second, lots[1])
    other = swapped(coadd)
    near = neighbours(strip[:HALO], strip[HALO:], "px")
    (parts, between), _ = lax.optimization_barrier(((parts, between), coadd))
    held = stage(outer, mine, psf_taps, between, tables[0], [parts], lots[:1])
    far = swapped(jnp.concatenate(near, axis=0))
    more = [(coadd, *near), (other, far, far)]
    return stage(inner, mine, psf_taps, between, tables[1], [parts, more], lots, held)


def codes(arrived):
    note = arrived[:, arrived.shape[1] - NOTE, :: SIDE // CAP]
    return note.astype(jnp.float32).astype(jnp.int32).reshape(-1)


def solution(mesh):
    in_specs = (
        P(EVERY, None, None),
        P(EVERY, None, None),
        P("visit", None),
        P("visit", None, None),
        P("visit", None, None),
        P(EVERY),
        P(EVERY, None),
        P(EVERY, None),
        P(),
    )
    out_specs = (P("py", "px"), P("py", "px"))
    return jax.shard_map(
        per_device, mesh=mesh, in_specs=in_specs, out_specs=out_specs, check_vma=False
    )
```
